32 devices in a mesh: dp: 8 (over z, y), expert: 4 (over x, core).
Axes of the slice: x: 2, y: 2, z: 4, core: 2. Of those that a mesh axis runs over, the one named last changes fastest.
Arguments:
- tokens: bfloat16 [16384, 1024], P(('dp', 'expert')), may hold values from -6 to 6
- cotangent: bfloat16 [16384, 1024], P(('dp', 'expert')), may hold values from -6 to 6
- gain_one: float32 [1024], replicated, may hold values from 0.25 to 1.75
- w_query: bfloat16 [1024, 1024], P('dp'), may hold values from -0.1875 to 0.1875
- w_key: bfloat16 [1024, 1024], P('dp'), may hold values from -0.1875 to 0.1875
- w_value: bfloat16 [1024, 1024], P('dp'), may hold values from -0.1875 to 0.1875
- w_out: bfloat16 [1024, 1024], P('dp'), may hold values from -1.5 to 1.5
- rel_table: float32 [32, 16], replicated, may hold values from -4 to 4
- gain_two: float32 [1024], replicated, may hold values from 0.25 to 1.75
- w_router: bfloat16 [1024, 4], replicated, may hold values from -0.125 to 0.125
- w_gate: bfloat16 [4, 1024, 2816], P(None, 'dp'), may hold values from -0.1875 to 0.1875
- w_up: bfloat16 [4, 1024, 2816], P(None, 'dp'), may hold values from -0.1875 to 0.1875
- w_down: bfloat16 [4, 2816, 1024], P(None, 'dp'), may hold values from -0.4375 to 0.4375
- expert_ids: int32 [16384, 2], P(('dp', 'expert')), may hold values from 0 to 3, as said below
- slot_index: int32 [16384, 2], P(('dp', 'expert')), may hold values from 0 to 1279, as said below
- slot_kept: int32 [16384, 2], P(('dp', 'expert')), may hold values from 0 to 1, as said below
- seq_bucket: int32 [32], P(('dp', 'expert')), may hold values 0 or 1
Outputs:
- block_out: bfloat16 [16384, 1024], P(('dp', 'expert'))
- input_grad: float32 [16384, 1024], P(('dp', 'expert'))
- gain_one_grad: float32 [1024], replicated
- query_grad: float32 [1024, 1024], P('dp')
- key_grad: float32 [1024, 1024], P('dp')
- value_grad: float32 [1024, 1024], P('dp')
- out_grad: float32 [1024, 1024], P('dp')
- table_grad: float32 [32, 16], replicated
- gain_two_grad: float32 [1024], replicated
- router_grad: float32 [1024, 4], replicated
- gate_grad: float32 [4, 1024, 2816], P(None, 'dp')
- up_grad: float32 [4, 1024, 2816], P(None, 'dp')
- down_grad: float32 [4, 2816, 1024], P(None, 'dp')
The draws below stay inside these ranges and needn't reach their ends.
Inputs may be any that keep to these rules, and one draw needn't show every extreme that they name: `expert_ids`: each token names two different experts. `slot_index`: A kept pair of a token on the device at index d of expert has a slot s with d * 80 <= s % 320 < (d + 1) * 80; within one dp index no two kept pairs share an expert and a slot; a dropped pair has slot 0. `slot_kept`: 1 where the pair holds its slot, 0 where it is dropped.
All inputs are finite; a program needn't handle non-finite values. No bound on the sum of `seq_bucket` on one device may be relied on, other than what follows from the above.
Results may differ from the reference program's by a relative error of at most 0.017.
Values may be sent and summed in bfloat16 or wider, within the bound.
No kernel may reach another device: no remote copies, remote signals or barrier semaphores. Data moves between devices by JAX's collectives and lax.ppermute only.
A program may use at most 704 MiB of HBM per device.

```python
import math
import jax
import jax.numpy as jnp
import numpy as np
from jax import lax

D = 1024
H = 16
HEAD = 64
FF = 2816
EXPERTS = 4
BUCKETS = 32
LONG = 512
SHORT = 128
TOK_DEV = 512
TOKENS = 16384
SLOT_Q = 80
CAPACITY = 1280
N_DP = 8
N_EXPERT = 4


def route_draw(key):
    devices = TOKENS // TOK_DEV
    key_fav = jax.random.fold_in(key, 21)
    key_coin = jax.random.fold_in(key, 22)
    key_drawn = jax.random.fold_in(key, 23)
    key_second = jax.random.fold_in(key, 24)
    key_order = jax.random.fold_in(key, 25)
    favorite = jax.random.randint(key_fav, (devices, 1), 0, EXPERTS)
    coin_flip = jax.random.randint(key_coin, (devices, TOK_DEV), 0, 2)
    uniform_pick = jax.random.randint(key_drawn, (devices, TOK_DEV), 0, EXPERTS)
    first_pick = jnp.where(coin_flip == 1, favorite, uniform_pick)
    second_pick = (first_pick + jax.random.randint(key_second, (devices, TOK_DEV), 1, EXPERTS)) % EXPERTS
    pair_ids = jnp.stack([first_pick, second_pick], -1).reshape(devices, 2 * TOK_DEV).astype(jnp.int32)
    onehot = (pair_ids[:, :, None] == jnp.arange(EXPERTS, dtype=jnp.int32)).astype(jnp.int32)
    queue_rank = jnp.sum((jnp.cumsum(onehot, 1) - 1) * onehot, -1)
    scores = jax.random.randint(key_order, (N_DP, EXPERTS, N_EXPERT), 0, 1 << 20) * N_EXPERT + jnp.arange(N_EXPERT, dtype=jnp.int32)
    owner_order = jnp.argsort(scores, -1).astype(jnp.int32)
    group_of = jnp.arange(devices, dtype=jnp.int32) // N_EXPERT
    sender = jnp.arange(devices, dtype=jnp.int32) % N_EXPERT
    owner_step = queue_rank // SLOT_Q
    kept_pair = owner_step < N_EXPERT
    owner_id = owner_order[group_of[:, None], pair_ids, jnp.minimum(owner_step, N_EXPERT - 1)]
    slot_num = owner_id * (N_EXPERT * SLOT_Q) + sender[:, None] * SLOT_Q + queue_rank % SLOT_Q
    slot_num = jnp.where(kept_pair, slot_num, 0)
    return (pair_ids.reshape(TOKENS, 2), slot_num.reshape(TOKENS, 2), kept_pair.astype(jnp.int32).reshape(TOKENS, 2))


def draw_expert_ids(key, part):
    return route_draw(key)[0]


def draw_slot_index(key, part):
    return route_draw(key)[1]


def draw_slot_kept(key, part):
    return route_draw(key)[2]


def set_ends(drawn, stream_key, least, top_value):
    longest = drawn.shape.index(max(drawn.shape))
    spots = []
    for shift in (0, 1):
        where = [jax.random.randint(jax.random.fold_in(stream_key, axis), (), 0, length) for axis, length in enumerate(drawn.shape)]
        where[longest] = (where[longest] + shift) % drawn.shape[longest]
        spots.append(tuple(where))
    return drawn.at[spots[0]].set(least).at[spots[1]].set(top_value)


def levels(own_key, shape, cuts, smallest, high):
    loudness, own = 1.0, jax.random.fold_in(own_key, 6)
    for position, parts in cuts:
        steps = jnp.exp(jax.random.uniform(jax.random.fold_in(own, position), (parts,), jnp.float32, smallest / len(cuts), high / len(cuts)))
        loudness = loudness * jnp.repeat(steps, shape[position] // parts).reshape([-1 if axis == position else 1 for axis in range(len(shape))])
    return loudness


def noise(stream_key, shape, width, bound, split=(), held_as=jnp.bfloat16):
    entries = jax.random.normal(stream_key, shape, jnp.float32) * width
    if len(split) > 0:
        entries = levels(stream_key, shape, split, -0.22, 0.18) * entries
    return jnp.clip(entries, min=-bound, max=bound).astype(held_as)


def setup_inputs(seed: int = 0) -> dict:
    streams_of = jax.random.split(jax.random.key(seed), 18)
    return {
        "tokens": noise(streams_of[0], (TOKENS, D), 1.0, 6.0, ((0, 32),)),
        "cotangent": noise(streams_of[1], (TOKENS, D), 1.0, 6.0, ((0, 32),)),
        "gain_one": jnp.clip(1.0 + 0.15 * jax.random.normal(streams_of[2], (D,), jnp.float32), 0.25, 1.75),
        "w_query": noise(streams_of[3], (D, D), D ** -0.5, 0.1875, ((0, 8),)),
        "w_key": noise(streams_of[4], (D, D), D ** -0.5, 0.1875, ((0, 8),)),
        "w_value": noise(streams_of[5], (D, D), D ** -0.5, 0.1875, ((0, 8),)),
        "w_out": noise(streams_of[6], (D, D), (D // 64) ** -0.5, 1.5, ((0, 8),)),
        "rel_table": noise(streams_of[7], (BUCKETS, H), 1.0, 4.0, (), jnp.float32),
        "gain_two": jnp.clip(1.0 + 0.15 * jax.random.normal(streams_of[8], (D,), jnp.float32), 0.25, 1.75),
        "w_router": noise(streams_of[9], (D, EXPERTS), (2 * D) ** -0.5, 0.125),
        "w_gate": noise(streams_of[10], (EXPERTS, D, FF), D ** -0.5, 0.1875, ((1, 8),)),
        "w_up": noise(streams_of[11], (EXPERTS, D, FF), D ** -0.5, 0.1875, ((1, 8),)),
        "w_down": noise(streams_of[12], (EXPERTS, FF, D), (FF // 16) ** -0.5, 0.4375, ((1, 8),)),
        "expert_ids": draw_expert_ids(jax.random.fold_in(streams_of[17], 71), 0),
        "slot_index": draw_slot_index(jax.random.fold_in(streams_of[17], 71), 0),
        "slot_kept": draw_slot_kept(jax.random.fold_in(streams_of[17], 71), 0),
        "seq_bucket": set_ends((jax.random.randint(streams_of[16], (TOKENS // LONG,), 0, 2) < 1).astype(jnp.int32), jax.random.fold_in(streams_of[16], 1), 0, 1),
    }


@jax.custom_vjp
def low(v):
    return lax.optimization_barrier(v.astype(jnp.bfloat16)).astype(jnp.float32)

@jax.custom_vjp
def low_back(v):
    return v

def low_keep(v):
    return (low(v), None)

def low_pass(kept, grad):
    return (grad,)

def back_keep(v):
    return (v, None)

def back_low(kept, grad):
    return (low(grad),)
low.defvjp(low_keep, low_pass)
low_back.defvjp(back_keep, back_low)
EPSILON = 1e-06

def bucket_table(length):
    offsets = np.arange(-(length - 1), length)
    distance = np.abs(offsets)
    half_count = BUCKETS // 2
    exact_count = half_count // 2
    widened = np.maximum(distance, 1)
    far_bucket = exact_count + np.floor(np.log(widened / exact_count) / np.log(128.0 / exact_count) * (half_count - exact_count)).astype(np.int32)
    far_bucket = np.minimum(far_bucket, half_count - 1)
    inside = np.where(distance < exact_count, distance, far_bucket)
    return (np.where(offsets > 0, half_count, 0) + inside).astype(np.int32)

def position_index(length):
    places = np.arange(length)
    return bucket_table(length)[places[None, :] - places[:, None] + length - 1]

def make_bias(rel_table):
    return jnp.transpose(rel_table[position_index(LONG)], (2, 0, 1))

def allowed_pairs(block_flag):
    groups = jnp.arange(LONG, dtype=jnp.int32) // SHORT
    return jnp.logical_or(groups[:, None] == groups[None, :], block_flag == 0)

def precise(left, right):
    return jnp.dot(left, right, precision=lax.Precision.HIGHEST)

def round_both(values):
    return low(low_back(values))

def rms_scale(values):
    return values * lax.rsqrt(lax.optimization_barrier(jnp.mean(values * values, -1, keepdims=True)) + EPSILON)

def softmax_last(scores):
    highest = lax.optimization_barrier(jnp.max(scores, -1, keepdims=True))
    raised = jnp.exp(scores - highest)
    return raised / lax.optimization_barrier(jnp.sum(raised, -1, keepdims=True))

def expert_apply(inputs):
    buffer_rows, gate_matrix, up_matrix, down_matrix = inputs
    gate_pre = low_back(precise(buffer_rows, gate_matrix))
    up_pre = low_back(precise(buffer_rows, up_matrix))
    hidden = low(jax.nn.gelu(gate_pre) * up_pre)
    return round_both(precise(hidden, down_matrix))

def block_forward(params, expert_ids, slot_index, slot_kept, seq_bucket):
    row_data, gain_one, w_query, w_key, w_value, w_out, rel_table, gain_two, w_router, w_gate, w_up, w_down = params
    normed = low(rms_scale(row_data) * gain_one)
    head_shape = (TOKENS // LONG, LONG, H, HEAD)
    query_rows = round_both(precise(normed, w_query)).reshape(head_shape)
    key_rows = round_both(precise(normed, w_key)).reshape(head_shape)
    value_rows = round_both(precise(normed, w_value)).reshape(head_shape)
    score_bias = make_bias(rel_table)

    def attend(inputs):
        query_block, key_block, value_block, block_flag = inputs
        scores = jnp.einsum('qhd,khd->hqk', query_block, key_block, precision=lax.Precision.HIGHEST)
        scores = low_back(scores * (1.0 / math.sqrt(HEAD)) + score_bias)
        scores = jnp.where(allowed_pairs(block_flag)[None], scores, -1e+30)
        prob_rows = softmax_last(scores)
        return jnp.einsum('hqk,khd->qhd', low(prob_rows), value_block, precision=lax.Precision.HIGHEST)
    context = lax.map(jax.checkpoint(attend), (query_rows, key_rows, value_rows, seq_bucket))
    context = round_both(context.reshape(TOKENS, D))
    mid_rows = row_data + low_back(precise(context, w_out))
    normed_two = low(rms_scale(mid_rows) * gain_two)
    router = softmax_last(low_back(precise(normed_two, w_router)))
    gate_vals = jnp.take_along_axis(router, expert_ids, 1) * slot_kept.astype(jnp.float32)
    slot_room = EXPERTS * N_DP * CAPACITY
    token_ids = jnp.broadcast_to(jnp.arange(TOKENS, dtype=jnp.int32)[:, None], (TOKENS, 2))
    group_of = token_ids // (N_EXPERT * TOK_DEV)
    flat_slot = (expert_ids * N_DP + group_of) * CAPACITY + slot_index
    target = jnp.where(slot_kept == 1, flat_slot, slot_room).reshape(-1)
    holder = jnp.full((slot_room + 1,), TOKENS, jnp.int32).at[target].set(token_ids.reshape(-1))[:slot_room]
    padded = jnp.concatenate([normed_two, jnp.zeros((1, D), jnp.float32)], 0)
    buffers = low_back(padded[holder]).reshape(EXPERTS, N_DP * CAPACITY, D)
    results = lax.map(jax.checkpoint(expert_apply), (buffers, w_gate, w_up, w_down)).reshape(slot_room, D)
    gathered = jnp.concatenate([results, jnp.zeros((1, D), jnp.float32)], 0)[target].reshape(TOKENS, 2, D)
    return mid_rows + lax.optimization_barrier(jnp.sum(gathered * gate_vals[:, :, None], 1))

def reference(tokens, cotangent, gain_one, w_query, w_key, w_value, w_out, rel_table, gain_two, w_router, w_gate, w_up, w_down, expert_ids, slot_index, slot_kept, seq_bucket):
    floats = [array_in.astype(jnp.float32) for array_in in (tokens, gain_one, w_query, w_key, w_value, w_out, rel_table, gain_two, w_router, w_gate, w_up, w_down)]

    def forward(*params):
        return block_forward(params, expert_ids, slot_index, slot_kept, seq_bucket)
    block_sum, pullback = jax.vjp(forward, *floats)
    gradients = pullback(cotangent.astype(jnp.float32))
    return (block_sum.astype(jnp.bfloat16), gradients[0], gradients[1], gradients[2], gradients[3], gradients[4], gradients[5], gradients[6], gradients[7], gradients[8], gradients[9], gradients[10], gradients[11])
```

```python
import math

import jax
import jax.numpy as jnp
import numpy as np
from jax import lax
from jax.experimental import pallas as pl
from jax.experimental.pallas import tpu as pltpu
from jax.sharding import PartitionSpec as P

D = 1024
H = 16
HEAD = 64
EXPERTS = 4
BUCKETS = 32
LONG = 512
SHORT = 128
PAIR = 2 * HEAD
TILES = LONG // SHORT
EPSILON = 1e-06
FF_TILE = 256
LAY_TILE = 512
MIB = 1024 * 1024
MASKED = -1e30


def bucket_of(offsets):
    distance = np.abs(offsets)
    half_count = BUCKETS // 2
    exact_count = half_count // 2
    widened = np.maximum(distance, 1)
    far_bucket = exact_count + np.floor(
        np.log(widened / exact_count) / np.log(128.0 / exact_count) * (half_count - exact_count)
    ).astype(np.int32)
    far_bucket = np.minimum(far_bucket, half_count - 1)
    inside = np.where(distance < exact_count, distance, far_bucket)
    return (np.where(offsets > 0, half_count, 0) + inside).astype(np.int32)


def near_buckets():
    places = np.arange(SHORT)
    inside = places[:, None] - places[None, :]
    return np.stack([bucket_of(SHORT * step + inside) for step in (-1, 0, 1)]).reshape(-1)


def near_onehot():
    buckets = jnp.asarray(near_buckets().astype(np.int8)).astype(jnp.int32)
    return (jnp.arange(BUCKETS, dtype=jnp.int32)[:, None] == buckets[None, :]).astype(jnp.float32)


FAR_BEFORE = BUCKETS // 2 - 1
FAR_AFTER = BUCKETS - 1


def ring_order(count):
    cols = 4 if count >= 16 else 2
    rows = count // cols
    cycle = [(0, col) for col in range(cols)]
    for row in range(1, rows):
        span = range(cols - 1, 0, -1) if row % 2 else range(1, cols)
        cycle += [(row, col) for col in span]
    cycle += [(row, 0) for row in range(rows - 1, 0, -1)]
    return [row * cols + col for row, col in cycle]


def ring_tables(count):
    ring = ring_order(count)
    ahead = [(ring[i], ring[(i + 1) % count]) for i in range(count)]
    behind = [(there, here) for here, there in ahead]
    place = {index: i for i, index in enumerate(ring)}
    seats = np.asarray(
        [[ring[(place[g] + d) % count] for d in range(count)] for g in range(count)], np.int32
    )
    return ahead, behind, seats


def after(value, *others):
    return lax.optimization_barrier((value, *others))[0]


def matmul(left, right):
    return jnp.dot(left, right, preferred_element_type=jnp.float32)


def dot_dims(left, right, left_dim, right_dim):
    return lax.dot_general(
        left, right, (((left_dim,), (right_dim,)), ((), ())), preferred_element_type=jnp.float32
    )


def tie(values, others):
    values = tuple(values)
    return lax.optimization_barrier(values + tuple(others))[: len(values)]


def pick(array, index, axis=0):
    return lax.dynamic_index_in_dim(array, index, axis, keepdims=False, allow_negative_indices=False)


def lay_kernel(places, spots_ref, *refs):
    *piece_refs, out_ref = refs
    for piece_ref, place in zip(piece_refs, places):
        index = place(spots_ref)
        out_ref[index] = piece_ref[: index[-1].size]


def lay_together(spots, pieces, shape, places, tile, start=0):
    lead = (0,) * (len(shape) - 1)
    first = start // tile
    return pl.pallas_call(
        lambda *refs: lay_kernel(places, *refs),
        grid_spec=pltpu.PrefetchScalarGridSpec(
            num_scalar_prefetch=1,
            grid=(shape[-1] // tile,),
            in_specs=[
                pl.BlockSpec((piece.shape[0], tile), lambda i, spots: (0, i + first))
                for piece in pieces
            ],
            out_specs=pl.BlockSpec((*shape[:-1], tile), lambda i, spots: (*lead, i)),
        ),
        out_shape=jax.ShapeDtypeStruct(shape, jnp.bfloat16),
        compiler_params=pltpu.CompilerParams(vmem_limit_bytes=16 * MIB),
        cost_estimate=pl.CostEstimate(
            flops=0, bytes_accessed=4 * math.prod(shape), transcendentals=0
        ),
    )(spots, *pieces)


class RingGather:
    def __init__(self, block, seat):
        self.count = lax.axis_size("dp")
        self.ahead, self.behind, _ = ring_tables(self.count)
        self.seat, self.rows, self.taken = seat, block.shape[0], 0
        self.low = self.high = block
        self.mid = min((self.rows // 2 + 15) // 16 * 16, self.rows)
        self.pieces = [(block, 0, 0)]

    def arrived(self):
        return (self.low, self.high)

    def step(self, *others):
        half = self.count // 2
        if self.taken >= half:
            return
        if self.taken == 0:
            self.sent = (low,) = tie((self.low,), others)
            high = low
        else:
            self.sent = low, high = tie((self.low, self.high), others)
        self.taken += 1
        last = self.taken == half
        low, high = (low[: self.mid], high[self.mid :]) if last else (low, high)
        self.low = lax.ppermute(low, "dp", self.ahead)
        self.high = lax.ppermute(high, "dp", self.behind)
        self.pieces += [
            (self.low, (half if last else -self.taken) % self.count, 0),
            (self.high, self.taken, self.mid if last else 0),
        ]

    def finish(self, *others):
        while self.taken < self.count // 2:
            self.step()
        columns = self.pieces[0][0].shape[1]
        places = []
        for piece, step, start in self.pieces:

            def place(spots, step=step, start=start, rows=piece.shape[0]):
                return (spots[step], pl.ds(start, rows))

            places.append(place)
        out = lay_together(
            after(self.seat, *others),
            [piece for piece, _, _ in self.pieces],
            (self.count, self.rows, columns),
            places,
            columns // 2,
        )
        return out.reshape(-1, columns)


def ring_sum_kernel(received, outs, *refs):
    own_refs, received_refs = refs[:outs], refs[outs:-outs]
    side = pl.program_id(0)
    for out in range(outs):
        total = own_refs[out][...].astype(jnp.float32)
        for received_ref, (target, only) in zip(received_refs, received):
            if target == out:
                more = received_ref[...].astype(jnp.float32)
                total = total + (more if only is None else jnp.where(side == only, more, 0.0))
        refs[out - outs][...] = total.astype(jnp.bfloat16)


class RingSum:
    def __init__(self, parts, seat, entry=None):
        self.count = lax.axis_size("dp")
        self.ahead, self.behind, _ = ring_tables(self.count)
        self.seat, self.parts, self.entry, self.taken = seat, parts, entry, 0
        if entry is None:
            self.shape = (parts.shape[1], parts.shape[2] // 2)
        else:
            self.shape = (D // self.count, parts.shape[2])
        self.low = self.high = None

    def own(self, step, side=0):
        step = step % self.count
        if self.entry is None:
            return self.parts, pl.BlockSpec(
                (None, *self.shape), lambda i, seat: (seat[step], 0, i + side)
            )
        first = self.entry + side
        return self.parts, pl.BlockSpec(
            (None, *self.shape), lambda i, seat: (first + i, seat[step], 0)
        )

    def call(self, own, received, operands, others=(), halves=2, joined=False):
        moved = 2 * halves * math.prod(self.shape)

        def block(item):
            if item.shape[0] == 1:
                return pl.BlockSpec((None, *self.shape), lambda i, seat: (0, 0, 0))
            return pl.BlockSpec((None, *self.shape), lambda i, seat: (i, 0, 0))

        if joined:
            out_spec = pl.BlockSpec(self.shape, lambda i, seat: (0, i))
            out_shape = (self.shape[0], halves * self.shape[1])
        else:
            out_spec = pl.BlockSpec((None, *self.shape), lambda i, seat: (i, 0, 0))
            out_shape = (halves, *self.shape)
        return pl.pallas_call(
            lambda seat_ref, *refs: ring_sum_kernel(received, len(own), *refs),
            grid_spec=pltpu.PrefetchScalarGridSpec(
                num_scalar_prefetch=1,
                grid=(halves,),
                in_specs=[spec for _, spec in own] + [block(item) for item in operands],
                out_specs=[out_spec] * len(own),
            ),
            out_shape=[jax.ShapeDtypeStruct(out_shape, jnp.bfloat16)] * len(own),
            compiler_params=pltpu.CompilerParams(
                vmem_limit_bytes=(16 if self.entry is None else 40) * MIB
            ),
            cost_estimate=pl.CostEstimate(
                flops=2 * moved,
                bytes_accessed=moved * (len(operands) + 2 * len(own)),
                transcendentals=0,
            ),
        )(after(self.seat, *others), *(part for part, _ in own), *operands)

    def arrived(self):
        return (self.low, self.high)

    def received(self, targets):
        single = self.taken == 1
        return [(targets[0], 0 if single else None), (targets[1], 1 if single else None)]

    def step(self, *others):
        half = self.count // 2
        if self.taken >= half:
            return
        distance = half - self.taken
        if self.taken:
            received, operands = self.received((0, 1)), tie(self.arrived(), others)
            sent = self.call(self.following, received, operands)
        else:
            own = (self.own(distance), self.own(-distance, 1))
            sent = self.call(own, [], (), others, 1)
        self.low = lax.ppermute(sent[0], "dp", self.ahead)
        self.high = lax.ppermute(sent[1], "dp", self.behind)
        self.taken += 1
        distance -= 1
        steps = (distance, -distance) if distance else (0,)
        self.following = [self.own(step) for step in steps]
        self.sent = tuple(sent)

    def finish(self, *others, joined=False):
        while self.taken < self.count // 2:
            self.step()
        received, operands = self.received((0, 0)), tie(self.arrived(), others)
        return self.call(self.following, received, operands, joined=joined)[0]


def swap(value, bit):
    count = lax.axis_size("expert")
    return lax.ppermute(value, "expert", [(i, i ^ bit) for i in range(count)])


class Exchange:
    def __init__(self, own, near, far):
        self.own, self.count, self.rows = own, lax.axis_size("expert"), own.shape[0]
        self.near, self.last = swap(near, 1), None
        if self.count == 4:
            self.far = swap(far, 2)
        else:
            blocks = far.reshape(-1, self.rows, far.shape[1])
            self.far = [swap(block, bit + 2) for bit, block in enumerate(blocks)]

    def forward(self, *others):
        if self.count == 4:
            self.last = swap(after(self.far, *others)[self.rows :], 1)
        return self

    def arrived(self):
        return (self.near, self.last) if self.count == 4 else tuple(self.far)

    def together(self, seat, *others):
        if self.count == 4:
            pieces = [self.own, self.near, self.far, self.last]
        else:
            pieces = [self.own, self.near, *self.far]
        places = [
            lambda spots, d=d: (pl.ds(d * self.rows, self.rows),) for d in range(len(pieces))
        ]
        shape = (self.count * self.rows, self.own.shape[1])
        return lay_together(after(seat, *others), pieces, shape, places, LAY_TILE)


class Spread:
    def __init__(self, value):
        self.bit = lax.axis_size("expert") // 2
        self.held = {0: (value, None)}
        self.hop()

    @classmethod
    def pair(cls, both):
        spreads = cls(both[0]), cls(both[1])
        for lead, spread in enumerate(spreads):
            spread.held[0] = (both, lead)
        return spreads

    @classmethod
    def hop_own(cls, first, second, both, *others):
        swapped = swap(after(both, *others), 1)
        for lead, spread in enumerate((first, second)):
            spread.held[1] = (swapped, lead)
            spread.own_last = (swapped,)

    def hop(self, *others):
        if not self.bit:
            return
        keys = [key for key in self.held if key ^ self.bit not in self.held]
        items = [self.held[key] for key in keys]
        items = tie((item if lead is None else item[lead] for item, lead in items), others)
        fresh = {key ^ self.bit: swap(item, self.bit) for key, item in zip(keys, items)}
        self.last = tuple(fresh.values())
        self.held.update({key: (item, None) for key, item in fresh.items()})
        self.bit //= 2

    def arrived(self):
        return self.last

    def outputs(self, device, *others):
        while self.bit:
            self.hop()
        keys = sorted(self.held)
        shares = len(keys) // EXPERTS
        rows, columns = self.held[0][0].shape[-2:]
        tile = columns // 2

        def spec(lead):
            if lead is None:
                return pl.BlockSpec((rows, tile), lambda i, spots: (0, i))
            return pl.BlockSpec((None, rows, tile), lambda i, spots: (lead, 0, i))

        def kernel(spots_ref, *refs):
            *block_refs, out_ref = refs
            for first in range(0, len(keys), shares):
                total = block_refs[first][...].astype(jnp.float32)
                for block_ref in block_refs[first + 1 : first + shares]:
                    total = total + block_ref[...].astype(jnp.float32)
                out_ref[spots_ref[first]] = total

        spots = jnp.stack([device ^ key if shares == 1 else lax.div(device ^ key, shares) for key in keys])
        return pl.pallas_call(
            kernel,
            grid_spec=pltpu.PrefetchScalarGridSpec(
                num_scalar_prefetch=1,
                grid=(2,),
                in_specs=[spec(self.held[key][1]) for key in keys],
                out_specs=pl.BlockSpec((EXPERTS, rows, tile), lambda i, spots: (0, 0, i)),
            ),
            out_shape=jax.ShapeDtypeStruct((EXPERTS, rows, columns), jnp.float32),
            compiler_params=pltpu.CompilerParams(vmem_limit_bytes=24 * MIB),
            cost_estimate=pl.CostEstimate(
                flops=0, bytes_accessed=6 * EXPERTS * rows * columns, transcendentals=0
            ),
        )(after(spots, *others), *(self.held[key][0] for key in keys))


class SumAll:
    def __init__(self, parts):
        self.shapes = [part.shape for part in parts]
        self.flat = jnp.concatenate([part.reshape(-1, 128) for part in parts], 0)
        self.hops = []
        for axis in ("expert", "dp"):
            bit, count = 1, lax.axis_size(axis)
            while bit < count:
                self.hops.append((axis, [(i, i ^ bit) for i in range(count)]))
                bit *= 2
        over_x = self.hops.pop(1)
        self.hops.append(over_x)

    def hop(self, *others):
        if not self.hops:
            return self.flat
        axis, pairs = self.hops.pop(0)
        flat = after(self.flat, *others)
        self.flat = flat + lax.ppermute(flat, axis, pairs)
        return self.flat

    def finish(self, *others):
        while self.hops:
            self.hop(*others)
        sums, start = [], 0
        for shape in self.shapes:
            rows = math.prod(shape) // 128
            sums.append(self.flat[start : start + rows].reshape(shape))
            start += rows
        return sums


def norm_backward(grad_rows, row_data, inverse, gain_vec):
    scaled = grad_rows * gain_vec
    inner_mean = jnp.mean(scaled * row_data, -1, keepdims=True)
    grad_input = inverse * scaled - row_data * inverse * inverse * inverse * inner_mean
    return (grad_input, jnp.sum(grad_rows * row_data * inverse, 0))


def other_head_zeroed(rows_t, head):
    own = rows_t[head * HEAD : (head + 1) * HEAD]
    rest = jnp.zeros_like(own)
    return jnp.concatenate([own, rest] if head == 0 else [rest, own], 0)


def tile_biases(bias_ref, far_ref, pair, head, penalty):
    near = {
        -1: bias_ref[head, 0] + penalty,
        0: bias_ref[head, 1],
        1: bias_ref[head, 2] + penalty,
    }
    before = far_ref[0, 2 * pair + head] + penalty
    later = far_ref[1, 2 * pair + head] + penalty
    return lambda step: near[step] if abs(step) < 2 else (before if step < 0 else later)


def transposed(rows):
    return rows.astype(jnp.float32).T


def attend_forward_kernel(
    flag_ref, far_ref, q_ref, k_ref, v_ref, bias_ref, ctx_ref, lse_ref
):
    block, pair = pl.program_id(0), pl.program_id(1)
    penalty = jnp.where(flag_ref[block] == 0, 0.0, MASKED).astype(jnp.float32)
    query_t = (transposed(q_ref[...]) * (1.0 / math.sqrt(HEAD))).astype(jnp.bfloat16)
    value_t = transposed(v_ref[...]).astype(jnp.bfloat16)
    key_rows = k_ref[...]
    parts = []
    for head in range(2):
        bias = tile_biases(bias_ref, far_ref, pair, head, penalty)
        scores = dot_dims(key_rows, other_head_zeroed(query_t, head), 1, 0)
        value_head = value_t[head * HEAD : (head + 1) * HEAD]
        pieces = []
        for col in range(TILES):
            cols = slice(col * SHORT, (col + 1) * SHORT)
            panel = jnp.concatenate(
                [
                    scores[row * SHORT : (row + 1) * SHORT, cols] + bias(row - col)
                    for row in range(TILES)
                ],
                0,
            )
            highest = jnp.max(panel, 0, keepdims=True)
            raised = jnp.exp(panel - highest)
            total = jnp.sum(raised, 0, keepdims=True)
            piece = matmul(value_head, raised.astype(jnp.bfloat16))
            pieces.append(piece / total)
            lse_ref[0, 0, head : head + 1, cols] = highest + jnp.log(total)
        parts.append(pieces)
    for col in range(TILES):
        joined = jnp.concatenate([parts[0][col], parts[1][col]], 0)
        ctx_ref[col * SHORT : (col + 1) * SHORT, :] = joined.T.astype(jnp.bfloat16)


def attend_forward(qkv, flags, far, bias):
    tok_count = qkv.shape[0]
    blocks = tok_count // LONG
    pairs = H // 2

    def column(first):
        return pl.BlockSpec((LONG, PAIR), lambda b, p, flag: (b, first + p))

    return pl.pallas_call(
        attend_forward_kernel,
        grid_spec=pltpu.PrefetchScalarGridSpec(
            num_scalar_prefetch=1,
            grid=(blocks, pairs),
            in_specs=[
                pl.BlockSpec(memory_space=pltpu.SMEM),
                column(0),
                column(pairs),
                column(2 * pairs),
                pl.BlockSpec((2, 3, SHORT, SHORT), lambda b, p, flag: (p, 0, 0, 0)),
            ],
            out_specs=[
                column(0),
                pl.BlockSpec((1, 1, 2, LONG), lambda b, p, flag: (b, p, 0, 0)),
            ],
        ),
        out_shape=[
            jax.ShapeDtypeStruct((tok_count, D), jnp.bfloat16),
            jax.ShapeDtypeStruct((blocks, pairs, 2, LONG), jnp.float32),
        ],
        compiler_params=pltpu.CompilerParams(vmem_limit_bytes=16 * MIB),
        cost_estimate=pl.CostEstimate(
            flops=8 * H * LONG * LONG * HEAD * blocks,
            bytes_accessed=8 * tok_count * D + 12 * H * SHORT * SHORT,
            transcendentals=H * LONG * LONG * blocks,
        ),
    )(flags, far, qkv, qkv, qkv, bias)


def attend_backward_kernel(
    flag_ref,
    far_ref,
    q_ref,
    k_ref,
    v_ref,
    grad_ref,
    lse_ref,
    bias_ref,
    dq_ref,
    dk_ref,
    dv_ref,
    near_ref,
    away_ref,
    weight_scr,
    score_scr,
):
    pair, block = pl.program_id(0), pl.program_id(1)
    penalty = jnp.where(flag_ref[block] == 0, 0.0, MASKED).astype(jnp.float32)
    scaled = (q_ref[...].astype(jnp.float32) * (1.0 / math.sqrt(HEAD))).astype(jnp.bfloat16)
    query_t = transposed(scaled).astype(jnp.bfloat16)
    grad_t = transposed(grad_ref[...]).astype(jnp.bfloat16)
    key_t = transposed(k_ref[...]).astype(jnp.bfloat16)
    key_rows, value_rows, grad_rows = k_ref[...], v_ref[...], grad_ref[...]

    @pl.when(block == 0)
    def _():
        near_ref[...] = jnp.zeros_like(near_ref)
        away_ref[...] = jnp.zeros_like(away_ref)

    query_parts, key_parts, value_parts = [], [], []
    for head in range(2):
        bias = tile_biases(bias_ref, far_ref, pair, head, penalty)
        scores = dot_dims(key_rows, other_head_zeroed(query_t, head), 1, 0)
        grad_probs = dot_dims(value_rows, other_head_zeroed(grad_t, head), 1, 0)
        key_head = key_t[head * HEAD : (head + 1) * HEAD]
        near = {-1: None, 0: None, 1: None}
        away = [None, None]
        for col in range(TILES):
            cols = slice(col * SHORT, (col + 1) * SHORT)
            total = lse_ref[0, 0, head : head + 1, cols]
            probs = jnp.exp(
                jnp.concatenate(
                    [
                        scores[row * SHORT : (row + 1) * SHORT, cols] + bias(row - col)
                        for row in range(TILES)
                    ],
                    0,
                )
                - total
            )
            panel = grad_probs[:, cols]
            inner = jnp.sum(probs * panel, 0, keepdims=True)
            grad_scores = (probs * (panel - inner)).astype(jnp.bfloat16)
            weight_scr[:, cols] = probs.astype(jnp.bfloat16)
            score_scr[:, cols] = grad_scores
            rounded = grad_scores.astype(jnp.float32)
            for row in range(TILES):
                tile = rounded[row * SHORT : (row + 1) * SHORT]
                step = row - col
                if abs(step) < 2:
                    near[step] = tile if near[step] is None else near[step] + tile
                else:
                    side = 0 if step < 0 else 1
                    tile = jnp.sum(tile, 0, keepdims=True)
                    away[side] = tile if away[side] is None else away[side] + tile
        for step in (-1, 0, 1):
            near_ref[head, step + 1] += near[step]
        for side in range(2):
            away_ref[0, head, side : side + 1, :] += away[side]
        query_parts.append(matmul(key_head, score_scr[...]))
        key_parts.append(matmul(score_scr[...], scaled))
        value_parts.append(matmul(weight_scr[...], grad_rows))
    lane = lax.broadcasted_iota(jnp.int32, (LONG, PAIR), 1)
    dk_ref[...] = jnp.where(lane < HEAD, key_parts[0], key_parts[1]).astype(jnp.bfloat16)
    dv_ref[...] = jnp.where(lane < HEAD, value_parts[0], value_parts[1]).astype(jnp.bfloat16)
    joined = jnp.concatenate(query_parts, 0) * (1.0 / math.sqrt(HEAD))
    dq_ref[...] = joined.T.astype(jnp.bfloat16)


def attend_backward(qkv, grad_context, lse, flags, far, bias):
    tok_count = qkv.shape[0]
    blocks = tok_count // LONG
    pairs = H // 2

    def column(first):
        return pl.BlockSpec((LONG, PAIR), lambda p, b, flag: (b, first + p))

    rows = jax.ShapeDtypeStruct((tok_count, D), jnp.bfloat16)
    return pl.pallas_call(
        attend_backward_kernel,
        grid_spec=pltpu.PrefetchScalarGridSpec(
            num_scalar_prefetch=1,
            grid=(pairs, blocks),
            in_specs=[
                pl.BlockSpec(memory_space=pltpu.SMEM),
                column(0),
                column(pairs),
                column(2 * pairs),
                column(0),
                pl.BlockSpec((1, 1, 2, LONG), lambda p, b, flag: (b, p, 0, 0)),
                pl.BlockSpec((2, 3, SHORT, SHORT), lambda p, b, flag: (p, 0, 0, 0)),
            ],
            out_specs=[
                column(0),
                column(0),
                column(0),
                pl.BlockSpec((2, 3, SHORT, SHORT), lambda p, b, flag: (p, 0, 0, 0)),
                pl.BlockSpec((1, 2, 2, SHORT), lambda p, b, flag: (p, 0, 0, 0)),
            ],
            scratch_shapes=[
                pltpu.VMEM((LONG, LONG), jnp.bfloat16),
                pltpu.VMEM((LONG, LONG), jnp.bfloat16),
            ],
        ),
        out_shape=[
            rows,
            rows,
            rows,
            jax.ShapeDtypeStruct((H, 3, SHORT, SHORT), jnp.float32),
            jax.ShapeDtypeStruct((pairs, 2, 2, SHORT), jnp.float32),
        ],
        compiler_params=pltpu.CompilerParams(vmem_limit_bytes=24 * MIB),
        cost_estimate=pl.CostEstimate(
            flops=20 * H * LONG * LONG * HEAD * blocks,
            bytes_accessed=16 * tok_count * D + 24 * H * SHORT * SHORT,
            transcendentals=H * LONG * LONG * blocks,
        ),
    )(flags, far, qkv, qkv, qkv, grad_context, lse, bias)


ROW_TILE = 256
GELU_SCALE = math.sqrt(2.0 / math.pi)
GELU_CUBE = 0.044715


def row_tiles(rows):
    return [slice(start, min(start + ROW_TILE, rows)) for start in range(0, rows, ROW_TILE)]


def gate_kernel(rows_ref, weight_ref, act_ref, slope_ref):
    for part in row_tiles(rows_ref.shape[0]):
        pre = matmul(rows_ref[part, :], weight_ref[...])
        square = pre * pre
        angle = jnp.tanh(pre * (GELU_SCALE + (GELU_SCALE * GELU_CUBE) * square))
        half = 0.5 + 0.5 * angle
        act_ref[part, :] = (pre * half).astype(jnp.bfloat16)
        bend = (0.5 * GELU_SCALE) + (1.5 * GELU_SCALE * GELU_CUBE) * square
        slope_ref[part, :] = (half + pre * (1.0 - angle * angle) * bend).astype(jnp.bfloat16)


def up_kernel(rows_ref, weight_ref, act_ref, slope_ref, grads_ref, hid_ref, lift_ref, down_ref):
    for part in row_tiles(rows_ref.shape[0]):
        lift = matmul(rows_ref[part, :], weight_ref[...])
        hid_ref[part, :] = (act_ref[part, :].astype(jnp.float32) * lift).astype(jnp.bfloat16)
        lift_ref[part, :] = (slope_ref[part, :].astype(jnp.float32) * lift).astype(jnp.bfloat16)
    down_ref[...] = dot_dims(hid_ref[...], grads_ref[...], 0, 0).astype(jnp.bfloat16)


def hidden_back_kernel(grads_ref, down_ref, lift_ref, act_ref, rows_t_ref, out_ref):
    for part in row_tiles(grads_ref.shape[0]):
        back = dot_dims(grads_ref[part, :], down_ref[...], 1, 1)
        out_ref[0, part, :] = (back * lift_ref[part, :].astype(jnp.float32)).astype(jnp.bfloat16)
        out_ref[1, part, :] = (back * act_ref[part, :].astype(jnp.float32)).astype(jnp.bfloat16)
    rows = rows_t_ref.shape[0]
    for part in row_tiles(rows):
        out_ref[2, part, :] = matmul(rows_t_ref[part, :], out_ref[0]).astype(jnp.bfloat16)
        out_ref[3, part, :] = matmul(rows_t_ref[part, :], out_ref[1]).astype(jnp.bfloat16)
    rest = jnp.zeros((2, out_ref.shape[1] - rows, out_ref.shape[2]), jnp.bfloat16)
    out_ref[2:, rows:, :] = rest


def rows_back_kernel(pre_ref, up_ref, gate_w_ref, up_w_ref, *out_refs):
    total = dot_dims(pre_ref[...], gate_w_ref[...], 1, 1) + dot_dims(up_ref[...], up_w_ref[...], 1, 1)
    start = 0
    for out_ref in out_refs:
        rows = out_ref.shape[0]
        out_ref[...] = total[start : start + rows].astype(jnp.bfloat16)
        start += rows


def kernel_call(kernel, operands, in_specs, out_specs, out_shape, steps, flops, vmem):
    moved = sum(2 * math.prod(item.shape) for item in (*operands, *out_shape))
    return pl.pallas_call(
        kernel,
        grid=(steps,),
        in_specs=in_specs,
        out_specs=out_specs,
        out_shape=[jax.ShapeDtypeStruct(item.shape, jnp.bfloat16) for item in out_shape],
        compiler_params=pltpu.CompilerParams(vmem_limit_bytes=vmem * MIB),
        cost_estimate=pl.CostEstimate(flops=flops, bytes_accessed=moved, transcendentals=0),
    )(*operands)


def width_tiles(width):
    return pl.cdiv(width, FF_TILE)


def whole_spec(shape, buffers=2):
    return pl.BlockSpec(shape, lambda i: (0, 0), pipeline_mode=pl.Buffered(buffers))


def gate_forward(rows, weight):
    count, width = rows.shape[0], weight.shape[1]
    tile = pl.BlockSpec((count, FF_TILE), lambda i: (0, i))
    shape = jax.ShapeDtypeStruct((count, width), jnp.bfloat16)
    return kernel_call(
        gate_kernel,
        (rows, weight),
        [whole_spec(rows.shape), pl.BlockSpec((D, FF_TILE), lambda i: (0, i))],
        [tile, tile],
        [shape, shape],
        width_tiles(width),
        2 * count * D * width,
        59,
    )


def up_forward(rows, weight, act, slope, grads):
    count, width = rows.shape[0], weight.shape[1]
    tile = pl.BlockSpec((count, FF_TILE), lambda i: (0, i))
    shape = jax.ShapeDtypeStruct((count, width), jnp.bfloat16)
    return kernel_call(
        up_kernel,
        (rows, weight, act, slope, grads),
        [
            whole_spec(rows.shape),
            pl.BlockSpec((D, FF_TILE), lambda i: (0, i)),
            tile,
            tile,
            whole_spec(grads.shape),
        ],
        [tile, tile, pl.BlockSpec((FF_TILE, D), lambda i: (i, 0))],
        [shape, shape, jax.ShapeDtypeStruct((width, D), jnp.bfloat16)],
        width_tiles(width),
        4 * count * D * width,
        59,
    )


def hidden_back(grads, weight, lift, act, rows_t):
    count, width = lift.shape
    tile = pl.BlockSpec((count, FF_TILE), lambda i: (0, i))
    return kernel_call(
        hidden_back_kernel,
        (grads, weight, lift, act, rows_t),
        [
            whole_spec(grads.shape),
            pl.BlockSpec((FF_TILE, D), lambda i: (i, 0)),
            tile,
            tile,
            whole_spec(rows_t.shape),
        ],
        [pl.BlockSpec((4, count, FF_TILE), lambda i: (0, 0, i))],
        [jax.ShapeDtypeStruct((4, count, width), jnp.bfloat16)],
        width_tiles(width),
        6 * count * D * width,
        59,
    )[0]


def rows_back(hidden_grads, gate_weight, up_weight, splits):
    _, count, width = hidden_grads.shape
    weight_tile = pl.BlockSpec((ROW_TILE, width), lambda i: (i, 0))

    def entry(number):
        return pl.BlockSpec(
            (None, count, width), lambda i: (number, 0, 0), pipeline_mode=pl.Buffered(1)
        )

    return kernel_call(
        rows_back_kernel,
        (hidden_grads, hidden_grads, gate_weight, up_weight),
        [entry(0), entry(1), weight_tile, weight_tile],
        [pl.BlockSpec((rows, ROW_TILE), lambda i: (0, i)) for rows in splits],
        [jax.ShapeDtypeStruct((rows, D), jnp.bfloat16) for rows in splits],
        D // ROW_TILE,
        4 * count * D * width,
        59,
    )


def table_sums(near, away):
    near_part = lax.dot_general(
        near_onehot(),
        near.reshape(H, -1),
        (((1,), (1,)), ((), ())),
        precision=lax.Precision.HIGHEST,
        preferred_element_type=jnp.float32,
    )
    far_part = jnp.sum(away, -1).reshape(H, 2)
    sides = np.zeros((BUCKETS, 2), np.float32)
    sides[FAR_BEFORE, 0] = sides[FAR_AFTER, 1] = 1.0
    return near_part + jnp.sum(sides[:, None, :] * far_part[None], -1)


def body(
    tokens,
    cotangent,
    gain_one,
    w_query,
    w_key,
    w_value,
    w_out,
    rel_table,
    gain_two,
    w_router,
    w_gate,
    w_up,
    w_down,
    expert_ids,
    slot_index,
    slot_kept,
    seq_bucket,
):
    tok_count = tokens.shape[0]
    dp_count = lax.axis_size("dp")
    owner_count = lax.axis_size("expert")
    shares = owner_count // EXPERTS
    group = lax.axis_index("dp")
    device = lax.axis_index("expert")
    expert = device if shares == 1 else lax.div(device, shares)
    core = device & 1
    seat = pick(jnp.asarray(ring_tables(dp_count)[2]), group)

    half_rows = w_query.shape[0] // 2

    def own_half(weight):
        return lax.dynamic_slice_in_dim(
            weight, core * half_rows, half_rows, 0, allow_negative_indices=False
        )

    slot_quota = 5 * tok_count // (2 * EXPERTS * owner_count)
    slot_span = owner_count * slot_quota
    owners_each = owner_count // shares
    block_rows = owners_each * slot_quota
    slot_room = owner_count * block_rows

    def routes(ids, slots, kept):
        owner = slots // slot_span
        dest = ids * shares + owner // owners_each
        local_slot = (
            (dest ^ device) * block_rows
            + (owner % owners_each) * slot_quota
            + slots % slot_span
            - device * slot_quota
        )
        target = jnp.where(kept == 1, local_slot, slot_room)
        room = jnp.arange(slot_room, dtype=jnp.int32)
        from_slot = [
            (target[:, k : k + 1] == room[None, :]).astype(jnp.bfloat16) for k in range(2)
        ]
        to_slot = jnp.logical_or(
            target[:, 0][None, :] == room[:, None], target[:, 1][None, :] == room[:, None]
        ).astype(jnp.bfloat16)
        return from_slot, to_slot

    def parts_of(rows):
        return rows[:block_rows], rows[block_rows : 2 * block_rows], rows[2 * block_rows :]

    def outgoing(rows, to_slot):
        return [matmul(part, rows).astype(jnp.bfloat16) for part in reversed(parts_of(to_slot))][::-1]

    def route(rows):
        logits = matmul(rows, w_router)
        raised = jnp.exp(logits - jnp.max(logits, -1, keepdims=True))
        return raised / jnp.sum(raised, -1, keepdims=True)

    weight_ring = RingGather(
        jnp.concatenate([own_half(weight) for weight in (w_query, w_key, w_value, w_out)], 1), seat
    )
    weight_ring.step()
    row_one = tokens.astype(jnp.float32)
    inv_one = lax.rsqrt(jnp.mean(row_one * row_one, -1, keepdims=True) + EPSILON)
    normed = (row_one * inv_one * gain_one).astype(jnp.bfloat16)
    theirs = [swap(weight_ring.pieces[0][0], 1)]

    def weight_step(*others):
        if weight_ring.taken < dp_count // 2:
            weight_ring.step(*others)
            theirs.extend(swap(piece, 1) for piece in weight_ring.sent)

    weight_step(inv_one)
    ids, slots, kept = tie((expert_ids, slot_index, slot_kept), weight_ring.sent)
    from_slot, to_slot = routes(ids, slots, kept)
    weight_step(to_slot, theirs[0])
    cots, table = tie((cotangent, rel_table), weight_ring.sent)
    cot_blocks = outgoing(cots, to_slot)
    bias = lax.dot_general(
        after(table, *cot_blocks),
        near_onehot(),
        (((0,), (0,)), ((), ())),
        precision=lax.Precision.HIGHEST,
        preferred_element_type=jnp.float32,
    ).reshape(H, 3, SHORT, SHORT)
    far = jnp.stack([rel_table[FAR_BEFORE], rel_table[FAR_AFTER]])
    weight_step(bias, *theirs[1:3])
    while weight_ring.taken < dp_count // 2:
        weight_step()
    gate_ring = RingGather(pick(w_gate, expert), seat)
    gate_ring.step(*weight_ring.sent)
    theirs.extend(swap(piece, 1) for piece in weight_ring.arrived())
    places = []
    for side in range(2):
        for piece, step, start in weight_ring.pieces:

            def place(spots, step=step, side=side, start=start, rows=piece.shape[0]):
                return (spots[step], spots[dp_count + side], pl.ds(start, rows))

            places.append(place)
    spots = jnp.concatenate([seat, jnp.stack([core, 1 - core])])
    pieces = [piece for piece, _, _ in weight_ring.pieces] + theirs
    full_qkv = lay_together(spots, pieces, (dp_count, 2, half_rows, 3 * D), places, LAY_TILE)
    full_out = lay_together(spots, pieces, (dp_count, 2, half_rows, D), places, LAY_TILE, 3 * D)
    full_qkv, full_out = full_qkv.reshape(D, 3 * D), full_out.reshape(D, D)
    up_own, down_own = tie((pick(w_up, expert), pick(w_down, expert)), (full_qkv,))
    up_ring = RingGather(up_own, seat)
    down_ring = RingGather(down_own, seat)

    gate_ring.step(full_qkv, up_own, down_own)
    (normed_now,) = tie((normed,), gate_ring.sent)
    qkv = matmul(normed_now, full_qkv).astype(jnp.bfloat16)
    context, lse = attend_forward(qkv, seq_bucket, far, bias)
    (context,) = tie((context,), gate_ring.arrived())
    gate_ring.step(context)
    (context,) = tie((context,), gate_ring.sent)
    mid_rows = row_one + matmul(context, full_out)
    inv_two = lax.rsqrt(jnp.mean(mid_rows * mid_rows, -1, keepdims=True) + EPSILON)
    normed_two = (mid_rows * inv_two * gain_two).astype(jnp.bfloat16)
    row_blocks = outgoing(normed_two, to_slot)
    row_exchange = Exchange(*row_blocks)
    gate_ring.step(*row_blocks)
    up_ring.step(*gate_ring.sent)
    gate_full = gate_ring.finish(*up_ring.sent)
    router = route(after(normed_two, gate_full))
    chosen = (ids[:, :, None] == jnp.arange(EXPERTS, dtype=jnp.int32)).astype(jnp.float32)
    kept_pair = kept.astype(jnp.float32)
    gate_vals = jnp.sum(chosen * router[:, None, :], -1) * kept_pair
    up_ring.step(gate_vals)

    slot_rows = row_exchange.forward(*up_ring.sent).together(seat)
    cot_exchange = Exchange(*tie(cot_blocks, (slot_rows,)))
    down_ring.step(slot_rows)
    (gate_now,) = tie((gate_full,), (*down_ring.sent, cot_exchange.near))
    act, slope = gate_forward(slot_rows, gate_now)
    act, slope = tie((act, slope), up_ring.arrived())
    up_ring.step(act)
    (rows_now,) = tie((slot_rows,), up_ring.sent)
    slot_gate = lax.dynamic_index_in_dim(
        route(rows_now), expert, 1, allow_negative_indices=False
    )
    slot_rows_t = rows_now.T
    cot_exchange.forward(slot_gate, slot_rows_t, *up_ring.arrived())
    slot_cots = cot_exchange.together(seat)
    slot_grads = (slot_gate * slot_cots.astype(jnp.float32)).astype(jnp.bfloat16)
    up_ring.step(slot_gate, slot_rows_t)
    down_ring.step(*up_ring.arrived())
    up_full = up_ring.finish(*down_ring.sent, slot_grads)
    down_ring.step(up_full, slot_grads)
    (up_full,) = tie((up_full,), down_ring.sent)
    hidden, lift_slope, down_parts = up_forward(slot_rows, up_full, act, slope, slot_grads)
    hidden, lift_slope = tie((hidden, lift_slope), down_ring.arrived())
    down_ring.step(hidden)
    down_sum = RingSum(down_parts.reshape(dp_count, -1, D), seat)
    down_sum.step(*down_ring.sent)
    down_full = down_ring.finish(*down_sum.sent)

    expert_rows = matmul(hidden, down_full).astype(jnp.bfloat16)
    expert_blocks = tie(parts_of(expert_rows), down_sum.arrived())
    returned = Exchange(*expert_blocks)
    down_sum.step(expert_rows)
    (back_grads,) = tie((slot_grads,), down_sum.sent)
    hidden_grads = hidden_back(back_grads, down_full, lift_slope, act, slot_rows_t)
    (hidden_grads,) = tie(
        (hidden_grads,),
        (*down_sum.arrived(), returned.near, *(returned.arrived() if owner_count > 4 else (returned.far,))),
    )
    returned.forward(hidden_grads)
    gate_up_sum = RingSum(hidden_grads, seat, 2)
    gate_up_sum.step(hidden_grads)
    down_sum.step(*gate_up_sum.sent, *returned.arrived())
    (hidden_now,) = tie((hidden_grads,), (*down_sum.sent, *gate_up_sum.sent))
    splits = (block_rows, block_rows, slot_room - 2 * block_rows)
    grad_rows = rows_back(hidden_now, gate_full, up_full, splits)
    returned_grads = Exchange(*grad_rows)
    gate_up_sum.step(*grad_rows)

    returned = returned.together(seat, *gate_up_sum.sent, *down_sum.arrived())
    pair_values = [matmul(picks, returned) for picks in from_slot]
    block_out = (
        mid_rows + pair_values[0] * gate_vals[:, 0:1] + pair_values[1] * gate_vals[:, 1:2]
    ).astype(jnp.bfloat16)
    grad_final = cotangent.astype(jnp.float32)
    grad_gates = (
        jnp.stack([jnp.sum(grad_final * values, -1) for values in pair_values], 1) * kept_pair
    )
    grad_router = jnp.sum(chosen * grad_gates[:, :, None], 1)
    grad_logits = (
        router * (grad_router - jnp.sum(router * grad_router, -1, keepdims=True))
    ).astype(jnp.bfloat16)
    returned_grads.forward(grad_logits, *gate_up_sum.arrived())
    gate_up_sum.step(grad_logits)
    returned_grads = returned_grads.together(seat, *gate_up_sum.sent)
    grad_normed_two = matmul(grad_logits, w_router.T) + matmul(
        from_slot[0] + from_slot[1], returned_grads
    )
    grad_mid_norm, gain_two_local = norm_backward(grad_normed_two, mid_rows, inv_two, gain_two)
    grad_mid = grad_final + grad_mid_norm

    grad_branch = grad_mid.astype(jnp.bfloat16)
    grad_context = dot_dims(grad_branch, full_out, 1, 1).astype(jnp.bfloat16)

    def core_parts(local):
        split = local.reshape(dp_count, 2, half_rows, -1)
        return pick(split, core, 1), pick(split, 1 - core, 1)

    out_mine, out_other = core_parts(dot_dims(context, grad_branch, 0, 0).astype(jnp.bfloat16))
    (grad_context,) = tie((grad_context,), (out_mine, out_other))
    grad_query, grad_key, grad_value, near, away = attend_backward(
        qkv, grad_context, lse, seq_bucket, far, bias
    )
    down_sum.step(grad_query)
    out_other = swap(after(out_other, grad_query), 1)
    qkv_grads = jnp.concatenate([grad_query, grad_key, grad_value], 1)
    qkv_mine, qkv_other = core_parts(dot_dims(normed, qkv_grads, 0, 0).astype(jnp.bfloat16))
    gate_up_sum.step(qkv_other, qkv_mine, *down_sum.arrived())
    down_share = down_sum.finish(*gate_up_sum.sent, joined=True)
    qkv_other = swap(after(qkv_other, *gate_up_sum.sent), 1)
    down_blocks = Spread(after(down_share, *gate_up_sum.sent))
    qkv_mine, out_mine = tie((qkv_mine, out_mine), gate_up_sum.sent)
    weight_parts = jnp.concatenate(
        [
            (mine.astype(jnp.float32) + other.astype(jnp.float32)).astype(jnp.bfloat16)
            for mine, other in ((qkv_mine, qkv_other), (out_mine, out_other))
        ],
        2,
    )
    weight_sum = RingSum(weight_parts, seat)
    near, away = tie((near, away), gate_up_sum.sent)
    table_local = table_sums(near, away)
    weight_sum.step(weight_parts, table_local, *down_blocks.arrived())
    (late_grads,) = tie((qkv_grads,), weight_sum.sent)
    grad_normed = dot_dims(late_grads, full_qkv, 1, 1)
    grad_row_one, gain_one_local = norm_backward(grad_normed, row_one, inv_one, gain_one)
    input_grad = grad_mid + grad_row_one
    down_blocks.hop(*weight_sum.sent)

    gate_up_share = gate_up_sum.finish(input_grad)
    gate_blocks, up_blocks = Spread.pair(gate_up_share)
    weight_sum.step(gate_up_share, *down_blocks.arrived())
    (late_rows,) = tie((normed_two,), weight_sum.sent)
    small = SumAll((gain_one_local, table_local, gain_two_local, matmul(late_rows.T, grad_logits)))
    weight_sum.step(small.hop(*weight_sum.sent), *gate_blocks.arrived())
    Spread.hop_own(gate_blocks, up_blocks, gate_up_share, *weight_sum.sent)
    weight_sum.step(small.hop(*weight_sum.sent), *up_blocks.arrived(), *up_blocks.own_last)
    gate_blocks.hop(*weight_sum.sent)
    up_blocks.hop(*weight_sum.sent)
    down_out = down_blocks.outputs(device, *weight_sum.sent)
    rounded = weight_sum.finish(
        down_out, small.hop(*weight_sum.sent), *gate_blocks.arrived(), *up_blocks.arrived()
    )
    gate_out = gate_blocks.outputs(device, rounded, small.hop(rounded))
    up_out = up_blocks.outputs(device, gate_out)
    bit = owner_count // 2
    while bit > 1:
        arriving = after(swap(rounded, bit), gate_out, up_out)
        share = rounded.astype(jnp.float32) + arriving.astype(jnp.float32)
        rounded = share.astype(jnp.bfloat16)
        bit //= 2
    other = swap(rounded, 1)
    small.hop(rounded)
    gain_one_grad, table_grad, gain_two_grad, router_grad = small.finish()
    weight_grads = jnp.concatenate(
        [jnp.where(core == 0, rounded, other), jnp.where(core == 0, other, rounded)], 1
    ).astype(jnp.float32)
    query_grad, key_grad, value_grad, out_grad = (
        weight_grads[i // 2, :, i % 2 * D : (i % 2 + 1) * D] for i in range(4)
    )
    return (
        block_out,
        input_grad,
        gain_one_grad,
        query_grad,
        key_grad,
        value_grad,
        out_grad,
        table_grad,
        gain_two_grad,
        router_grad,
        gate_out,
        up_out,
        down_out,
    )


def solution(mesh):
    placed = (
        P(("dp", "expert"), None),
        P(("dp", "expert"), None),
        P(),
        P("dp", None),
        P("dp", None),
        P("dp", None),
        P("dp", None),
        P(),
        P(),
        P(),
        P(None, "dp", None),
        P(None, "dp", None),
        P(None, "dp", None),
        P(("dp", "expert"), None),
        P(("dp", "expert"), None),
        P(("dp", "expert"), None),
        P(("dp", "expert")),
    )
    return jax.shard_map(
        body,
        mesh=mesh,
        in_specs=placed,
        out_specs=(
            P(("dp", "expert"), None),
            P(("dp", "expert"), None),
            P(),
            P("dp", None),
            P("dp", None),
            P("dp", None),
            P("dp", None),
            P(),
            P(),
            P(),
            P(None, "dp", None),
            P(None, "dp", None),
            P(None, "dp", None),
        ),
        check_vma=False,
    )
```

```python
import math

import jax
import jax.numpy as jnp
import numpy as np
from jax import lax
from jax.experimental import pallas as pl
from jax.experimental.pallas import tpu as pltpu
from jax.sharding import PartitionSpec as P

D = 1024
H = 16
HEAD = 64
EXPERTS = 4
BUCKETS = 32
LONG = 512
SHORT = 128
PAIR = 2 * HEAD
TILES = LONG // SHORT
EPSILON = 1e-06
FF_TILE = 256
LAY_TILE = 512
MIB = 1024 * 1024
MASKED = -1e30


def bucket_of(offsets):
    distance = np.abs(offsets)
    half_count = BUCKETS // 2
    exact_count = half_count // 2
    widened = np.maximum(distance, 1)
    far_bucket = exact_count + np.floor(
        np.log(widened / exact_count) / np.log(128.0 / exact_count) * (half_count - exact_count)
    ).astype(np.int32)
    far_bucket = np.minimum(far_bucket, half_count - 1)
    inside = np.where(distance < exact_count, distance, far_bucket)
    return (np.where(offsets > 0, half_count, 0) + inside).astype(np.int32)


def near_buckets():
    places = np.arange(SHORT)
    inside = places[:, None] - places[None, :]
    return np.stack([bucket_of(SHORT * step + inside) for step in (-1, 0, 1)]).reshape(-1)


def near_onehot():
    buckets = jnp.asarray(near_buckets().astype(np.int8)).astype(jnp.int32)
    return (jnp.arange(BUCKETS, dtype=jnp.int32)[:, None] == buckets[None, :]).astype(jnp.float32)


FAR_BEFORE = BUCKETS // 2 - 1
FAR_AFTER = BUCKETS - 1


def ring_order(count):
    cols = 4 if count >= 16 else 2
    rows = count // cols
    cycle = [(0, col) for col in range(cols)]
    for row in range(1, rows):
        span = range(cols - 1, 0, -1) if row % 2 else range(1, cols)
        cycle += [(row, col) for col in span]
    cycle += [(row, 0) for row in range(rows - 1, 0, -1)]
    return [row * cols + col for row, col in cycle]


def ring_tables(count):
    ring = ring_order(count)
    ahead = [(ring[i], ring[(i + 1) % count]) for i in range(count)]
    behind = [(there, here) for here, there in ahead]
    place = {index: i for i, index in enumerate(ring)}
    seats = np.asarray(
        [[ring[(place[g] + d) % count] for d in range(count)] for g in range(count)], np.int32
    )
    return ahead, behind, seats


def after(value, *others):
    return lax.optimization_barrier((value, *others))[0]


def matmul(left, right):
    return jnp.dot(left, right, preferred_element_type=jnp.float32)


def dot_dims(left, right, left_dim, right_dim):
    return lax.dot_general(
        left, right, (((left_dim,), (right_dim,)), ((), ())), preferred_element_type=jnp.float32
    )


def tie(values, others):
    values = tuple(values)
    return lax.optimization_barrier(values + tuple(others))[: len(values)]


def pick(array, index, axis=0):
    return lax.dynamic_index_in_dim(array, index, axis, keepdims=False, allow_negative_indices=False)


def lay_kernel(places, spots_ref, *refs):
    *piece_refs, out_ref = refs
    for piece_ref, place in zip(piece_refs, places):
        index = place(spots_ref)
        out_ref[index] = piece_ref[: index[-1].size]


def lay_together(spots, pieces, shape, places, tile, start=0):
    lead = (0,) * (len(shape) - 1)
    first = start // tile
    return pl.pallas_call(
        lambda *refs: lay_kernel(places, *refs),
        grid_spec=pltpu.PrefetchScalarGridSpec(
            num_scalar_prefetch=1,
            grid=(shape[-1] // tile,),
            in_specs=[
                pl.BlockSpec((piece.shape[0], tile), lambda i, spots: (0, i + first))
                for piece in pieces
            ],
            out_specs=pl.BlockSpec((*shape[:-1], tile), lambda i, spots: (*lead, i)),
        ),
        out_shape=jax.ShapeDtypeStruct(shape, jnp.bfloat16),
        compiler_params=pltpu.CompilerParams(vmem_limit_bytes=16 * MIB),
        cost_estimate=pl.CostEstimate(
            flops=0, bytes_accessed=4 * math.prod(shape), transcendentals=0
        ),
    )(spots, *pieces)


class RingGather:
    def __init__(self, block, seat):
        self.count = lax.axis_size("dp")
        self.ahead, self.behind, _ = ring_tables(self.count)
        self.seat, self.rows, self.taken = seat, block.shape[0], 0
        self.low = self.high = block
        self.mid = min((self.rows // 2 + 15) // 16 * 16, self.rows)
        self.pieces = [(block, 0, 0)]

    def arrived(self):
        return (self.low, self.high)

    def step(self, *others):
        half = self.count // 2
        if self.taken >= half:
            return
        if self.taken == 0:
            self.sent = (low,) = tie((self.low,), others)
            high = low
        else:
            self.sent = low, high = tie((self.low, self.high), others)
        self.taken += 1
        last = self.taken == half
        low, high = (low[: self.mid], high[self.mid :]) if last else (low, high)
        self.low = lax.ppermute(low, "dp", self.ahead)
        self.high = lax.ppermute(high, "dp", self.behind)
        self.pieces += [
            (self.low, (half if last else -self.taken) % self.count, 0),
            (self.high, self.taken, self.mid if last else 0),
        ]

    def finish(self, *others):
        while self.taken < self.count // 2:
            self.step()
        columns = self.pieces[0][0].shape[1]
        places = []
        for piece, step, start in self.pieces:

            def place(spots, step=step, start=start, rows=piece.shape[0]):
                return (spots[step], pl.ds(start, rows))

            places.append(place)
        out = lay_together(
            after(self.seat, *others),
            [piece for piece, _, _ in self.pieces],
            (self.count, self.rows, columns),
            places,
            columns // 2,
        )
        return out.reshape(-1, columns)


def ring_sum_kernel(received, outs, *refs):
    own_refs, received_refs = refs[:outs], refs[outs:-outs]
    side = pl.program_id(0)
    for out in range(outs):
        total = own_refs[out][...].astype(jnp.float32)
        for received_ref, (target, only) in zip(received_refs, received):
            if target == out:
                more = received_ref[...].astype(jnp.float32)
                total = total + (more if only is None else jnp.where(side == only, more, 0.0))
        refs[out - outs][...] = total.astype(jnp.bfloat16)


class RingSum:
    def __init__(self, parts, seat, entry=None):
        self.count = lax.axis_size("dp")
        self.ahead, self.behind, _ = ring_tables(self.count)
        self.seat, self.parts, self.entry, self.taken = seat, parts, entry, 0
        if entry is None:
            self.shape = (parts.shape[1], parts.shape[2] // 2)
        else:
            self.shape = (D // self.count, parts.shape[2])
        self.low = self.high = None

    def own(self, step, side=0):
        step = step % self.count
        if self.entry is None:
            return self.parts, pl.BlockSpec(
                (None, *self.shape), lambda i, seat: (seat[step], 0, i + side)
            )
        first = self.entry + side
        return self.parts, pl.BlockSpec(
            (None, *self.shape), lambda i, seat: (first + i, seat[step], 0)
        )

    def call(self, own, received, operands, others=(), halves=2, joined=False):
        moved = 2 * halves * math.prod(self.shape)

        def block(item):
            if item.shape[0] == 1:
                return pl.BlockSpec((None, *self.shape), lambda i, seat: (0, 0, 0))
            return pl.BlockSpec((None, *self.shape), lambda i, seat: (i, 0, 0))

        if joined:
            out_spec = pl.BlockSpec(self.shape, lambda i, seat: (0, i))
            out_shape = (self.shape[0], halves * self.shape[1])
        else:
            out_spec = pl.BlockSpec((None, *self.shape), lambda i, seat: (i, 0, 0))
            out_shape = (halves, *self.shape)
        return pl.pallas_call(
            lambda seat_ref, *refs: ring_sum_kernel(received, len(own), *refs),
            grid_spec=pltpu.PrefetchScalarGridSpec(
                num_scalar_prefetch=1,
                grid=(halves,),
                in_specs=[spec for _, spec in own] + [block(item) for item in operands],
                out_specs=[out_spec] * len(own),
            ),
            out_shape=[jax.ShapeDtypeStruct(out_shape, jnp.bfloat16)] * len(own),
            compiler_params=pltpu.CompilerParams(
                vmem_limit_bytes=(16 if self.entry is None else 40) * MIB
            ),
            cost_estimate=pl.CostEstimate(
                flops=2 * moved,
                bytes_accessed=moved * (len(operands) + 2 * len(own)),
                transcendentals=0,
            ),
        )(after(self.seat, *others), *(part for part, _ in own), *operands)

    def arrived(self):
        return (self.low, self.high)

    def received(self, targets):
        single = self.taken == 1
        return [(targets[0], 0 if single else None), (targets[1], 1 if single else None)]

    def step(self, *others):
        half = self.count // 2
        if self.taken >= half:
            return
        distance = half - self.taken
        if self.taken:
            received, operands = self.received((0, 1)), tie(self.arrived(), others)
            sent = self.call(self.following, received, operands)
        else:
            own = (self.own(distance), self.own(-distance, 1))
            sent = self.call(own, [], (), others, 1)
        self.low = lax.ppermute(sent[0], "dp", self.ahead)
        self.high = lax.ppermute(sent[1], "dp", self.behind)
        self.taken += 1
        distance -= 1
        steps = (distance, -distance) if distance else (0,)
        self.following = [self.own(step) for step in steps]
        self.sent = tuple(sent)

    def finish(self, *others, joined=False):
        while self.taken < self.count // 2:
            self.step()
        received, operands = self.received((0, 0)), tie(self.arrived(), others)
        return self.call(self.following, received, operands, joined=joined)[0]


def swap(value, bit):
    count = lax.axis_size("expert")
    return lax.ppermute(value, "expert", [(i, i ^ bit) for i in range(count)])


class Exchange:
    def __init__(self, own, near, far):
        self.own, self.count, self.rows = own, lax.axis_size("expert"), own.shape[0]
        self.near, self.last = swap(near, 1), None
        if self.count == 4:
            self.far = swap(far, 2)
        else:
            blocks = far.reshape(-1, self.rows, far.shape[1])
            self.far = [swap(block, bit + 2) for bit, block in enumerate(blocks)]

    def forward(self, *others):
        if self.count == 4:
            self.last = swap(after(self.far, *others)[self.rows :], 1)
        return self

    def arrived(self):
        return (self.near, self.last) if self.count == 4 else tuple(self.far)

    def together(self, seat, *others):
        if self.count == 4:
            pieces = [self.own, self.near, self.far, self.last]
        else:
            pieces = [self.own, self.near, *self.far]
        places = [
            lambda spots, d=d: (pl.ds(d * self.rows, self.rows),) for d in range(len(pieces))
        ]
        shape = (self.count * self.rows, self.own.shape[1])
        return lay_together(after(seat, *others), pieces, shape, places, LAY_TILE)


class Spread:
    def __init__(self, value):
        self.bit = lax.axis_size("expert") // 2
        self.held = {0: (value, None)}
        self.hop()

    @classmethod
    def hop_own(cls, first, second, both, *others):
        swapped = swap(after(both, *others), 1)
        for lead, spread in enumerate((first, second)):
            spread.held[0] = (both, lead)
            spread.held[1] = (swapped, lead)
            spread.own_last = (swapped,)

    def hop(self, *others):
        if not self.bit:
            return
        keys = [key for key in self.held if key ^ self.bit not in self.held]
        items = [self.held[key] for key in keys]
        items = tie((item if lead is None else item[lead] for item, lead in items), others)
        fresh = {key ^ self.bit: swap(item, self.bit) for key, item in zip(keys, items)}
        self.last = tuple(fresh.values())
        self.held.update({key: (item, None) for key, item in fresh.items()})
        self.bit //= 2

    def arrived(self):
        return self.last

    def outputs(self, device, *others):
        while self.bit:
            self.hop()
        keys = sorted(self.held)
        shares = len(keys) // EXPERTS
        rows, columns = self.held[0][0].shape[-2:]
        tile = columns // 2

        def spec(lead):
            if lead is None:
                return pl.BlockSpec((rows, tile), lambda i, spots: (0, i))
            return pl.BlockSpec((None, rows, tile), lambda i, spots: (lead, 0, i))

        def kernel(spots_ref, *refs):
            *block_refs, out_ref = refs
            for first in range(0, len(keys), shares):
                total = block_refs[first][...].astype(jnp.float32)
                for block_ref in block_refs[first + 1 : first + shares]:
                    total = total + block_ref[...].astype(jnp.float32)
                out_ref[spots_ref[first]] = total

        spots = jnp.stack([device ^ key if shares == 1 else lax.div(device ^ key, shares) for key in keys])
        return pl.pallas_call(
            kernel,
            grid_spec=pltpu.PrefetchScalarGridSpec(
                num_scalar_prefetch=1,
                grid=(2,),
                in_specs=[spec(self.held[key][1]) for key in keys],
                out_specs=pl.BlockSpec((EXPERTS, rows, tile), lambda i, spots: (0, 0, i)),
            ),
            out_shape=jax.ShapeDtypeStruct((EXPERTS, rows, columns), jnp.float32),
            compiler_params=pltpu.CompilerParams(vmem_limit_bytes=24 * MIB),
            cost_estimate=pl.CostEstimate(
                flops=0, bytes_accessed=6 * EXPERTS * rows * columns, transcendentals=0
            ),
        )(after(spots, *others), *(self.held[key][0] for key in keys))


class SumAll:
    def __init__(self, parts):
        self.shapes = [part.shape for part in parts]
        self.flat = jnp.concatenate([part.reshape(-1, 128) for part in parts], 0)
        self.hops = []
        for axis in ("expert", "dp"):
            bit, count = 1, lax.axis_size(axis)
            while bit < count:
                self.hops.append((axis, [(i, i ^ bit) for i in range(count)]))
                bit *= 2
        over_x = self.hops.pop(1)
        self.hops.append(over_x)

    def hop(self, *others):
        if not self.hops:
            return self.flat
        axis, pairs = self.hops.pop(0)
        flat = after(self.flat, *others)
        self.flat = flat + lax.ppermute(flat, axis, pairs)
        return self.flat

    def finish(self, *others):
        while self.hops:
            self.hop(*others)
        sums, start = [], 0
        for shape in self.shapes:
            rows = math.prod(shape) // 128
            sums.append(self.flat[start : start + rows].reshape(shape))
            start += rows
        return sums


def norm_backward(grad_rows, row_data, inverse, gain_vec):
    scaled = grad_rows * gain_vec
    inner_mean = jnp.mean(scaled * row_data, -1, keepdims=True)
    grad_input = inverse * scaled - row_data * inverse * inverse * inverse * inner_mean
    return (grad_input, jnp.sum(grad_rows * row_data * inverse, 0))


def other_head_zeroed(rows_t, head):
    own = rows_t[head * HEAD : (head + 1) * HEAD]
    rest = jnp.zeros_like(own)
    return jnp.concatenate([own, rest] if head == 0 else [rest, own], 0)


def tile_biases(bias_ref, far_ref, pair, head, penalty):
    near = {
        -1: bias_ref[head, 0] + penalty,
        0: bias_ref[head, 1],
        1: bias_ref[head, 2] + penalty,
    }
    before = far_ref[0, 2 * pair + head] + penalty
    later = far_ref[1, 2 * pair + head] + penalty
    return lambda step: near[step] if abs(step) < 2 else (before if step < 0 else later)


def transposed(rows):
    return rows.astype(jnp.float32).T


def attend_forward_kernel(
    flag_ref, far_ref, q_ref, k_ref, v_ref, bias_ref, ctx_ref, lse_ref
):
    block, pair = pl.program_id(0), pl.program_id(1)
    penalty = jnp.where(flag_ref[block] == 0, 0.0, MASKED).astype(jnp.float32)
    query_t = (transposed(q_ref[...]) * (1.0 / math.sqrt(HEAD))).astype(jnp.bfloat16)
    value_t = transposed(v_ref[...]).astype(jnp.bfloat16)
    key_rows = k_ref[...]
    parts = []
    for head in range(2):
        bias = tile_biases(bias_ref, far_ref, pair, head, penalty)
        scores = dot_dims(key_rows, other_head_zeroed(query_t, head), 1, 0)
        value_head = value_t[head * HEAD : (head + 1) * HEAD]
        pieces = []
        for col in range(TILES):
            cols = slice(col * SHORT, (col + 1) * SHORT)
            panel = jnp.concatenate(
                [
                    scores[row * SHORT : (row + 1) * SHORT, cols] + bias(row - col)
                    for row in range(TILES)
                ],
                0,
            )
            highest = jnp.max(panel, 0, keepdims=True)
            raised = jnp.exp(panel - highest)
            total = jnp.sum(raised, 0, keepdims=True)
            piece = matmul(value_head, raised.astype(jnp.bfloat16))
            pieces.append(piece / total)
            lse_ref[0, 0, head : head + 1, cols] = highest + jnp.log(total)
        parts.append(pieces)
    for col in range(TILES):
        joined = jnp.concatenate([parts[0][col], parts[1][col]], 0)
        ctx_ref[col * SHORT : (col + 1) * SHORT, :] = joined.T.astype(jnp.bfloat16)


def attend_forward(qkv, flags, far, bias):
    tok_count = qkv.shape[0]
    blocks = tok_count // LONG
    pairs = H // 2

    def column(first):
        return pl.BlockSpec((LONG, PAIR), lambda b, p, flag: (b, first + p))

    return pl.pallas_call(
        attend_forward_kernel,
        grid_spec=pltpu.PrefetchScalarGridSpec(
            num_scalar_prefetch=1,
            grid=(blocks, pairs),
            in_specs=[
                pl.BlockSpec(memory_space=pltpu.SMEM),
                column(0),
                column(pairs),
                column(2 * pairs),
                pl.BlockSpec((2, 3, SHORT, SHORT), lambda b, p, flag: (p, 0, 0, 0)),
            ],
            out_specs=[
                column(0),
                pl.BlockSpec((1, 1, 2, LONG), lambda b, p, flag: (b, p, 0, 0)),
            ],
        ),
        out_shape=[
            jax.ShapeDtypeStruct((tok_count, D), jnp.bfloat16),
            jax.ShapeDtypeStruct((blocks, pairs, 2, LONG), jnp.float32),
        ],
        compiler_params=pltpu.CompilerParams(vmem_limit_bytes=16 * MIB),
        cost_estimate=pl.CostEstimate(
            flops=8 * H * LONG * LONG * HEAD * blocks,
            bytes_accessed=8 * tok_count * D + 12 * H * SHORT * SHORT,
            transcendentals=H * LONG * LONG * blocks,
        ),
    )(flags, far, qkv, qkv, qkv, bias)


def attend_backward_kernel(
    flag_ref,
    far_ref,
    q_ref,
    k_ref,
    v_ref,
    grad_ref,
    lse_ref,
    bias_ref,
    dq_ref,
    dk_ref,
    dv_ref,
    near_ref,
    away_ref,
    weight_scr,
    score_scr,
):
    pair, block = pl.program_id(0), pl.program_id(1)
    penalty = jnp.where(flag_ref[block] == 0, 0.0, MASKED).astype(jnp.float32)
    scaled = (q_ref[...].astype(jnp.float32) * (1.0 / math.sqrt(HEAD))).astype(jnp.bfloat16)
    query_t = transposed(scaled).astype(jnp.bfloat16)
    grad_t = transposed(grad_ref[...]).astype(jnp.bfloat16)
    key_t = transposed(k_ref[...]).astype(jnp.bfloat16)
    key_rows, value_rows, grad_rows = k_ref[...], v_ref[...], grad_ref[...]

    @pl.when(block == 0)
    def _():
        near_ref[...] = jnp.zeros_like(near_ref)
        away_ref[...] = jnp.zeros_like(away_ref)

    query_parts, key_parts, value_parts = [], [], []
    for head in range(2):
        bias = tile_biases(bias_ref, far_ref, pair, head, penalty)
        scores = dot_dims(key_rows, other_head_zeroed(query_t, head), 1, 0)
        grad_probs = dot_dims(value_rows, other_head_zeroed(grad_t, head), 1, 0)
        key_head = key_t[head * HEAD : (head + 1) * HEAD]
        near = {-1: None, 0: None, 1: None}
        away = [None, None]
        for col in range(TILES):
            cols = slice(col * SHORT, (col + 1) * SHORT)
            total = lse_ref[0, 0, head : head + 1, cols]
            probs = jnp.exp(
                jnp.concatenate(
                    [
                        scores[row * SHORT : (row + 1) * SHORT, cols] + bias(row - col)
                        for row in range(TILES)
                    ],
                    0,
                )
                - total
            )
            panel = grad_probs[:, cols]
            inner = jnp.sum(probs * panel, 0, keepdims=True)
            grad_scores = (probs * (panel - inner)).astype(jnp.bfloat16)
            weight_scr[:, cols] = probs.astype(jnp.bfloat16)
            score_scr[:, cols] = grad_scores
            rounded = grad_scores.astype(jnp.float32)
            for row in range(TILES):
                tile = rounded[row * SHORT : (row + 1) * SHORT]
                step = row - col
                if abs(step) < 2:
                    near[step] = tile if near[step] is None else near[step] + tile
                else:
                    side = 0 if step < 0 else 1
                    tile = jnp.sum(tile, 0, keepdims=True)
                    away[side] = tile if away[side] is None else away[side] + tile
        for step in (-1, 0, 1):
            near_ref[head, step + 1] += near[step]
        for side in range(2):
            away_ref[0, head, side : side + 1, :] += away[side]
        query_parts.append(matmul(key_head, score_scr[...]))
        key_parts.append(matmul(score_scr[...], scaled))
        value_parts.append(matmul(weight_scr[...], grad_rows))
    lane = lax.broadcasted_iota(jnp.int32, (LONG, PAIR), 1)
    dk_ref[...] = jnp.where(lane < HEAD, key_parts[0], key_parts[1]).astype(jnp.bfloat16)
    dv_ref[...] = jnp.where(lane < HEAD, value_parts[0], value_parts[1]).astype(jnp.bfloat16)
    joined = jnp.concatenate(query_parts, 0) * (1.0 / math.sqrt(HEAD))
    dq_ref[...] = joined.T.astype(jnp.bfloat16)


def attend_backward(qkv, grad_context, lse, flags, far, bias):
    tok_count = qkv.shape[0]
    blocks = tok_count // LONG
    pairs = H // 2

    def column(first):
        return pl.BlockSpec((LONG, PAIR), lambda p, b, flag: (b, first + p))

    rows = jax.ShapeDtypeStruct((tok_count, D), jnp.bfloat16)
    return pl.pallas_call(
        attend_backward_kernel,
        grid_spec=pltpu.PrefetchScalarGridSpec(
            num_scalar_prefetch=1,
            grid=(pairs, blocks),
            in_specs=[
                pl.BlockSpec(memory_space=pltpu.SMEM),
                column(0),
                column(pairs),
                column(2 * pairs),
                column(0),
                pl.BlockSpec((1, 1, 2, LONG), lambda p, b, flag: (b, p, 0, 0)),
                pl.BlockSpec((2, 3, SHORT, SHORT), lambda p, b, flag: (p, 0, 0, 0)),
            ],
            out_specs=[
                column(0),
                column(0),
                column(0),
                pl.BlockSpec((2, 3, SHORT, SHORT), lambda p, b, flag: (p, 0, 0, 0)),
                pl.BlockSpec((1, 2, 2, SHORT), lambda p, b, flag: (p, 0, 0, 0)),
            ],
            scratch_shapes=[
                pltpu.VMEM((LONG, LONG), jnp.bfloat16),
                pltpu.VMEM((LONG, LONG), jnp.bfloat16),
            ],
        ),
        out_shape=[
            rows,
            rows,
            rows,
            jax.ShapeDtypeStruct((H, 3, SHORT, SHORT), jnp.float32),
            jax.ShapeDtypeStruct((pairs, 2, 2, SHORT), jnp.float32),
        ],
        compiler_params=pltpu.CompilerParams(vmem_limit_bytes=24 * MIB),
        cost_estimate=pl.CostEstimate(
            flops=20 * H * LONG * LONG * HEAD * blocks,
            bytes_accessed=16 * tok_count * D + 24 * H * SHORT * SHORT,
            transcendentals=H * LONG * LONG * blocks,
        ),
    )(flags, far, qkv, qkv, qkv, grad_context, lse, bias)


ROW_TILE = 256
GELU_SCALE = math.sqrt(2.0 / math.pi)
GELU_CUBE = 0.044715


def row_tiles(rows):
    return [slice(start, min(start + ROW_TILE, rows)) for start in range(0, rows, ROW_TILE)]


def gate_kernel(rows_ref, weight_ref, act_ref, slope_ref):
    for part in row_tiles(rows_ref.shape[0]):
        pre = matmul(rows_ref[part, :], weight_ref[...])
        square = pre * pre
        angle = jnp.tanh(pre * (GELU_SCALE + (GELU_SCALE * GELU_CUBE) * square))
        half = 0.5 + 0.5 * angle
        act_ref[part, :] = (pre * half).astype(jnp.bfloat16)
        bend = (0.5 * GELU_SCALE) + (1.5 * GELU_SCALE * GELU_CUBE) * square
        slope_ref[part, :] = (half + pre * (1.0 - angle * angle) * bend).astype(jnp.bfloat16)


def up_kernel(rows_ref, weight_ref, act_ref, slope_ref, grads_ref, hid_ref, lift_ref, down_ref):
    for part in row_tiles(rows_ref.shape[0]):
        lift = matmul(rows_ref[part, :], weight_ref[...])
        hid_ref[part, :] = (act_ref[part, :].astype(jnp.float32) * lift).astype(jnp.bfloat16)
        lift_ref[part, :] = (slope_ref[part, :].astype(jnp.float32) * lift).astype(jnp.bfloat16)
    down_ref[...] = dot_dims(hid_ref[...], grads_ref[...], 0, 0).astype(jnp.bfloat16)


def hidden_back_kernel(grads_ref, down_ref, lift_ref, act_ref, rows_t_ref, out_ref):
    for part in row_tiles(grads_ref.shape[0]):
        back = dot_dims(grads_ref[part, :], down_ref[...], 1, 1)
        out_ref[0, part, :] = (back * lift_ref[part, :].astype(jnp.float32)).astype(jnp.bfloat16)
        out_ref[1, part, :] = (back * act_ref[part, :].astype(jnp.float32)).astype(jnp.bfloat16)
    rows = rows_t_ref.shape[0]
    for part in row_tiles(rows):
        out_ref[2, part, :] = matmul(rows_t_ref[part, :], out_ref[0]).astype(jnp.bfloat16)
        out_ref[3, part, :] = matmul(rows_t_ref[part, :], out_ref[1]).astype(jnp.bfloat16)
    rest = jnp.zeros((2, out_ref.shape[1] - rows, out_ref.shape[2]), jnp.bfloat16)
    out_ref[2:, rows:, :] = rest


def rows_back_kernel(pre_ref, up_ref, gate_w_ref, up_w_ref, *out_refs):
    total = dot_dims(pre_ref[...], gate_w_ref[...], 1, 1) + dot_dims(up_ref[...], up_w_ref[...], 1, 1)
    start = 0
    for out_ref in out_refs:
        rows = out_ref.shape[0]
        out_ref[...] = total[start : start + rows].astype(jnp.bfloat16)
        start += rows


def kernel_call(kernel, operands, in_specs, out_specs, out_shape, steps, flops, vmem):
    moved = sum(2 * math.prod(item.shape) for item in (*operands, *out_shape))
    return pl.pallas_call(
        kernel,
        grid=(steps,),
        in_specs=in_specs,
        out_specs=out_specs,
        out_shape=[jax.ShapeDtypeStruct(item.shape, jnp.bfloat16) for item in out_shape],
        compiler_params=pltpu.CompilerParams(vmem_limit_bytes=vmem * MIB),
        cost_estimate=pl.CostEstimate(flops=flops, bytes_accessed=moved, transcendentals=0),
    )(*operands)


def width_tiles(width):
    return pl.cdiv(width, FF_TILE)


def whole_spec(shape, buffers=2):
    return pl.BlockSpec(shape, lambda i: (0, 0), pipeline_mode=pl.Buffered(buffers))


def gate_forward(rows, weight):
    count, width = rows.shape[0], weight.shape[1]
    tile = pl.BlockSpec((count, FF_TILE), lambda i: (0, i))
    shape = jax.ShapeDtypeStruct((count, width), jnp.bfloat16)
    return kernel_call(
        gate_kernel,
        (rows, weight),
        [whole_spec(rows.shape), pl.BlockSpec((D, FF_TILE), lambda i: (0, i))],
        [tile, tile],
        [shape, shape],
        width_tiles(width),
        2 * count * D * width,
        59,
    )


def up_forward(rows, weight, act, slope, grads):
    count, width = rows.shape[0], weight.shape[1]
    tile = pl.BlockSpec((count, FF_TILE), lambda i: (0, i))
    shape = jax.ShapeDtypeStruct((count, width), jnp.bfloat16)
    return kernel_call(
        up_kernel,
        (rows, weight, act, slope, grads),
        [
            whole_spec(rows.shape),
            pl.BlockSpec((D, FF_TILE), lambda i: (0, i)),
            tile,
            tile,
            whole_spec(grads.shape),
        ],
        [tile, tile, pl.BlockSpec((FF_TILE, D), lambda i: (i, 0))],
        [shape, shape, jax.ShapeDtypeStruct((width, D), jnp.bfloat16)],
        width_tiles(width),
        4 * count * D * width,
        59,
    )


def hidden_back(grads, weight, lift, act, rows_t):
    count, width = lift.shape
    tile = pl.BlockSpec((count, FF_TILE), lambda i: (0, i))
    return kernel_call(
        hidden_back_kernel,
        (grads, weight, lift, act, rows_t),
        [
            whole_spec(grads.shape),
            pl.BlockSpec((FF_TILE, D), lambda i: (i, 0)),
            tile,
            tile,
            whole_spec(rows_t.shape),
        ],
        [pl.BlockSpec((4, count, FF_TILE), lambda i: (0, 0, i))],
        [jax.ShapeDtypeStruct((4, count, width), jnp.bfloat16)],
        width_tiles(width),
        6 * count * D * width,
        59,
    )[0]


def rows_back(hidden_grads, gate_weight, up_weight, splits):
    _, count, width = hidden_grads.shape
    weight_tile = pl.BlockSpec((ROW_TILE, width), lambda i: (i, 0))

    def entry(number):
        return pl.BlockSpec(
            (None, count, width), lambda i: (number, 0, 0), pipeline_mode=pl.Buffered(1)
        )

    return kernel_call(
        rows_back_kernel,
        (hidden_grads, hidden_grads, gate_weight, up_weight),
        [entry(0), entry(1), weight_tile, weight_tile],
        [pl.BlockSpec((rows, ROW_TILE), lambda i: (0, i)) for rows in splits],
        [jax.ShapeDtypeStruct((rows, D), jnp.bfloat16) for rows in splits],
        D // ROW_TILE,
        4 * count * D * width,
        59,
    )


def table_sums(near, away):
    near_part = lax.dot_general(
        near_onehot(),
        near.reshape(H, -1),
        (((1,), (1,)), ((), ())),
        precision=lax.Precision.HIGHEST,
        preferred_element_type=jnp.float32,
    )
    far_part = jnp.sum(away, -1).reshape(H, 2)
    sides = np.zeros((BUCKETS, 2), np.float32)
    sides[FAR_BEFORE, 0] = sides[FAR_AFTER, 1] = 1.0
    return near_part + jnp.sum(sides[:, None, :] * far_part[None], -1)


def body(
    tokens,
    cotangent,
    gain_one,
    w_query,
    w_key,
    w_value,
    w_out,
    rel_table,
    gain_two,
    w_router,
    w_gate,
    w_up,
    w_down,
    expert_ids,
    slot_index,
    slot_kept,
    seq_bucket,
):
    tok_count = tokens.shape[0]
    dp_count = lax.axis_size("dp")
    owner_count = lax.axis_size("expert")
    shares = owner_count // EXPERTS
    group = lax.axis_index("dp")
    device = lax.axis_index("expert")
    expert = device if shares == 1 else lax.div(device, shares)
    core = device & 1
    seat = pick(jnp.asarray(ring_tables(dp_count)[2]), group)

    half_rows = w_query.shape[0] // 2

    def own_half(weight):
        return lax.dynamic_slice_in_dim(
            weight, core * half_rows, half_rows, 0, allow_negative_indices=False
        )

    slot_quota = 5 * tok_count // (2 * EXPERTS * owner_count)
    slot_span = owner_count * slot_quota
    owners_each = owner_count // shares
    block_rows = owners_each * slot_quota
    slot_room = owner_count * block_rows

    def routes(ids, slots, kept):
        owner = slots // slot_span
        dest = ids * shares + owner // owners_each
        local_slot = (
            (dest ^ device) * block_rows
            + (owner % owners_each) * slot_quota
            + slots % slot_span
            - device * slot_quota
        )
        target = jnp.where(kept == 1, local_slot, slot_room)
        room = jnp.arange(slot_room, dtype=jnp.int32)
        from_slot = [
            (target[:, k : k + 1] == room[None, :]).astype(jnp.bfloat16) for k in range(2)
        ]
        to_slot = jnp.logical_or(
            target[:, 0][None, :] == room[:, None], target[:, 1][None, :] == room[:, None]
        ).astype(jnp.bfloat16)
        return from_slot, to_slot

    def parts_of(rows):
        return rows[:block_rows], rows[block_rows : 2 * block_rows], rows[2 * block_rows :]

    def outgoing(rows, to_slot):
        return [matmul(part, rows).astype(jnp.bfloat16) for part in reversed(parts_of(to_slot))][::-1]

    def route(rows):
        logits = matmul(rows, w_router)
        raised = jnp.exp(logits - jnp.max(logits, -1, keepdims=True))
        return raised / jnp.sum(raised, -1, keepdims=True)

    weight_ring = RingGather(
        jnp.concatenate([own_half(weight) for weight in (w_query, w_key, w_value, w_out)], 1), seat
    )
    weight_ring.step()
    row_one = tokens.astype(jnp.float32)
    inv_one = lax.rsqrt(jnp.mean(row_one * row_one, -1, keepdims=True) + EPSILON)
    normed = (row_one * inv_one * gain_one).astype(jnp.bfloat16)
    theirs = [swap(weight_ring.pieces[0][0], 1)]

    def weight_step(*others):
        if weight_ring.taken < dp_count // 2:
            weight_ring.step(*others)
            theirs.extend(swap(piece, 1) for piece in weight_ring.sent)

    weight_step(inv_one)
    ids, slots, kept = tie((expert_ids, slot_index, slot_kept), weight_ring.sent)
    from_slot, to_slot = routes(ids, slots, kept)
    def core_columns(rows):
        split = rows.reshape(tok_count, dp_count, 2, half_rows)
        return [pick(split, side, 2).reshape(tok_count, -1) for side in (core, 1 - core)]

    normed_mine, normed_other = core_columns(normed)
    weight_step(to_slot, theirs[0], normed_mine, normed_other)
    cots, table = tie((cotangent, rel_table), weight_ring.sent)
    cot_blocks = outgoing(cots, to_slot)
    bias = lax.dot_general(
        after(table, *cot_blocks),
        near_onehot(),
        (((0,), (0,)), ((), ())),
        precision=lax.Precision.HIGHEST,
        preferred_element_type=jnp.float32,
    ).reshape(H, 3, SHORT, SHORT)
    far = jnp.stack([rel_table[FAR_BEFORE], rel_table[FAR_AFTER]])
    weight_step(bias, *theirs[1:3])
    while weight_ring.taken < dp_count // 2:
        weight_step()
    gate_ring = RingGather(pick(w_gate, expert), seat)
    gate_ring.step(*weight_ring.sent)
    theirs.extend(swap(piece, 1) for piece in weight_ring.arrived())
    places = []
    for side in range(2):
        for piece, step, start in weight_ring.pieces:

            def place(spots, step=step, side=side, start=start, rows=piece.shape[0]):
                return (spots[step], spots[dp_count + side], pl.ds(start, rows))

            places.append(place)
    spots = jnp.concatenate([seat, jnp.stack([core, 1 - core])])
    pieces = [piece for piece, _, _ in weight_ring.pieces] + theirs
    full_qkv = lay_together(spots, pieces, (dp_count, 2, half_rows, 3 * D), places, LAY_TILE)
    full_out = lay_together(spots, pieces, (dp_count, 2, half_rows, D), places, LAY_TILE, 3 * D)
    full_qkv, full_out = full_qkv.reshape(D, 3 * D), full_out.reshape(D, D)
    up_own, down_own = tie((pick(w_up, expert), pick(w_down, expert)), (full_qkv,))
    up_ring = RingGather(up_own, seat)
    down_ring = RingGather(down_own, seat)

    gate_ring.step(full_qkv, up_own, down_own)
    (normed_now,) = tie((normed,), gate_ring.sent)
    qkv = matmul(normed_now, full_qkv).astype(jnp.bfloat16)
    context, lse = attend_forward(qkv, seq_bucket, far, bias)
    (context,) = tie((context,), gate_ring.arrived())
    gate_ring.step(context)
    (context,) = tie((context,), gate_ring.sent)
    mid_rows = row_one + matmul(context, full_out)
    inv_two = lax.rsqrt(jnp.mean(mid_rows * mid_rows, -1, keepdims=True) + EPSILON)
    normed_two = (mid_rows * inv_two * gain_two).astype(jnp.bfloat16)
    row_blocks = outgoing(normed_two, to_slot)
    row_exchange = Exchange(*row_blocks)
    gate_ring.step(*row_blocks)
    up_ring.step(*gate_ring.sent)
    gate_full = gate_ring.finish(*up_ring.sent)
    router = route(after(normed_two, gate_full))
    chosen = (ids[:, :, None] == jnp.arange(EXPERTS, dtype=jnp.int32)).astype(jnp.float32)
    kept_pair = kept.astype(jnp.float32)
    gate_vals = jnp.sum(chosen * router[:, None, :], -1) * kept_pair
    up_ring.step(gate_vals)

    slot_rows = row_exchange.forward(*up_ring.sent).together(seat)
    cot_exchange = Exchange(*tie(cot_blocks, (slot_rows,)))
    down_ring.step(slot_rows)
    (gate_now,) = tie((gate_full,), (*down_ring.sent, cot_exchange.near))
    act, slope = gate_forward(slot_rows, gate_now)
    act, slope = tie((act, slope), up_ring.arrived())
    up_ring.step(act)
    (rows_now,) = tie((slot_rows,), up_ring.sent)
    slot_gate = lax.dynamic_index_in_dim(
        route(rows_now), expert, 1, allow_negative_indices=False
    )
    slot_rows_t = rows_now.T
    cot_exchange.forward(slot_gate, slot_rows_t, *up_ring.arrived())
    slot_cots = cot_exchange.together(seat)
    slot_grads = (slot_gate * slot_cots.astype(jnp.float32)).astype(jnp.bfloat16)
    context_mine, context_other = core_columns(after(context, *up_ring.sent))
    up_ring.step(slot_gate, slot_rows_t, context_mine, context_other)
    down_ring.step(*up_ring.arrived())
    up_full = up_ring.finish(*down_ring.sent, slot_grads)
    down_ring.step(up_full, slot_grads)
    (up_full,) = tie((up_full,), down_ring.sent)
    hidden, lift_slope, down_parts = up_forward(slot_rows, up_full, act, slope, slot_grads)
    hidden, lift_slope = tie((hidden, lift_slope), down_ring.arrived())
    down_ring.step(hidden)
    down_sum = RingSum(down_parts.reshape(dp_count, -1, D), seat)
    down_sum.step(*down_ring.sent)
    down_full = down_ring.finish(*down_sum.sent)

    expert_rows = matmul(hidden, down_full).astype(jnp.bfloat16)
    expert_blocks = tie(parts_of(expert_rows), down_sum.arrived())
    returned = Exchange(*expert_blocks)
    down_sum.step(expert_rows)
    (back_grads,) = tie((slot_grads,), down_sum.sent)
    hidden_grads = hidden_back(back_grads, down_full, lift_slope, act, slot_rows_t)
    (hidden_grads,) = tie(
        (hidden_grads,),
        (*down_sum.arrived(), returned.near, *(returned.arrived() if owner_count > 4 else (returned.far,))),
    )
    returned.forward(hidden_grads)
    gate_up_sum = RingSum(hidden_grads, seat, 2)
    gate_up_sum.step(hidden_grads)
    down_sum.step(*gate_up_sum.sent, *returned.arrived())
    (hidden_now,) = tie((hidden_grads,), (*down_sum.sent, *gate_up_sum.sent))
    splits = (block_rows, block_rows, slot_room - 2 * block_rows)
    grad_rows = rows_back(hidden_now, gate_full, up_full, splits)
    returned_grads = Exchange(*grad_rows)
    gate_up_sum.step(*grad_rows)

    returned = returned.together(seat, *gate_up_sum.sent, *down_sum.arrived())
    pair_values = [matmul(picks, returned) for picks in from_slot]
    block_out = (
        mid_rows + pair_values[0] * gate_vals[:, 0:1] + pair_values[1] * gate_vals[:, 1:2]
    ).astype(jnp.bfloat16)
    grad_final = cotangent.astype(jnp.float32)
    grad_gates = (
        jnp.stack([jnp.sum(grad_final * values, -1) for values in pair_values], 1) * kept_pair
    )
    grad_router = jnp.sum(chosen * grad_gates[:, :, None], 1)
    grad_logits = (
        router * (grad_router - jnp.sum(router * grad_router, -1, keepdims=True))
    ).astype(jnp.bfloat16)
    returned_grads.forward(grad_logits, *gate_up_sum.arrived())
    down_sum.step(grad_logits, *gate_up_sum.arrived())
    gate_up_sum.step(*down_sum.sent)
    returned_grads = returned_grads.together(seat, *gate_up_sum.sent)
    grad_normed_two = matmul(grad_logits, w_router.T) + matmul(
        from_slot[0] + from_slot[1], returned_grads
    )
    grad_mid_norm, gain_two_local = norm_backward(grad_normed_two, mid_rows, inv_two, gain_two)
    grad_mid = grad_final + grad_mid_norm

    grad_branch = grad_mid.astype(jnp.bfloat16)
    grad_context = dot_dims(grad_branch, full_out, 1, 1).astype(jnp.bfloat16)

    def half_product(columns, grads):
        product = dot_dims(columns, grads, 0, 0).astype(jnp.bfloat16)
        return product.reshape(dp_count, half_rows, -1)

    out_other = half_product(context_other, grad_branch)
    out_mine = half_product(context_mine, grad_branch)
    (grad_context,) = tie((grad_context,), (out_mine, out_other))
    out_other = swap(out_other, 1)
    grad_query, grad_key, grad_value, near, away = attend_backward(
        qkv, grad_context, lse, seq_bucket, far, bias
    )
    grad_query, grad_key, grad_value, near, away = tie(
        (grad_query, grad_key, grad_value, near, away), (*down_sum.arrived(), out_other)
    )
    qkv_grads = jnp.concatenate([grad_query, grad_key, grad_value], 1)
    qkv_other = half_product(normed_other, qkv_grads)
    qkv_mine = half_product(after(normed_mine, qkv_other), qkv_grads)
    gate_up_sum.step(qkv_other, qkv_mine)
    qkv_other = swap(after(qkv_other, *gate_up_sum.sent), 1)
    down_share = down_sum.finish(*gate_up_sum.sent, joined=True)
    down_blocks = Spread(after(down_share, *gate_up_sum.sent))
    qkv_mine, out_mine = tie((qkv_mine, out_mine), gate_up_sum.sent)
    weight_parts = jnp.concatenate(
        [
            (mine.astype(jnp.float32) + other.astype(jnp.float32)).astype(jnp.bfloat16)
            for mine, other in ((qkv_mine, qkv_other), (out_mine, out_other))
        ],
        2,
    )
    weight_sum = RingSum(weight_parts, seat)
    near, away = tie((near, away), gate_up_sum.sent)
    table_local = table_sums(near, away)
    weight_sum.step(weight_parts, table_local, *down_blocks.arrived())
    (late_grads,) = tie((qkv_grads,), weight_sum.sent)
    grad_normed = dot_dims(late_grads, full_qkv, 1, 1)
    grad_row_one, gain_one_local = norm_backward(grad_normed, row_one, inv_one, gain_one)
    input_grad = grad_mid + grad_row_one
    down_blocks.hop(*weight_sum.sent)

    gate_up_share = gate_up_sum.finish(input_grad)
    gate_blocks, up_blocks = Spread(gate_up_share[0]), Spread(gate_up_share[1])
    weight_sum.step(gate_up_share, *down_blocks.arrived())
    (late_rows,) = tie((normed_two,), weight_sum.sent)
    small = SumAll((gain_one_local, table_local, gain_two_local, matmul(late_rows.T, grad_logits)))
    weight_sum.step(small.hop(*weight_sum.sent), *gate_blocks.arrived())
    Spread.hop_own(gate_blocks, up_blocks, gate_up_share, *weight_sum.sent)
    weight_sum.step(small.hop(*weight_sum.sent), *up_blocks.arrived(), *up_blocks.own_last)
    gate_blocks.hop(*weight_sum.sent)
    up_blocks.hop(*weight_sum.sent)
    down_out = down_blocks.outputs(device, *weight_sum.sent)
    rounded = weight_sum.finish(
        down_out, small.hop(*weight_sum.sent), *gate_blocks.arrived(), *up_blocks.arrived()
    )
    gate_out = gate_blocks.outputs(device, rounded, small.hop(rounded))
    up_out = up_blocks.outputs(device, gate_out)
    bit = owner_count // 2
    while bit > 1:
        arriving = after(swap(rounded, bit), gate_out, up_out)
        share = rounded.astype(jnp.float32) + arriving.astype(jnp.float32)
        rounded = share.astype(jnp.bfloat16)
        bit //= 2
    other = swap(rounded, 1)
    small.hop(rounded)
    gain_one_grad, table_grad, gain_two_grad, router_grad = small.finish()
    weight_grads = jnp.concatenate(
        [jnp.where(core == 0, rounded, other), jnp.where(core == 0, other, rounded)], 1
    ).astype(jnp.float32)
    query_grad, key_grad, value_grad, out_grad = (
        weight_grads[i // 2, :, i % 2 * D : (i % 2 + 1) * D] for i in range(4)
    )
    return (
        block_out,
        input_grad,
        gain_one_grad,
        query_grad,
        key_grad,
        value_grad,
        out_grad,
        table_grad,
        gain_two_grad,
        router_grad,
        gate_out,
        up_out,
        down_out,
    )


def solution(mesh):
    placed = (
        P(("dp", "expert"), None),
        P(("dp", "expert"), None),
        P(),
        P("dp", None),
        P("dp", None),
        P("dp", None),
        P("dp", None),
        P(),
        P(),
        P(),
        P(None, "dp", None),
        P(None, "dp", None),
        P(None, "dp", None),
        P(("dp", "expert"), None),
        P(("dp", "expert"), None),
        P(("dp", "expert"), None),
        P(("dp", "expert")),
    )
    return jax.shard_map(
        body,
        mesh=mesh,
        in_specs=placed,
        out_specs=(
            P(("dp", "expert"), None),
            P(("dp", "expert"), None),
            P(),
            P("dp", None),
            P("dp", None),
            P("dp", None),
            P("dp", None),
            P(),
            P(),
            P(),
            P(None, "dp", None),
            P(None, "dp", None),
            P(None, "dp", None),
        ),
        check_vma=False,
    )
```

```python
import math

import jax
import jax.numpy as jnp
import numpy as np
from jax import lax
from jax.experimental import pallas as pl
from jax.experimental.pallas import tpu as pltpu
from jax.sharding import PartitionSpec as P

D = 1024
H = 16
HEAD = 64
EXPERTS = 4
BUCKETS = 32
LONG = 512
SHORT = 128
PAIR = 2 * HEAD
TILES = LONG // SHORT
EPSILON = 1e-06
FF_TILE = 256
LAY_TILE = 512
MIB = 1024 * 1024
MASKED = -1e30


def bucket_of(offsets):
    distance = np.abs(offsets)
    half_count = BUCKETS // 2
    exact_count = half_count // 2
    widened = np.maximum(distance, 1)
    far_bucket = exact_count + np.floor(
        np.log(widened / exact_count) / np.log(128.0 / exact_count) * (half_count - exact_count)
    ).astype(np.int32)
    far_bucket = np.minimum(far_bucket, half_count - 1)
    inside = np.where(distance < exact_count, distance, far_bucket)
    return (np.where(offsets > 0, half_count, 0) + inside).astype(np.int32)


def near_buckets():
    places = np.arange(SHORT)
    inside = places[:, None] - places[None, :]
    return np.stack([bucket_of(SHORT * step + inside) for step in (-1, 0, 1)]).reshape(-1)


def near_onehot():
    buckets = jnp.asarray(near_buckets().astype(np.int8)).astype(jnp.int32)
    return (jnp.arange(BUCKETS, dtype=jnp.int32)[:, None] == buckets[None, :]).astype(jnp.float32)


FAR_BEFORE = BUCKETS // 2 - 1
FAR_AFTER = BUCKETS - 1


def ring_order(count):
    cols = 4 if count >= 16 else 2
    rows = count // cols
    cycle = [(0, col) for col in range(cols)]
    for row in range(1, rows):
        span = range(cols - 1, 0, -1) if row % 2 else range(1, cols)
        cycle += [(row, col) for col in span]
    cycle += [(row, 0) for row in range(rows - 1, 0, -1)]
    return [row * cols + col for row, col in cycle]


def ring_tables(count):
    ring = ring_order(count)
    ahead = [(ring[i], ring[(i + 1) % count]) for i in range(count)]
    behind = [(there, here) for here, there in ahead]
    place = {index: i for i, index in enumerate(ring)}
    seats = np.asarray(
        [[ring[(place[g] + d) % count] for d in range(count)] for g in range(count)], np.int32
    )
    return ahead, behind, seats


def after(value, *others):
    return lax.optimization_barrier((value, *others))[0]


def matmul(left, right):
    return jnp.dot(left, right, preferred_element_type=jnp.float32)


def dot_dims(left, right, left_dim, right_dim):
    return lax.dot_general(
        left, right, (((left_dim,), (right_dim,)), ((), ())), preferred_element_type=jnp.float32
    )


def tie(values, others):
    values = tuple(values)
    return lax.optimization_barrier(values + tuple(others))[: len(values)]


def pick(array, index, axis=0):
    return lax.dynamic_index_in_dim(array, index, axis, keepdims=False, allow_negative_indices=False)


def lay_kernel(places, spots_ref, *refs):
    *piece_refs, out_ref = refs
    for piece_ref, place in zip(piece_refs, places):
        index = place(spots_ref)
        out_ref[index] = piece_ref[: index[-1].size]


def lay_together(spots, pieces, shape, places, tile, start=0):
    lead = (0,) * (len(shape) - 1)
    first = start // tile
    return pl.pallas_call(
        lambda *refs: lay_kernel(places, *refs),
        grid_spec=pltpu.PrefetchScalarGridSpec(
            num_scalar_prefetch=1,
            grid=(shape[-1] // tile,),
            in_specs=[
                pl.BlockSpec((piece.shape[0], tile), lambda i, spots: (0, i + first))
                for piece in pieces
            ],
            out_specs=pl.BlockSpec((*shape[:-1], tile), lambda i, spots: (*lead, i)),
        ),
        out_shape=jax.ShapeDtypeStruct(shape, jnp.bfloat16),
        compiler_params=pltpu.CompilerParams(vmem_limit_bytes=16 * MIB),
        cost_estimate=pl.CostEstimate(
            flops=0, bytes_accessed=4 * math.prod(shape), transcendentals=0
        ),
    )(spots, *pieces)


class RingGather:
    def __init__(self, block, seat):
        self.count = lax.axis_size("dp")
        self.ahead, self.behind, _ = ring_tables(self.count)
        self.seat, self.rows, self.taken = seat, block.shape[0], 0
        self.low = self.high = block
        self.mid = min((self.rows // 2 + 15) // 16 * 16, self.rows)
        self.pieces = [(block, 0, 0)]

    def arrived(self):
        return (self.low, self.high)

    def step(self, *others):
        half = self.count // 2
        if self.taken >= half:
            return
        if self.taken == 0:
            self.sent = (low,) = tie((self.low,), others)
            high = low
        else:
            self.sent = low, high = tie((self.low, self.high), others)
        self.taken += 1
        last = self.taken == half
        low, high = (low[: self.mid], high[self.mid :]) if last else (low, high)
        self.low = lax.ppermute(low, "dp", self.ahead)
        self.high = lax.ppermute(high, "dp", self.behind)
        self.pieces += [
            (self.low, (half if last else -self.taken) % self.count, 0),
            (self.high, self.taken, self.mid if last else 0),
        ]

    def finish(self, *others):
        while self.taken < self.count // 2:
            self.step()
        columns = self.pieces[0][0].shape[1]
        places = []
        for piece, step, start in self.pieces:

            def place(spots, step=step, start=start, rows=piece.shape[0]):
                return (spots[step], pl.ds(start, rows))

            places.append(place)
        out = lay_together(
            after(self.seat, *others),
            [piece for piece, _, _ in self.pieces],
            (self.count, self.rows, columns),
            places,
            columns // 2,
        )
        return out.reshape(-1, columns)


def ring_sum_kernel(received, outs, *refs):
    own_refs, received_refs = refs[:outs], refs[outs:-outs]
    side = pl.program_id(0)
    for out in range(outs):
        total = own_refs[out][...].astype(jnp.float32)
        for received_ref, (target, only) in zip(received_refs, received):
            if target == out:
                more = received_ref[...].astype(jnp.float32)
                total = total + (more if only is None else jnp.where(side == only, more, 0.0))
        refs[out - outs][...] = total.astype(jnp.bfloat16)


class RingSum:
    def __init__(self, parts, seat, entry=None):
        self.count = lax.axis_size("dp")
        self.ahead, self.behind, _ = ring_tables(self.count)
        self.seat, self.parts, self.entry, self.taken = seat, parts, entry, 0
        if entry is None:
            self.shape = (parts.shape[1], parts.shape[2] // 2)
        else:
            self.shape = (D // self.count, parts.shape[2])
        self.low = self.high = None

    def own(self, step, side=0):
        step = step % self.count
        if self.entry is None:
            return self.parts, pl.BlockSpec(
                (None, *self.shape), lambda i, seat: (seat[step], 0, i + side)
            )
        first = self.entry + side
        return self.parts, pl.BlockSpec(
            (None, *self.shape), lambda i, seat: (first + i, seat[step], 0)
        )

    def call(self, own, received, operands, others=(), halves=2, joined=False):
        moved = 2 * halves * math.prod(self.shape)

        def block(item):
            if item.shape[0] == 1:
                return pl.BlockSpec((None, *self.shape), lambda i, seat: (0, 0, 0))
            return pl.BlockSpec((None, *self.shape), lambda i, seat: (i, 0, 0))

        if joined:
            out_spec = pl.BlockSpec(self.shape, lambda i, seat: (0, i))
            out_shape = (self.shape[0], halves * self.shape[1])
        else:
            out_spec = pl.BlockSpec((None, *self.shape), lambda i, seat: (i, 0, 0))
            out_shape = (halves, *self.shape)
        return pl.pallas_call(
            lambda seat_ref, *refs: ring_sum_kernel(received, len(own), *refs),
            grid_spec=pltpu.PrefetchScalarGridSpec(
                num_scalar_prefetch=1,
                grid=(halves,),
                in_specs=[spec for _, spec in own] + [block(item) for item in operands],
                out_specs=[out_spec] * len(own),
            ),
            out_shape=[jax.ShapeDtypeStruct(out_shape, jnp.bfloat16)] * len(own),
            compiler_params=pltpu.CompilerParams(
                vmem_limit_bytes=(16 if self.entry is None else 40) * MIB
            ),
            cost_estimate=pl.CostEstimate(
                flops=2 * moved,
                bytes_accessed=moved * (len(operands) + 2 * len(own)),
                transcendentals=0,
            ),
        )(after(self.seat, *others), *(part for part, _ in own), *operands)

    def arrived(self):
        return (self.low, self.high)

    def received(self, targets):
        single = self.taken == 1
        return [(targets[0], 0 if single else None), (targets[1], 1 if single else None)]

    def step(self, *others):
        half = self.count // 2
        if self.taken >= half:
            return
        distance = half - self.taken
        if self.taken:
            received, operands = self.received((0, 1)), tie(self.arrived(), others)
            sent = self.call(self.following, received, operands)
        else:
            own = (self.own(distance), self.own(-distance, 1))
            sent = self.call(own, [], (), others, 1)
        self.low = lax.ppermute(sent[0], "dp", self.ahead)
        self.high = lax.ppermute(sent[1], "dp", self.behind)
        self.taken += 1
        distance -= 1
        steps = (distance, -distance) if distance else (0,)
        self.following = [self.own(step) for step in steps]
        self.sent = tuple(sent)

    def finish(self, *others, joined=False):
        while self.taken < self.count // 2:
            self.step()
        received, operands = self.received((0, 0)), tie(self.arrived(), others)
        return self.call(self.following, received, operands, joined=joined)[0]


def swap(value, bit):
    count = lax.axis_size("expert")
    return lax.ppermute(value, "expert", [(i, i ^ bit) for i in range(count)])


class Exchange:
    def __init__(self, own, near, far):
        self.own, self.count, self.rows = own, lax.axis_size("expert"), own.shape[0]
        self.near, self.last = swap(near, 1), None
        if self.count == 4:
            self.far = swap(far, 2)
        else:
            blocks = far.reshape(-1, self.rows, far.shape[1])
            self.far = [swap(block, bit + 2) for bit, block in enumerate(blocks)]

    def forward(self, *others):
        if self.count == 4:
            self.last = swap(after(self.far, *others)[self.rows :], 1)
        return self

    def arrived(self):
        return (self.near, self.last) if self.count == 4 else tuple(self.far)

    def together(self, seat, *others):
        if self.count == 4:
            pieces = [self.own, self.near, self.far, self.last]
        else:
            pieces = [self.own, self.near, *self.far]
        places = [
            lambda spots, d=d: (pl.ds(d * self.rows, self.rows),) for d in range(len(pieces))
        ]
        shape = (self.count * self.rows, self.own.shape[1])
        return lay_together(after(seat, *others), pieces, shape, places, LAY_TILE)


class Spread:
    def __init__(self, value):
        self.bit = lax.axis_size("expert") // 2
        self.held = {0: (value, None)}
        self.hop()

    @classmethod
    def hop_own(cls, first, second, both, *others):
        swapped = swap(after(both, *others), 1)
        for lead, spread in enumerate((first, second)):
            spread.held[0] = (both, lead)
            spread.held[1] = (swapped, lead)
            spread.own_last = (swapped,)

    def hop(self, *others):
        if not self.bit:
            return
        keys = [key for key in self.held if key ^ self.bit not in self.held]
        items = [self.held[key] for key in keys]
        items = tie((item if lead is None else item[lead] for item, lead in items), others)
        fresh = {key ^ self.bit: swap(item, self.bit) for key, item in zip(keys, items)}
        self.last = tuple(fresh.values())
        self.held.update({key: (item, None) for key, item in fresh.items()})
        self.bit //= 2

    def arrived(self):
        return self.last

    def outputs(self, device, *others):
        while self.bit:
            self.hop()
        keys = sorted(self.held)
        shares = len(keys) // EXPERTS
        rows, columns = self.held[0][0].shape[-2:]
        tile = columns // 2

        def spec(lead):
            if lead is None:
                return pl.BlockSpec((rows, tile), lambda i, spots: (0, i))
            return pl.BlockSpec((None, rows, tile), lambda i, spots: (lead, 0, i))

        def kernel(spots_ref, *refs):
            *block_refs, out_ref = refs
            for first in range(0, len(keys), shares):
                total = block_refs[first][...].astype(jnp.float32)
                for block_ref in block_refs[first + 1 : first + shares]:
                    total = total + block_ref[...].astype(jnp.float32)
                out_ref[spots_ref[first]] = total

        spots = jnp.stack([device ^ key if shares == 1 else lax.div(device ^ key, shares) for key in keys])
        return pl.pallas_call(
            kernel,
            grid_spec=pltpu.PrefetchScalarGridSpec(
                num_scalar_prefetch=1,
                grid=(2,),
                in_specs=[spec(self.held[key][1]) for key in keys],
                out_specs=pl.BlockSpec((EXPERTS, rows, tile), lambda i, spots: (0, 0, i)),
            ),
            out_shape=jax.ShapeDtypeStruct((EXPERTS, rows, columns), jnp.float32),
            compiler_params=pltpu.CompilerParams(vmem_limit_bytes=24 * MIB),
            cost_estimate=pl.CostEstimate(
                flops=0, bytes_accessed=6 * EXPERTS * rows * columns, transcendentals=0
            ),
        )(after(spots, *others), *(self.held[key][0] for key in keys))


class SumAll:
    def __init__(self, parts):
        self.shapes = [part.shape for part in parts]
        self.flat = jnp.concatenate([part.reshape(-1, 128) for part in parts], 0)
        self.hops = []
        for axis in ("expert", "dp"):
            bit, count = 1, lax.axis_size(axis)
            while bit < count:
                self.hops.append((axis, [(i, i ^ bit) for i in range(count)]))
                bit *= 2
        over_x = self.hops.pop(1)
        self.hops.append(over_x)

    def hop(self, *others):
        if not self.hops:
            return self.flat
        axis, pairs = self.hops.pop(0)
        flat = after(self.flat, *others)
        self.flat = flat + lax.ppermute(flat, axis, pairs)
        return self.flat

    def finish(self, *others):
        while self.hops:
            self.hop(*others)
        sums, start = [], 0
        for shape in self.shapes:
            rows = math.prod(shape) // 128
            sums.append(self.flat[start : start + rows].reshape(shape))
            start += rows
        return sums


def norm_backward(grad_rows, row_data, inverse, gain_vec):
    scaled = grad_rows * gain_vec
    inner_mean = jnp.mean(scaled * row_data, -1, keepdims=True)
    grad_input = inverse * scaled - row_data * inverse * inverse * inverse * inner_mean
    return (grad_input, jnp.sum(grad_rows * row_data * inverse, 0))


def other_head_zeroed(rows_t, head):
    own = rows_t[head * HEAD : (head + 1) * HEAD]
    rest = jnp.zeros_like(own)
    return jnp.concatenate([own, rest] if head == 0 else [rest, own], 0)


def tile_biases(bias_ref, far_ref, pair, head, penalty):
    near = {
        -1: bias_ref[head, 0] + penalty,
        0: bias_ref[head, 1],
        1: bias_ref[head, 2] + penalty,
    }
    before = far_ref[0, 2 * pair + head] + penalty
    later = far_ref[1, 2 * pair + head] + penalty
    return lambda step: near[step] if abs(step) < 2 else (before if step < 0 else later)


def transposed(rows):
    return rows.astype(jnp.float32).T


def attend_forward_kernel(
    flag_ref, far_ref, q_ref, k_ref, v_ref, bias_ref, ctx_ref, lse_ref
):
    block, pair = pl.program_id(0), pl.program_id(1)
    penalty = jnp.where(flag_ref[block] == 0, 0.0, MASKED).astype(jnp.float32)
    query_t = (transposed(q_ref[...]) * (1.0 / math.sqrt(HEAD))).astype(jnp.bfloat16)
    value_t = transposed(v_ref[...]).astype(jnp.bfloat16)
    key_rows = k_ref[...]
    parts = []
    for head in range(2):
        bias = tile_biases(bias_ref, far_ref, pair, head, penalty)
        scores = dot_dims(key_rows, other_head_zeroed(query_t, head), 1, 0)
        value_head = value_t[head * HEAD : (head + 1) * HEAD]
        pieces = []
        for col in range(TILES):
            cols = slice(col * SHORT, (col + 1) * SHORT)
            panel = jnp.concatenate(
                [
                    scores[row * SHORT : (row + 1) * SHORT, cols] + bias(row - col)
                    for row in range(TILES)
                ],
                0,
            )
            highest = jnp.max(panel, 0, keepdims=True)
            raised = jnp.exp(panel - highest)
            total = jnp.sum(raised, 0, keepdims=True)
            piece = matmul(value_head, raised.astype(jnp.bfloat16))
            pieces.append(piece / total)
            lse_ref[0, 0, head : head + 1, cols] = highest + jnp.log(total)
        parts.append(pieces)
    for col in range(TILES):
        joined = jnp.concatenate([parts[0][col], parts[1][col]], 0)
        ctx_ref[col * SHORT : (col + 1) * SHORT, :] = joined.T.astype(jnp.bfloat16)


def attend_forward(qkv, flags, far, bias):
    tok_count = qkv.shape[0]
    blocks = tok_count // LONG
    pairs = H // 2

    def column(first):
        return pl.BlockSpec((LONG, PAIR), lambda b, p, flag: (b, first + p))

    return pl.pallas_call(
        attend_forward_kernel,
        grid_spec=pltpu.PrefetchScalarGridSpec(
            num_scalar_prefetch=1,
            grid=(blocks, pairs),
            in_specs=[
                pl.BlockSpec(memory_space=pltpu.SMEM),
                column(0),
                column(pairs),
                column(2 * pairs),
                pl.BlockSpec((2, 3, SHORT, SHORT), lambda b, p, flag: (p, 0, 0, 0)),
            ],
            out_specs=[
                column(0),
                pl.BlockSpec((1, 1, 2, LONG), lambda b, p, flag: (b, p, 0, 0)),
            ],
        ),
        out_shape=[
            jax.ShapeDtypeStruct((tok_count, D), jnp.bfloat16),
            jax.ShapeDtypeStruct((blocks, pairs, 2, LONG), jnp.float32),
        ],
        compiler_params=pltpu.CompilerParams(vmem_limit_bytes=16 * MIB),
        cost_estimate=pl.CostEstimate(
            flops=8 * H * LONG * LONG * HEAD * blocks,
            bytes_accessed=8 * tok_count * D + 12 * H * SHORT * SHORT,
            transcendentals=H * LONG * LONG * blocks,
        ),
    )(flags, far, qkv, qkv, qkv, bias)


def attend_backward_kernel(
    flag_ref,
    far_ref,
    q_ref,
    k_ref,
    v_ref,
    grad_ref,
    lse_ref,
    bias_ref,
    dq_ref,
    dk_ref,
    dv_ref,
    near_ref,
    away_ref,
    weight_scr,
    score_scr,
):
    pair, block = pl.program_id(0), pl.program_id(1)
    penalty = jnp.where(flag_ref[block] == 0, 0.0, MASKED).astype(jnp.float32)
    scaled = (q_ref[...].astype(jnp.float32) * (1.0 / math.sqrt(HEAD))).astype(jnp.bfloat16)
    query_t = transposed(scaled).astype(jnp.bfloat16)
    grad_t = transposed(grad_ref[...]).astype(jnp.bfloat16)
    key_t = transposed(k_ref[...]).astype(jnp.bfloat16)
    key_rows, value_rows, grad_rows = k_ref[...], v_ref[...], grad_ref[...]

    @pl.when(block == 0)
    def _():
        near_ref[...] = jnp.zeros_like(near_ref)
        away_ref[...] = jnp.zeros_like(away_ref)

    query_parts, key_parts, value_parts = [], [], []
    for head in range(2):
        bias = tile_biases(bias_ref, far_ref, pair, head, penalty)
        scores = dot_dims(key_rows, other_head_zeroed(query_t, head), 1, 0)
        grad_probs = dot_dims(value_rows, other_head_zeroed(grad_t, head), 1, 0)
        key_head = key_t[head * HEAD : (head + 1) * HEAD]
        near = {-1: None, 0: None, 1: None}
        away = [None, None]
        for col in range(TILES):
            cols = slice(col * SHORT, (col + 1) * SHORT)
            total = lse_ref[0, 0, head : head + 1, cols]
            probs = jnp.exp(
                jnp.concatenate(
                    [
                        scores[row * SHORT : (row + 1) * SHORT, cols] + bias(row - col)
                        for row in range(TILES)
                    ],
                    0,
                )
                - total
            )
            panel = grad_probs[:, cols]
            inner = jnp.sum(probs * panel, 0, keepdims=True)
            grad_scores = (probs * (panel - inner)).astype(jnp.bfloat16)
            weight_scr[:, cols] = probs.astype(jnp.bfloat16)
            score_scr[:, cols] = grad_scores
            rounded = grad_scores.astype(jnp.float32)
            for row in range(TILES):
                tile = rounded[row * SHORT : (row + 1) * SHORT]
                step = row - col
                if abs(step) < 2:
                    near[step] = tile if near[step] is None else near[step] + tile
                else:
                    side = 0 if step < 0 else 1
                    tile = jnp.sum(tile, 0, keepdims=True)
                    away[side] = tile if away[side] is None else away[side] + tile
        for step in (-1, 0, 1):
            near_ref[head, step + 1] += near[step]
        for side in range(2):
            away_ref[0, head, side : side + 1, :] += away[side]
        query_parts.append(matmul(key_head, score_scr[...]))
        key_parts.append(matmul(score_scr[...], scaled))
        value_parts.append(matmul(weight_scr[...], grad_rows))
    lane = lax.broadcasted_iota(jnp.int32, (LONG, PAIR), 1)
    dk_ref[...] = jnp.where(lane < HEAD, key_parts[0], key_parts[1]).astype(jnp.bfloat16)
    dv_ref[...] = jnp.where(lane < HEAD, value_parts[0], value_parts[1]).astype(jnp.bfloat16)
    joined = jnp.concatenate(query_parts, 0) * (1.0 / math.sqrt(HEAD))
    dq_ref[...] = joined.T.astype(jnp.bfloat16)


def attend_backward(qkv, grad_context, lse, flags, far, bias):
    tok_count = qkv.shape[0]
    blocks = tok_count // LONG
    pairs = H // 2

    def column(first):
        return pl.BlockSpec((LONG, PAIR), lambda p, b, flag: (b, first + p))

    rows = jax.ShapeDtypeStruct((tok_count, D), jnp.bfloat16)
    return pl.pallas_call(
        attend_backward_kernel,
        grid_spec=pltpu.PrefetchScalarGridSpec(
            num_scalar_prefetch=1,
            grid=(pairs, blocks),
            in_specs=[
                pl.BlockSpec(memory_space=pltpu.SMEM),
                column(0),
                column(pairs),
                column(2 * pairs),
                column(0),
                pl.BlockSpec((1, 1, 2, LONG), lambda p, b, flag: (b, p, 0, 0)),
                pl.BlockSpec((2, 3, SHORT, SHORT), lambda p, b, flag: (p, 0, 0, 0)),
            ],
            out_specs=[
                column(0),
                column(0),
                column(0),
                pl.BlockSpec((2, 3, SHORT, SHORT), lambda p, b, flag: (p, 0, 0, 0)),
                pl.BlockSpec((1, 2, 2, SHORT), lambda p, b, flag: (p, 0, 0, 0)),
            ],
            scratch_shapes=[
                pltpu.VMEM((LONG, LONG), jnp.bfloat16),
                pltpu.VMEM((LONG, LONG), jnp.bfloat16),
            ],
        ),
        out_shape=[
            rows,
            rows,
            rows,
            jax.ShapeDtypeStruct((H, 3, SHORT, SHORT), jnp.float32),
            jax.ShapeDtypeStruct((pairs, 2, 2, SHORT), jnp.float32),
        ],
        compiler_params=pltpu.CompilerParams(vmem_limit_bytes=24 * MIB),
        cost_estimate=pl.CostEstimate(
            flops=20 * H * LONG * LONG * HEAD * blocks,
            bytes_accessed=16 * tok_count * D + 24 * H * SHORT * SHORT,
            transcendentals=H * LONG * LONG * blocks,
        ),
    )(flags, far, qkv, qkv, qkv, grad_context, lse, bias)


ROW_TILE = 256
GELU_SCALE = math.sqrt(2.0 / math.pi)
GELU_CUBE = 0.044715


def row_tiles(rows):
    return [slice(start, min(start + ROW_TILE, rows)) for start in range(0, rows, ROW_TILE)]


def gate_kernel(rows_ref, weight_ref, act_ref, slope_ref):
    for part in row_tiles(rows_ref.shape[0]):
        pre = matmul(rows_ref[part, :], weight_ref[...])
        square = pre * pre
        angle = jnp.tanh(pre * (GELU_SCALE + (GELU_SCALE * GELU_CUBE) * square))
        half = 0.5 + 0.5 * angle
        act_ref[part, :] = (pre * half).astype(jnp.bfloat16)
        bend = (0.5 * GELU_SCALE) + (1.5 * GELU_SCALE * GELU_CUBE) * square
        slope_ref[part, :] = (half + pre * (1.0 - angle * angle) * bend).astype(jnp.bfloat16)


def up_kernel(rows_ref, weight_ref, act_ref, slope_ref, grads_ref, hid_ref, lift_ref, down_ref):
    for part in row_tiles(rows_ref.shape[0]):
        lift = matmul(rows_ref[part, :], weight_ref[...])
        hid_ref[part, :] = (act_ref[part, :].astype(jnp.float32) * lift).astype(jnp.bfloat16)
        lift_ref[part, :] = (slope_ref[part, :].astype(jnp.float32) * lift).astype(jnp.bfloat16)
    down_ref[...] = dot_dims(hid_ref[...], grads_ref[...], 0, 0).astype(jnp.bfloat16)


def hidden_back_kernel(grads_ref, down_ref, lift_ref, act_ref, rows_t_ref, out_ref):
    for part in row_tiles(grads_ref.shape[0]):
        back = dot_dims(grads_ref[part, :], down_ref[...], 1, 1)
        out_ref[0, part, :] = (back * lift_ref[part, :].astype(jnp.float32)).astype(jnp.bfloat16)
        out_ref[1, part, :] = (back * act_ref[part, :].astype(jnp.float32)).astype(jnp.bfloat16)
    rows = rows_t_ref.shape[0]
    for part in row_tiles(rows):
        out_ref[2, part, :] = matmul(rows_t_ref[part, :], out_ref[0]).astype(jnp.bfloat16)
        out_ref[3, part, :] = matmul(rows_t_ref[part, :], out_ref[1]).astype(jnp.bfloat16)
    rest = jnp.zeros((2, out_ref.shape[1] - rows, out_ref.shape[2]), jnp.bfloat16)
    out_ref[2:, rows:, :] = rest


def rows_back_kernel(pre_ref, up_ref, gate_w_ref, up_w_ref, *out_refs):
    total = dot_dims(pre_ref[...], gate_w_ref[...], 1, 1) + dot_dims(up_ref[...], up_w_ref[...], 1, 1)
    start = 0
    for out_ref in out_refs:
        rows = out_ref.shape[0]
        out_ref[...] = total[start : start + rows].astype(jnp.bfloat16)
        start += rows


def kernel_call(kernel, operands, in_specs, out_specs, out_shape, steps, flops, vmem):
    moved = sum(2 * math.prod(item.shape) for item in (*operands, *out_shape))
    return pl.pallas_call(
        kernel,
        grid=(steps,),
        in_specs=in_specs,
        out_specs=out_specs,
        out_shape=[jax.ShapeDtypeStruct(item.shape, jnp.bfloat16) for item in out_shape],
        compiler_params=pltpu.CompilerParams(vmem_limit_bytes=vmem * MIB),
        cost_estimate=pl.CostEstimate(flops=flops, bytes_accessed=moved, transcendentals=0),
    )(*operands)


def width_tiles(width):
    return pl.cdiv(width, FF_TILE)


def whole_spec(shape, buffers=2):
    return pl.BlockSpec(shape, lambda i: (0, 0), pipeline_mode=pl.Buffered(buffers))


def gate_forward(rows, weight):
    count, width = rows.shape[0], weight.shape[1]
    tile = pl.BlockSpec((count, FF_TILE), lambda i: (0, i))
    shape = jax.ShapeDtypeStruct((count, width), jnp.bfloat16)
    return kernel_call(
        gate_kernel,
        (rows, weight),
        [whole_spec(rows.shape), pl.BlockSpec((D, FF_TILE), lambda i: (0, i))],
        [tile, tile],
        [shape, shape],
        width_tiles(width),
        2 * count * D * width,
        59,
    )


def up_forward(rows, weight, act, slope, grads):
    count, width = rows.shape[0], weight.shape[1]
    tile = pl.BlockSpec((count, FF_TILE), lambda i: (0, i))
    shape = jax.ShapeDtypeStruct((count, width), jnp.bfloat16)
    return kernel_call(
        up_kernel,
        (rows, weight, act, slope, grads),
        [
            whole_spec(rows.shape),
            pl.BlockSpec((D, FF_TILE), lambda i: (0, i)),
            tile,
            tile,
            whole_spec(grads.shape),
        ],
        [tile, tile, pl.BlockSpec((FF_TILE, D), lambda i: (i, 0))],
        [shape, shape, jax.ShapeDtypeStruct((width, D), jnp.bfloat16)],
        width_tiles(width),
        4 * count * D * width,
        59,
    )


def hidden_back(grads, weight, lift, act, rows_t):
    count, width = lift.shape
    tile = pl.BlockSpec((count, FF_TILE), lambda i: (0, i))
    return kernel_call(
        hidden_back_kernel,
        (grads, weight, lift, act, rows_t),
        [
            whole_spec(grads.shape),
            pl.BlockSpec((FF_TILE, D), lambda i: (i, 0)),
            tile,
            tile,
            whole_spec(rows_t.shape),
        ],
        [pl.BlockSpec((4, count, FF_TILE), lambda i: (0, 0, i))],
        [jax.ShapeDtypeStruct((4, count, width), jnp.bfloat16)],
        width_tiles(width),
        6 * count * D * width,
        59,
    )[0]


def rows_back(hidden_grads, gate_weight, up_weight, splits):
    _, count, width = hidden_grads.shape
    weight_tile = pl.BlockSpec((ROW_TILE, width), lambda i: (i, 0))

    def entry(number):
        return pl.BlockSpec(
            (None, count, width), lambda i: (number, 0, 0), pipeline_mode=pl.Buffered(1)
        )

    return kernel_call(
        rows_back_kernel,
        (hidden_grads, hidden_grads, gate_weight, up_weight),
        [entry(0), entry(1), weight_tile, weight_tile],
        [pl.BlockSpec((rows, ROW_TILE), lambda i: (0, i)) for rows in splits],
        [jax.ShapeDtypeStruct((rows, D), jnp.bfloat16) for rows in splits],
        D // ROW_TILE,
        4 * count * D * width,
        59,
    )


def table_sums(near, away):
    near_part = lax.dot_general(
        near_onehot(),
        near.reshape(H, -1),
        (((1,), (1,)), ((), ())),
        precision=lax.Precision.HIGHEST,
        preferred_element_type=jnp.float32,
    )
    far_part = jnp.sum(away, -1).reshape(H, 2)
    sides = np.zeros((BUCKETS, 2), np.float32)
    sides[FAR_BEFORE, 0] = sides[FAR_AFTER, 1] = 1.0
    return near_part + jnp.sum(sides[:, None, :] * far_part[None], -1)


def body(
    tokens,
    cotangent,
    gain_one,
    w_query,
    w_key,
    w_value,
    w_out,
    rel_table,
    gain_two,
    w_router,
    w_gate,
    w_up,
    w_down,
    expert_ids,
    slot_index,
    slot_kept,
    seq_bucket,
):
    tok_count = tokens.shape[0]
    dp_count = lax.axis_size("dp")
    owner_count = lax.axis_size("expert")
    shares = owner_count // EXPERTS
    group = lax.axis_index("dp")
    device = lax.axis_index("expert")
    expert = device if shares == 1 else lax.div(device, shares)
    core = device & 1
    seat = pick(jnp.asarray(ring_tables(dp_count)[2]), group)

    half_rows = w_query.shape[0] // 2

    def own_half(weight):
        return lax.dynamic_slice_in_dim(
            weight, core * half_rows, half_rows, 0, allow_negative_indices=False
        )

    slot_quota = 5 * tok_count // (2 * EXPERTS * owner_count)
    slot_span = owner_count * slot_quota
    owners_each = owner_count // shares
    block_rows = owners_each * slot_quota
    slot_room = owner_count * block_rows

    def routes(ids, slots, kept):
        owner = slots // slot_span
        dest = ids * shares + owner // owners_each
        local_slot = (
            (dest ^ device) * block_rows
            + (owner % owners_each) * slot_quota
            + slots % slot_span
            - device * slot_quota
        )
        target = jnp.where(kept == 1, local_slot, slot_room)
        room = jnp.arange(slot_room, dtype=jnp.int32)
        from_slot = [
            (target[:, k : k + 1] == room[None, :]).astype(jnp.bfloat16) for k in range(2)
        ]
        to_slot = jnp.logical_or(
            target[:, 0][None, :] == room[:, None], target[:, 1][None, :] == room[:, None]
        ).astype(jnp.bfloat16)
        return from_slot, to_slot

    def parts_of(rows):
        return rows[:block_rows], rows[block_rows : 2 * block_rows], rows[2 * block_rows :]

    def outgoing(rows, to_slot):
        return [matmul(part, rows).astype(jnp.bfloat16) for part in reversed(parts_of(to_slot))][::-1]

    def route(rows):
        logits = matmul(rows, w_router)
        raised = jnp.exp(logits - jnp.max(logits, -1, keepdims=True))
        return raised / jnp.sum(raised, -1, keepdims=True)

    weight_ring = RingGather(
        jnp.concatenate([own_half(weight) for weight in (w_query, w_key, w_value, w_out)], 1), seat
    )
    weight_ring.step()
    row_one = tokens.astype(jnp.float32)
    inv_one = lax.rsqrt(jnp.mean(row_one * row_one, -1, keepdims=True) + EPSILON)
    normed = (row_one * inv_one * gain_one).astype(jnp.bfloat16)
    theirs = [swap(weight_ring.pieces[0][0], 1)]

    def weight_step(*others):
        if weight_ring.taken < dp_count // 2:
            weight_ring.step(*others)
            theirs.extend(swap(piece, 1) for piece in weight_ring.sent)

    weight_step(inv_one)
    ids, slots, kept = tie((expert_ids, slot_index, slot_kept), weight_ring.sent)
    from_slot, to_slot = routes(ids, slots, kept)
    def core_columns(rows):
        split = rows.reshape(tok_count, dp_count, 2, half_rows)
        return [pick(split, side, 2).reshape(tok_count, -1) for side in (core, 1 - core)]

    normed_mine, normed_other = core_columns(normed)
    weight_step(to_slot, theirs[0], normed_mine, normed_other)
    cots, table = tie((cotangent, rel_table), weight_ring.sent)
    cot_blocks = outgoing(cots, to_slot)
    bias = lax.dot_general(
        after(table, *cot_blocks),
        near_onehot(),
        (((0,), (0,)), ((), ())),
        precision=lax.Precision.HIGHEST,
        preferred_element_type=jnp.float32,
    ).reshape(H, 3, SHORT, SHORT)
    far = jnp.stack([rel_table[FAR_BEFORE], rel_table[FAR_AFTER]])
    weight_step(bias, *theirs[1:3])
    while weight_ring.taken < dp_count // 2:
        weight_step()
    gate_ring = RingGather(pick(w_gate, expert), seat)
    gate_ring.step(*weight_ring.sent)
    theirs.extend(swap(piece, 1) for piece in weight_ring.arrived())
    places = []
    for side in range(2):
        for piece, step, start in weight_ring.pieces:

            def place(spots, step=step, side=side, start=start, rows=piece.shape[0]):
                return (spots[step], spots[dp_count + side], pl.ds(start, rows))

            places.append(place)
    spots = jnp.concatenate([seat, jnp.stack([core, 1 - core])])
    pieces = [piece for piece, _, _ in weight_ring.pieces] + theirs
    full_qkv = lay_together(spots, pieces, (dp_count, 2, half_rows, 3 * D), places, LAY_TILE)
    full_out = lay_together(spots, pieces, (dp_count, 2, half_rows, D), places, LAY_TILE, 3 * D)
    full_qkv, full_out = full_qkv.reshape(D, 3 * D), full_out.reshape(D, D)
    up_own, down_own = tie((pick(w_up, expert), pick(w_down, expert)), (full_qkv,))
    up_ring = RingGather(up_own, seat)
    down_ring = RingGather(down_own, seat)

    gate_ring.step(full_qkv, up_own, down_own)
    (normed_now,) = tie((normed,), gate_ring.sent)
    qkv = matmul(normed_now, full_qkv).astype(jnp.bfloat16)
    context, lse = attend_forward(qkv, seq_bucket, far, bias)
    (context,) = tie((context,), gate_ring.arrived())
    gate_ring.step(context)
    (context,) = tie((context,), gate_ring.sent)
    mid_rows = row_one + matmul(context, full_out)
    inv_two = lax.rsqrt(jnp.mean(mid_rows * mid_rows, -1, keepdims=True) + EPSILON)
    normed_two = (mid_rows * inv_two * gain_two).astype(jnp.bfloat16)
    row_blocks = outgoing(normed_two, to_slot)
    row_exchange = Exchange(*row_blocks)
    gate_ring.step(*row_blocks)
    up_ring.step(*gate_ring.sent)
    gate_full = gate_ring.finish(*up_ring.sent)
    router = route(after(normed_two, gate_full))
    chosen = (ids[:, :, None] == jnp.arange(EXPERTS, dtype=jnp.int32)).astype(jnp.float32)
    kept_pair = kept.astype(jnp.float32)
    gate_vals = jnp.sum(chosen * router[:, None, :], -1) * kept_pair
    up_ring.step(gate_vals)

    slot_rows = row_exchange.forward(*up_ring.sent).together(seat)
    cot_exchange = Exchange(*tie(cot_blocks, (slot_rows,)))
    down_ring.step(slot_rows)
    (gate_now,) = tie((gate_full,), (*down_ring.sent, cot_exchange.near))
    act, slope = gate_forward(slot_rows, gate_now)
    act, slope = tie((act, slope), up_ring.arrived())
    up_ring.step(act)
    (rows_now,) = tie((slot_rows,), up_ring.sent)
    slot_gate = lax.dynamic_index_in_dim(
        route(rows_now), expert, 1, allow_negative_indices=False
    )
    slot_rows_t = rows_now.T
    cot_exchange.forward(slot_gate, slot_rows_t, *up_ring.arrived())
    slot_cots = cot_exchange.together(seat)
    slot_grads = (slot_gate * slot_cots.astype(jnp.float32)).astype(jnp.bfloat16)
    up_ring.step(slot_gate, slot_rows_t)
    down_ring.step(*up_ring.arrived())
    up_full = up_ring.finish(*down_ring.sent, slot_grads)
    down_ring.step(up_full, slot_grads)
    (up_full,) = tie((up_full,), down_ring.sent)
    hidden, lift_slope, down_parts = up_forward(slot_rows, up_full, act, slope, slot_grads)
    hidden, lift_slope = tie((hidden, lift_slope), down_ring.arrived())
    down_ring.step(hidden)
    down_sum = RingSum(down_parts.reshape(dp_count, -1, D), seat)
    down_sum.step(*down_ring.sent)
    down_full = down_ring.finish(*down_sum.sent)

    expert_rows = matmul(hidden, down_full).astype(jnp.bfloat16)
    expert_blocks = tie(parts_of(expert_rows), down_sum.arrived())
    returned = Exchange(*expert_blocks)
    down_sum.step(expert_rows)
    (back_grads,) = tie((slot_grads,), down_sum.sent)
    hidden_grads = hidden_back(back_grads, down_full, lift_slope, act, slot_rows_t)
    (hidden_grads,) = tie(
        (hidden_grads,),
        (*down_sum.arrived(), returned.near, *(returned.arrived() if owner_count > 4 else (returned.far,))),
    )
    returned.forward(hidden_grads)
    gate_up_sum = RingSum(hidden_grads, seat, 2)
    gate_up_sum.step(hidden_grads)
    down_sum.step(*gate_up_sum.sent, *returned.arrived())
    (hidden_now,) = tie((hidden_grads,), (*down_sum.sent, *gate_up_sum.sent))
    splits = (block_rows, block_rows, slot_room - 2 * block_rows)
    grad_rows = rows_back(hidden_now, gate_full, up_full, splits)
    returned_grads = Exchange(*grad_rows)
    gate_up_sum.step(*grad_rows)

    returned = returned.together(seat, *gate_up_sum.sent, *down_sum.arrived())
    pair_values = [matmul(picks, returned) for picks in from_slot]
    block_out = (
        mid_rows + pair_values[0] * gate_vals[:, 0:1] + pair_values[1] * gate_vals[:, 1:2]
    ).astype(jnp.bfloat16)
    grad_final = cotangent.astype(jnp.float32)
    grad_gates = (
        jnp.stack([jnp.sum(grad_final * values, -1) for values in pair_values], 1) * kept_pair
    )
    grad_router = jnp.sum(chosen * grad_gates[:, :, None], 1)
    grad_logits = (
        router * (grad_router - jnp.sum(router * grad_router, -1, keepdims=True))
    ).astype(jnp.bfloat16)
    context_mine, context_other = core_columns(after(context, grad_logits))
    returned_grads.forward(grad_logits, context_mine, context_other, *gate_up_sum.arrived())
    down_sum.step(grad_logits, *gate_up_sum.arrived())
    gate_up_sum.step(*down_sum.sent)
    returned_grads = returned_grads.together(seat, *gate_up_sum.sent)
    grad_normed_two = matmul(grad_logits, w_router.T) + matmul(
        from_slot[0] + from_slot[1], returned_grads
    )
    grad_mid_norm, gain_two_local = norm_backward(grad_normed_two, mid_rows, inv_two, gain_two)
    grad_mid = grad_final + grad_mid_norm

    grad_branch = grad_mid.astype(jnp.bfloat16)
    grad_context = dot_dims(grad_branch, full_out, 1, 1).astype(jnp.bfloat16)

    def half_product(columns, grads):
        product = dot_dims(columns, grads, 0, 0).astype(jnp.bfloat16)
        return product.reshape(dp_count, half_rows, -1)

    out_other = half_product(context_other, grad_branch)
    out_mine = half_product(context_mine, grad_branch)
    (grad_context,) = tie((grad_context,), (out_mine, out_other))
    out_other = swap(out_other, 1)
    grad_query, grad_key, grad_value, near, away = attend_backward(
        qkv, grad_context, lse, seq_bucket, far, bias
    )
    grad_query, grad_key, grad_value, near, away = tie(
        (grad_query, grad_key, grad_value, near, away), (*down_sum.arrived(), out_other)
    )
    qkv_grads = jnp.concatenate([grad_query, grad_key, grad_value], 1)
    qkv_other = half_product(normed_other, qkv_grads)
    qkv_mine = half_product(after(normed_mine, qkv_other), qkv_grads)
    gate_up_sum.step(qkv_other, qkv_mine)
    qkv_other = swap(after(qkv_other, *gate_up_sum.sent), 1)
    down_share = down_sum.finish(*gate_up_sum.sent, joined=True)
    down_blocks = Spread(after(down_share, *gate_up_sum.sent))
    qkv_mine, out_mine = tie((qkv_mine, out_mine), gate_up_sum.sent)
    weight_parts = jnp.concatenate(
        [
            (mine.astype(jnp.float32) + other.astype(jnp.float32)).astype(jnp.bfloat16)
            for mine, other in ((qkv_mine, qkv_other), (out_mine, out_other))
        ],
        2,
    )
    weight_sum = RingSum(weight_parts, seat)
    near, away = tie((near, away), gate_up_sum.sent)
    table_local = table_sums(near, away)
    weight_sum.step(weight_parts, table_local, *down_blocks.arrived())
    (late_grads,) = tie((qkv_grads,), weight_sum.sent)
    grad_normed = dot_dims(late_grads, full_qkv, 1, 1)
    grad_row_one, gain_one_local = norm_backward(grad_normed, row_one, inv_one, gain_one)
    input_grad = grad_mid + grad_row_one
    down_blocks.hop(*weight_sum.sent)

    gate_up_share = gate_up_sum.finish(input_grad)
    gate_blocks, up_blocks = Spread(gate_up_share[0]), Spread(gate_up_share[1])
    weight_sum.step(gate_up_share, *down_blocks.arrived())
    (late_rows,) = tie((normed_two,), weight_sum.sent)
    small = SumAll((gain_one_local, table_local, gain_two_local, matmul(late_rows.T, grad_logits)))
    weight_sum.step(small.hop(*weight_sum.sent), *gate_blocks.arrived())
    Spread.hop_own(gate_blocks, up_blocks, gate_up_share, *weight_sum.sent)
    weight_sum.step(small.hop(*weight_sum.sent), *up_blocks.arrived(), *up_blocks.own_last)
    gate_blocks.hop(*weight_sum.sent)
    up_blocks.hop(*weight_sum.sent)
    down_out = down_blocks.outputs(device, *weight_sum.sent)
    rounded = weight_sum.finish(
        down_out, small.hop(*weight_sum.sent), *gate_blocks.arrived(), *up_blocks.arrived()
    )
    gate_out = gate_blocks.outputs(device, rounded, small.hop(rounded))
    up_out = up_blocks.outputs(device, gate_out)
    bit = owner_count // 2
    while bit > 1:
        arriving = after(swap(rounded, bit), gate_out, up_out)
        share = rounded.astype(jnp.float32) + arriving.astype(jnp.float32)
        rounded = share.astype(jnp.bfloat16)
        bit //= 2
    other = swap(rounded, 1)
    small.hop(rounded)
    gain_one_grad, table_grad, gain_two_grad, router_grad = small.finish()
    weight_grads = jnp.concatenate(
        [jnp.where(core == 0, rounded, other), jnp.where(core == 0, other, rounded)], 1
    ).astype(jnp.float32)
    query_grad, key_grad, value_grad, out_grad = (
        weight_grads[i // 2, :, i % 2 * D : (i % 2 + 1) * D] for i in range(4)
    )
    return (
        block_out,
        input_grad,
        gain_one_grad,
        query_grad,
        key_grad,
        value_grad,
        out_grad,
        table_grad,
        gain_two_grad,
        router_grad,
        gate_out,
        up_out,
        down_out,
    )


def solution(mesh):
    placed = (
        P(("dp", "expert"), None),
        P(("dp", "expert"), None),
        P(),
        P("dp", None),
        P("dp", None),
        P("dp", None),
        P("dp", None),
        P(),
        P(),
        P(),
        P(None, "dp", None),
        P(None, "dp", None),
        P(None, "dp", None),
        P(("dp", "expert"), None),
        P(("dp", "expert"), None),
        P(("dp", "expert"), None),
        P(("dp", "expert")),
    )
    return jax.shard_map(
        body,
        mesh=mesh,
        in_specs=placed,
        out_specs=(
            P(("dp", "expert"), None),
            P(("dp", "expert"), None),
            P(),
            P("dp", None),
            P("dp", None),
            P("dp", None),
            P("dp", None),
            P(),
            P(),
            P(),
            P(None, "dp", None),
            P(None, "dp", None),
            P(None, "dp", None),
        ),
        check_vma=False,
    )
```

```python
import math

import jax
import jax.numpy as jnp
import numpy as np
from jax import lax
from jax.experimental import pallas as pl
from jax.experimental.pallas import tpu as pltpu
from jax.sharding import PartitionSpec as P

D = 1024
H = 16
HEAD = 64
EXPERTS = 4
BUCKETS = 32
LONG = 512
SHORT = 128
PAIR = 2 * HEAD
TILES = LONG // SHORT
EPSILON = 1e-06
FF_TILE = 256
LAY_TILE = 512
MIB = 1024 * 1024
MASKED = -1e30


def bucket_of(offsets):
    distance = np.abs(offsets)
    half_count = BUCKETS // 2
    exact_count = half_count // 2
    widened = np.maximum(distance, 1)
    far_bucket = exact_count + np.floor(
        np.log(widened / exact_count) / np.log(128.0 / exact_count) * (half_count - exact_count)
    ).astype(np.int32)
    far_bucket = np.minimum(far_bucket, half_count - 1)
    inside = np.where(distance < exact_count, distance, far_bucket)
    return (np.where(offsets > 0, half_count, 0) + inside).astype(np.int32)


def near_buckets():
    places = np.arange(SHORT)
    inside = places[:, None] - places[None, :]
    return np.stack([bucket_of(SHORT * step + inside) for step in (-1, 0, 1)]).reshape(-1)


def near_onehot():
    buckets = jnp.asarray(near_buckets().astype(np.int8)).astype(jnp.int32)
    return (jnp.arange(BUCKETS, dtype=jnp.int32)[:, None] == buckets[None, :]).astype(jnp.float32)


FAR_BEFORE = BUCKETS // 2 - 1
FAR_AFTER = BUCKETS - 1


def ring_order(count):
    cols = 4 if count >= 16 else 2
    rows = count // cols
    cycle = [(0, col) for col in range(cols)]
    for row in range(1, rows):
        span = range(cols - 1, 0, -1) if row % 2 else range(1, cols)
        cycle += [(row, col) for col in span]
    cycle += [(row, 0) for row in range(rows - 1, 0, -1)]
    return [row * cols + col for row, col in cycle]


def ring_tables(count):
    ring = ring_order(count)
    ahead = [(ring[i], ring[(i + 1) % count]) for i in range(count)]
    behind = [(there, here) for here, there in ahead]
    place = {index: i for i, index in enumerate(ring)}
    seats = np.asarray(
        [[ring[(place[g] + d) % count] for d in range(count)] for g in range(count)], np.int32
    )
    return ahead, behind, seats


def after(value, *others):
    return lax.optimization_barrier((value, *others))[0]


def matmul(left, right):
    return jnp.dot(left, right, preferred_element_type=jnp.float32)


def dot_dims(left, right, left_dim, right_dim):
    return lax.dot_general(
        left, right, (((left_dim,), (right_dim,)), ((), ())), preferred_element_type=jnp.float32
    )


def tie(values, others):
    values = tuple(values)
    return lax.optimization_barrier(values + tuple(others))[: len(values)]


def pick(array, index, axis=0):
    return lax.dynamic_index_in_dim(array, index, axis, keepdims=False, allow_negative_indices=False)


def lay_kernel(places, spots_ref, *refs):
    *piece_refs, out_ref = refs
    for piece_ref, place in zip(piece_refs, places):
        index = place(spots_ref)
        out_ref[index] = piece_ref[: index[-1].size]


def lay_together(spots, pieces, shape, places, tile, start=0):
    lead = (0,) * (len(shape) - 1)
    first = start // tile
    return pl.pallas_call(
        lambda *refs: lay_kernel(places, *refs),
        grid_spec=pltpu.PrefetchScalarGridSpec(
            num_scalar_prefetch=1,
            grid=(shape[-1] // tile,),
            in_specs=[
                pl.BlockSpec((piece.shape[0], tile), lambda i, spots: (0, i + first))
                for piece in pieces
            ],
            out_specs=pl.BlockSpec((*shape[:-1], tile), lambda i, spots: (*lead, i)),
        ),
        out_shape=jax.ShapeDtypeStruct(shape, jnp.bfloat16),
        compiler_params=pltpu.CompilerParams(vmem_limit_bytes=16 * MIB),
        cost_estimate=pl.CostEstimate(
            flops=0, bytes_accessed=4 * math.prod(shape), transcendentals=0
        ),
    )(spots, *pieces)


class RingGather:
    def __init__(self, block, seat):
        self.count = lax.axis_size("dp")
        self.ahead, self.behind, _ = ring_tables(self.count)
        self.seat, self.rows, self.taken = seat, block.shape[0], 0
        self.low = self.high = block
        self.mid = min((self.rows // 2 + 15) // 16 * 16, self.rows)
        self.pieces = [(block, 0, 0)]

    def arrived(self):
        return (self.low, self.high)

    def step(self, *others):
        half = self.count // 2
        if self.taken >= half:
            return
        if self.taken == 0:
            self.sent = (low,) = tie((self.low,), others)
            high = low
        else:
            self.sent = low, high = tie((self.low, self.high), others)
        self.taken += 1
        last = self.taken == half
        low, high = (low[: self.mid], high[self.mid :]) if last else (low, high)
        self.low = lax.ppermute(low, "dp", self.ahead)
        self.high = lax.ppermute(high, "dp", self.behind)
        self.pieces += [
            (self.low, (half if last else -self.taken) % self.count, 0),
            (self.high, self.taken, self.mid if last else 0),
        ]

    def finish(self, *others):
        while self.taken < self.count // 2:
            self.step()
        columns = self.pieces[0][0].shape[1]
        places = []
        for piece, step, start in self.pieces:

            def place(spots, step=step, start=start, rows=piece.shape[0]):
                return (spots[step], pl.ds(start, rows))

            places.append(place)
        out = lay_together(
            after(self.seat, *others),
            [piece for piece, _, _ in self.pieces],
            (self.count, self.rows, columns),
            places,
            columns // 2,
        )
        return out.reshape(-1, columns)


def ring_sum_kernel(received, outs, *refs):
    own_refs, received_refs = refs[:outs], refs[outs:-outs]
    side = pl.program_id(0)
    for out in range(outs):
        total = own_refs[out][...].astype(jnp.float32)
        for received_ref, (target, only) in zip(received_refs, received):
            if target == out:
                more = received_ref[...].astype(jnp.float32)
                total = total + (more if only is None else jnp.where(side == only, more, 0.0))
        refs[out - outs][...] = total.astype(jnp.bfloat16)


class RingSum:
    def __init__(self, parts, seat, entry=None):
        self.count = lax.axis_size("dp")
        self.ahead, self.behind, _ = ring_tables(self.count)
        self.seat, self.parts, self.entry, self.taken = seat, parts, entry, 0
        if entry is None:
            self.shape = (parts.shape[1], parts.shape[2] // 2)
        else:
            self.shape = (D // self.count, parts.shape[2])
        self.low = self.high = None

    def own(self, step, side=0):
        step = step % self.count
        if self.entry is None:
            return self.parts, pl.BlockSpec(
                (None, *self.shape), lambda i, seat: (seat[step], 0, i + side)
            )
        first = self.entry + side
        return self.parts, pl.BlockSpec(
            (None, *self.shape), lambda i, seat: (first + i, seat[step], 0)
        )

    def call(self, own, received, operands, others=(), halves=2, joined=False):
        moved = 2 * halves * math.prod(self.shape)

        def block(item):
            if item.shape[0] == 1:
                return pl.BlockSpec((None, *self.shape), lambda i, seat: (0, 0, 0))
            return pl.BlockSpec((None, *self.shape), lambda i, seat: (i, 0, 0))

        if joined:
            out_spec = pl.BlockSpec(self.shape, lambda i, seat: (0, i))
            out_shape = (self.shape[0], halves * self.shape[1])
        else:
            out_spec = pl.BlockSpec((None, *self.shape), lambda i, seat: (i, 0, 0))
            out_shape = (halves, *self.shape)
        return pl.pallas_call(
            lambda seat_ref, *refs: ring_sum_kernel(received, len(own), *refs),
            grid_spec=pltpu.PrefetchScalarGridSpec(
                num_scalar_prefetch=1,
                grid=(halves,),
                in_specs=[spec for _, spec in own] + [block(item) for item in operands],
                out_specs=[out_spec] * len(own),
            ),
            out_shape=[jax.ShapeDtypeStruct(out_shape, jnp.bfloat16)] * len(own),
            compiler_params=pltpu.CompilerParams(
                vmem_limit_bytes=(16 if self.entry is None else 40) * MIB
            ),
            cost_estimate=pl.CostEstimate(
                flops=2 * moved,
                bytes_accessed=moved * (len(operands) + 2 * len(own)),
                transcendentals=0,
            ),
        )(after(self.seat, *others), *(part for part, _ in own), *operands)

    def arrived(self):
        return (self.low, self.high)

    def received(self, targets):
        single = self.taken == 1
        return [(targets[0], 0 if single else None), (targets[1], 1 if single else None)]

    def step(self, *others):
        half = self.count // 2
        if self.taken >= half:
            return
        distance = half - self.taken
        if self.taken:
            received, operands = self.received((0, 1)), tie(self.arrived(), others)
            sent = self.call(self.following, received, operands)
        else:
            own = (self.own(distance), self.own(-distance, 1))
            sent = self.call(own, [], (), others, 1)
        self.low = lax.ppermute(sent[0], "dp", self.ahead)
        self.high = lax.ppermute(sent[1], "dp", self.behind)
        self.taken += 1
        distance -= 1
        steps = (distance, -distance) if distance else (0,)
        self.following = [self.own(step) for step in steps]
        self.sent = tuple(sent)

    def finish(self, *others, joined=False):
        while self.taken < self.count // 2:
            self.step()
        received, operands = self.received((0, 0)), tie(self.arrived(), others)
        return self.call(self.following, received, operands, joined=joined)[0]


def swap(value, bit):
    count = lax.axis_size("expert")
    return lax.ppermute(value, "expert", [(i, i ^ bit) for i in range(count)])


class Exchange:
    def __init__(self, own, near, far):
        self.own, self.count, self.rows = own, lax.axis_size("expert"), own.shape[0]
        self.near, self.last = swap(near, 1), None
        if self.count == 4:
            self.far = swap(far, 2)
        else:
            blocks = far.reshape(-1, self.rows, far.shape[1])
            self.far = [swap(block, bit + 2) for bit, block in enumerate(blocks)]

    def forward(self, *others):
        if self.count == 4:
            self.last = swap(after(self.far, *others)[self.rows :], 1)
        return self

    def arrived(self):
        return (self.near, self.last) if self.count == 4 else tuple(self.far)

    def together(self, seat, *others):
        if self.count == 4:
            pieces = [self.own, self.near, self.far, self.last]
        else:
            pieces = [self.own, self.near, *self.far]
        places = [
            lambda spots, d=d: (pl.ds(d * self.rows, self.rows),) for d in range(len(pieces))
        ]
        shape = (self.count * self.rows, self.own.shape[1])
        return lay_together(after(seat, *others), pieces, shape, places, LAY_TILE)


class Spread:
    def __init__(self, value):
        self.bit = lax.axis_size("expert") // 2
        self.held = {0: (value, None)}
        self.hop()

    @classmethod
    def hop_own(cls, first, second, both, *others):
        swapped = swap(after(both, *others), 1)
        for lead, spread in enumerate((first, second)):
            spread.held[0] = (both, lead)
            spread.held[1] = (swapped, lead)
            spread.own_last = (swapped,)

    def hop(self, *others):
        if not self.bit:
            return
        keys = [key for key in self.held if key ^ self.bit not in self.held]
        items = [self.held[key] for key in keys]
        items = tie((item if lead is None else item[lead] for item, lead in items), others)
        fresh = {key ^ self.bit: swap(item, self.bit) for key, item in zip(keys, items)}
        self.last = tuple(fresh.values())
        self.held.update({key: (item, None) for key, item in fresh.items()})
        self.bit //= 2

    def arrived(self):
        return self.last

    def outputs(self, device, *others):
        while self.bit:
            self.hop()
        keys = sorted(self.held)
        shares = len(keys) // EXPERTS
        rows, columns = self.held[0][0].shape[-2:]
        tile = columns // 2

        def spec(lead):
            if lead is None:
                return pl.BlockSpec((rows, tile), lambda i, spots: (0, i))
            return pl.BlockSpec((None, rows, tile), lambda i, spots: (lead, 0, i))

        def kernel(spots_ref, *refs):
            *block_refs, out_ref = refs
            for first in range(0, len(keys), shares):
                total = block_refs[first][...].astype(jnp.float32)
                for block_ref in block_refs[first + 1 : first + shares]:
                    total = total + block_ref[...].astype(jnp.float32)
                out_ref[spots_ref[first]] = total

        spots = jnp.stack([device ^ key if shares == 1 else lax.div(device ^ key, shares) for key in keys])
        return pl.pallas_call(
            kernel,
            grid_spec=pltpu.PrefetchScalarGridSpec(
                num_scalar_prefetch=1,
                grid=(2,),
                in_specs=[spec(self.held[key][1]) for key in keys],
                out_specs=pl.BlockSpec((EXPERTS, rows, tile), lambda i, spots: (0, 0, i)),
            ),
            out_shape=jax.ShapeDtypeStruct((EXPERTS, rows, columns), jnp.float32),
            compiler_params=pltpu.CompilerParams(vmem_limit_bytes=24 * MIB),
            cost_estimate=pl.CostEstimate(
                flops=0, bytes_accessed=6 * EXPERTS * rows * columns, transcendentals=0
            ),
        )(after(spots, *others), *(self.held[key][0] for key in keys))


class SumAll:
    def __init__(self, parts):
        self.shapes = [part.shape for part in parts]
        self.flat = jnp.concatenate([part.reshape(-1, 128) for part in parts], 0)
        self.hops = []
        for axis in ("expert", "dp"):
            bit, count = 1, lax.axis_size(axis)
            while bit < count:
                self.hops.append((axis, [(i, i ^ bit) for i in range(count)]))
                bit *= 2
        over_x = self.hops.pop(1)
        self.hops.append(over_x)

    def hop(self, *others):
        if not self.hops:
            return self.flat
        axis, pairs = self.hops.pop(0)
        flat = after(self.flat, *others)
        self.flat = flat + lax.ppermute(flat, axis, pairs)
        return self.flat

    def finish(self, *others):
        while self.hops:
            self.hop(*others)
        sums, start = [], 0
        for shape in self.shapes:
            rows = math.prod(shape) // 128
            sums.append(self.flat[start : start + rows].reshape(shape))
            start += rows
        return sums


def norm_backward(grad_rows, row_data, inverse, gain_vec):
    scaled = grad_rows * gain_vec
    inner_mean = jnp.mean(scaled * row_data, -1, keepdims=True)
    grad_input = inverse * scaled - row_data * inverse * inverse * inverse * inner_mean
    return (grad_input, jnp.sum(grad_rows * row_data * inverse, 0))


def other_head_zeroed(rows_t, head):
    own = rows_t[head * HEAD : (head + 1) * HEAD]
    rest = jnp.zeros_like(own)
    return jnp.concatenate([own, rest] if head == 0 else [rest, own], 0)


def tile_biases(bias_ref, far_ref, pair, head, penalty):
    near = {
        -1: bias_ref[head, 0] + penalty,
        0: bias_ref[head, 1],
        1: bias_ref[head, 2] + penalty,
    }
    before = far_ref[0, 2 * pair + head] + penalty
    later = far_ref[1, 2 * pair + head] + penalty
    return lambda step: near[step] if abs(step) < 2 else (before if step < 0 else later)


def transposed(rows):
    return rows.astype(jnp.float32).T


def attend_forward_kernel(
    flag_ref, far_ref, q_ref, k_ref, v_ref, bias_ref, ctx_ref, lse_ref
):
    block, pair = pl.program_id(0), pl.program_id(1)
    penalty = jnp.where(flag_ref[block] == 0, 0.0, MASKED).astype(jnp.float32)
    query_t = (transposed(q_ref[...]) * (1.0 / math.sqrt(HEAD))).astype(jnp.bfloat16)
    value_t = transposed(v_ref[...]).astype(jnp.bfloat16)
    key_rows = k_ref[...]
    parts = []
    for head in range(2):
        bias = tile_biases(bias_ref, far_ref, pair, head, penalty)
        scores = dot_dims(key_rows, other_head_zeroed(query_t, head), 1, 0)
        value_head = value_t[head * HEAD : (head + 1) * HEAD]
        pieces = []
        for col in range(TILES):
            cols = slice(col * SHORT, (col + 1) * SHORT)
            panel = jnp.concatenate(
                [
                    scores[row * SHORT : (row + 1) * SHORT, cols] + bias(row - col)
                    for row in range(TILES)
                ],
                0,
            )
            highest = jnp.max(panel, 0, keepdims=True)
            raised = jnp.exp(panel - highest)
            total = jnp.sum(raised, 0, keepdims=True)
            piece = matmul(value_head, raised.astype(jnp.bfloat16))
            pieces.append(piece / total)
            lse_ref[0, 0, head : head + 1, cols] = highest + jnp.log(total)
        parts.append(pieces)
    for col in range(TILES):
        joined = jnp.concatenate([parts[0][col], parts[1][col]], 0)
        ctx_ref[col * SHORT : (col + 1) * SHORT, :] = joined.T.astype(jnp.bfloat16)


def attend_forward(qkv, flags, far, bias):
    tok_count = qkv.shape[0]
    blocks = tok_count // LONG
    pairs = H // 2

    def column(first):
        return pl.BlockSpec((LONG, PAIR), lambda b, p, flag: (b, first + p))

    return pl.pallas_call(
        attend_forward_kernel,
        grid_spec=pltpu.PrefetchScalarGridSpec(
            num_scalar_prefetch=1,
            grid=(blocks, pairs),
            in_specs=[
                pl.BlockSpec(memory_space=pltpu.SMEM),
                column(0),
                column(pairs),
                column(2 * pairs),
                pl.BlockSpec((2, 3, SHORT, SHORT), lambda b, p, flag: (p, 0, 0, 0)),
            ],
            out_specs=[
                column(0),
                pl.BlockSpec((1, 1, 2, LONG), lambda b, p, flag: (b, p, 0, 0)),
            ],
        ),
        out_shape=[
            jax.ShapeDtypeStruct((tok_count, D), jnp.bfloat16),
            jax.ShapeDtypeStruct((blocks, pairs, 2, LONG), jnp.float32),
        ],
        compiler_params=pltpu.CompilerParams(vmem_limit_bytes=16 * MIB),
        cost_estimate=pl.CostEstimate(
            flops=8 * H * LONG * LONG * HEAD * blocks,
            bytes_accessed=8 * tok_count * D + 12 * H * SHORT * SHORT,
            transcendentals=H * LONG * LONG * blocks,
        ),
    )(flags, far, qkv, qkv, qkv, bias)


def attend_backward_kernel(
    flag_ref,
    far_ref,
    q_ref,
    k_ref,
    v_ref,
    grad_ref,
    lse_ref,
    bias_ref,
    dq_ref,
    dk_ref,
    dv_ref,
    near_ref,
    away_ref,
    weight_scr,
    score_scr,
):
    pair, block = pl.program_id(0), pl.program_id(1)
    penalty = jnp.where(flag_ref[block] == 0, 0.0, MASKED).astype(jnp.float32)
    scaled = (q_ref[...].astype(jnp.float32) * (1.0 / math.sqrt(HEAD))).astype(jnp.bfloat16)
    query_t = transposed(scaled).astype(jnp.bfloat16)
    grad_t = transposed(grad_ref[...]).astype(jnp.bfloat16)
    key_t = transposed(k_ref[...]).astype(jnp.bfloat16)
    key_rows, value_rows, grad_rows = k_ref[...], v_ref[...], grad_ref[...]

    @pl.when(block == 0)
    def _():
        near_ref[...] = jnp.zeros_like(near_ref)
        away_ref[...] = jnp.zeros_like(away_ref)

    query_parts, key_parts, value_parts = [], [], []
    for head in range(2):
        bias = tile_biases(bias_ref, far_ref, pair, head, penalty)
        scores = dot_dims(key_rows, other_head_zeroed(query_t, head), 1, 0)
        grad_probs = dot_dims(value_rows, other_head_zeroed(grad_t, head), 1, 0)
        key_head = key_t[head * HEAD : (head + 1) * HEAD]
        near = {-1: None, 0: None, 1: None}
        away = [None, None]
        for col in range(TILES):
            cols = slice(col * SHORT, (col + 1) * SHORT)
            total = lse_ref[0, 0, head : head + 1, cols]
            probs = jnp.exp(
                jnp.concatenate(
                    [
                        scores[row * SHORT : (row + 1) * SHORT, cols] + bias(row - col)
                        for row in range(TILES)
                    ],
                    0,
                )
                - total
            )
            panel = grad_probs[:, cols]
            inner = jnp.sum(probs * panel, 0, keepdims=True)
            grad_scores = (probs * (panel - inner)).astype(jnp.bfloat16)
            weight_scr[:, cols] = probs.astype(jnp.bfloat16)
            score_scr[:, cols] = grad_scores
            rounded = grad_scores.astype(jnp.float32)
            for row in range(TILES):
                tile = rounded[row * SHORT : (row + 1) * SHORT]
                step = row - col
                if abs(step) < 2:
                    near[step] = tile if near[step] is None else near[step] + tile
                else:
                    side = 0 if step < 0 else 1
                    tile = jnp.sum(tile, 0, keepdims=True)
                    away[side] = tile if away[side] is None else away[side] + tile
        for step in (-1, 0, 1):
            near_ref[head, step + 1] += near[step]
        for side in range(2):
            away_ref[0, head, side : side + 1, :] += away[side]
        query_parts.append(matmul(key_head, score_scr[...]))
        key_parts.append(matmul(score_scr[...], scaled))
        value_parts.append(matmul(weight_scr[...], grad_rows))
    lane = lax.broadcasted_iota(jnp.int32, (LONG, PAIR), 1)
    dk_ref[...] = jnp.where(lane < HEAD, key_parts[0], key_parts[1]).astype(jnp.bfloat16)
    dv_ref[...] = jnp.where(lane < HEAD, value_parts[0], value_parts[1]).astype(jnp.bfloat16)
    joined = jnp.concatenate(query_parts, 0) * (1.0 / math.sqrt(HEAD))
    dq_ref[...] = joined.T.astype(jnp.bfloat16)


def attend_backward(qkv, grad_context, lse, flags, far, bias):
    tok_count = qkv.shape[0]
    blocks = tok_count // LONG
    pairs = H // 2

    def column(first):
        return pl.BlockSpec((LONG, PAIR), lambda p, b, flag: (b, first + p))

    rows = jax.ShapeDtypeStruct((tok_count, D), jnp.bfloat16)
    return pl.pallas_call(
        attend_backward_kernel,
        grid_spec=pltpu.PrefetchScalarGridSpec(
            num_scalar_prefetch=1,
            grid=(pairs, blocks),
            in_specs=[
                pl.BlockSpec(memory_space=pltpu.SMEM),
                column(0),
                column(pairs),
                column(2 * pairs),
                column(0),
                pl.BlockSpec((1, 1, 2, LONG), lambda p, b, flag: (b, p, 0, 0)),
                pl.BlockSpec((2, 3, SHORT, SHORT), lambda p, b, flag: (p, 0, 0, 0)),
            ],
            out_specs=[
                column(0),
                column(0),
                column(0),
                pl.BlockSpec((2, 3, SHORT, SHORT), lambda p, b, flag: (p, 0, 0, 0)),
                pl.BlockSpec((1, 2, 2, SHORT), lambda p, b, flag: (p, 0, 0, 0)),
            ],
            scratch_shapes=[
                pltpu.VMEM((LONG, LONG), jnp.bfloat16),
                pltpu.VMEM((LONG, LONG), jnp.bfloat16),
            ],
        ),
        out_shape=[
            rows,
            rows,
            rows,
            jax.ShapeDtypeStruct((H, 3, SHORT, SHORT), jnp.float32),
            jax.ShapeDtypeStruct((pairs, 2, 2, SHORT), jnp.float32),
        ],
        compiler_params=pltpu.CompilerParams(vmem_limit_bytes=24 * MIB),
        cost_estimate=pl.CostEstimate(
            flops=20 * H * LONG * LONG * HEAD * blocks,
            bytes_accessed=16 * tok_count * D + 24 * H * SHORT * SHORT,
            transcendentals=H * LONG * LONG * blocks,
        ),
    )(flags, far, qkv, qkv, qkv, grad_context, lse, bias)


ROW_TILE = 256
GELU_SCALE = math.sqrt(2.0 / math.pi)
GELU_CUBE = 0.044715


def row_tiles(rows):
    return [slice(start, min(start + ROW_TILE, rows)) for start in range(0, rows, ROW_TILE)]


def gate_kernel(rows_ref, weight_ref, act_ref, slope_ref):
    for part in row_tiles(rows_ref.shape[0]):
        pre = matmul(rows_ref[part, :], weight_ref[...])
        square = pre * pre
        angle = jnp.tanh(pre * (GELU_SCALE + (GELU_SCALE * GELU_CUBE) * square))
        half = 0.5 + 0.5 * angle
        act_ref[part, :] = (pre * half).astype(jnp.bfloat16)
        bend = (0.5 * GELU_SCALE) + (1.5 * GELU_SCALE * GELU_CUBE) * square
        slope_ref[part, :] = (half + pre * (1.0 - angle * angle) * bend).astype(jnp.bfloat16)


def up_kernel(rows_ref, weight_ref, act_ref, slope_ref, grads_ref, hid_ref, lift_ref, down_ref):
    for part in row_tiles(rows_ref.shape[0]):
        lift = matmul(rows_ref[part, :], weight_ref[...])
        hid_ref[part, :] = (act_ref[part, :].astype(jnp.float32) * lift).astype(jnp.bfloat16)
        lift_ref[part, :] = (slope_ref[part, :].astype(jnp.float32) * lift).astype(jnp.bfloat16)
    down_ref[...] = dot_dims(hid_ref[...], grads_ref[...], 0, 0).astype(jnp.bfloat16)


def hidden_back_kernel(grads_ref, down_ref, lift_ref, act_ref, rows_t_ref, out_ref):
    for part in row_tiles(grads_ref.shape[0]):
        back = dot_dims(grads_ref[part, :], down_ref[...], 1, 1)
        out_ref[0, part, :] = (back * lift_ref[part, :].astype(jnp.float32)).astype(jnp.bfloat16)
        out_ref[1, part, :] = (back * act_ref[part, :].astype(jnp.float32)).astype(jnp.bfloat16)
    rows = rows_t_ref.shape[0]
    for part in row_tiles(rows):
        out_ref[2, part, :] = matmul(rows_t_ref[part, :], out_ref[0]).astype(jnp.bfloat16)
        out_ref[3, part, :] = matmul(rows_t_ref[part, :], out_ref[1]).astype(jnp.bfloat16)
    rest = jnp.zeros((2, out_ref.shape[1] - rows, out_ref.shape[2]), jnp.bfloat16)
    out_ref[2:, rows:, :] = rest


def rows_back_kernel(pre_ref, up_ref, gate_w_ref, up_w_ref, *out_refs):
    total = dot_dims(pre_ref[...], gate_w_ref[...], 1, 1) + dot_dims(up_ref[...], up_w_ref[...], 1, 1)
    start = 0
    for out_ref in out_refs:
        rows = out_ref.shape[0]
        out_ref[...] = total[start : start + rows].astype(jnp.bfloat16)
        start += rows


def kernel_call(kernel, operands, in_specs, out_specs, out_shape, steps, flops, vmem):
    moved = sum(2 * math.prod(item.shape) for item in (*operands, *out_shape))
    return pl.pallas_call(
        kernel,
        grid=(steps,),
        in_specs=in_specs,
        out_specs=out_specs,
        out_shape=[jax.ShapeDtypeStruct(item.shape, jnp.bfloat16) for item in out_shape],
        compiler_params=pltpu.CompilerParams(vmem_limit_bytes=vmem * MIB),
        cost_estimate=pl.CostEstimate(flops=flops, bytes_accessed=moved, transcendentals=0),
    )(*operands)


def width_tiles(width):
    return pl.cdiv(width, FF_TILE)


def whole_spec(shape, buffers=2):
    return pl.BlockSpec(shape, lambda i: (0, 0), pipeline_mode=pl.Buffered(buffers))


def gate_forward(rows, weight):
    count, width = rows.shape[0], weight.shape[1]
    tile = pl.BlockSpec((count, FF_TILE), lambda i: (0, i))
    shape = jax.ShapeDtypeStruct((count, width), jnp.bfloat16)
    return kernel_call(
        gate_kernel,
        (rows, weight),
        [whole_spec(rows.shape), pl.BlockSpec((D, FF_TILE), lambda i: (0, i))],
        [tile, tile],
        [shape, shape],
        width_tiles(width),
        2 * count * D * width,
        59,
    )


def up_forward(rows, weight, act, slope, grads):
    count, width = rows.shape[0], weight.shape[1]
    tile = pl.BlockSpec((count, FF_TILE), lambda i: (0, i))
    shape = jax.ShapeDtypeStruct((count, width), jnp.bfloat16)
    return kernel_call(
        up_kernel,
        (rows, weight, act, slope, grads),
        [
            whole_spec(rows.shape),
            pl.BlockSpec((D, FF_TILE), lambda i: (0, i)),
            tile,
            tile,
            whole_spec(grads.shape),
        ],
        [tile, tile, pl.BlockSpec((FF_TILE, D), lambda i: (i, 0))],
        [shape, shape, jax.ShapeDtypeStruct((width, D), jnp.bfloat16)],
        width_tiles(width),
        4 * count * D * width,
        59,
    )


def hidden_back(grads, weight, lift, act, rows_t):
    count, width = lift.shape
    tile = pl.BlockSpec((count, FF_TILE), lambda i: (0, i))
    return kernel_call(
        hidden_back_kernel,
        (grads, weight, lift, act, rows_t),
        [
            whole_spec(grads.shape),
            pl.BlockSpec((FF_TILE, D), lambda i: (i, 0)),
            tile,
            tile,
            whole_spec(rows_t.shape),
        ],
        [pl.BlockSpec((4, count, FF_TILE), lambda i: (0, 0, i))],
        [jax.ShapeDtypeStruct((4, count, width), jnp.bfloat16)],
        width_tiles(width),
        6 * count * D * width,
        59,
    )[0]


def rows_back(hidden_grads, gate_weight, up_weight, splits):
    _, count, width = hidden_grads.shape
    weight_tile = pl.BlockSpec((ROW_TILE, width), lambda i: (i, 0))

    def entry(number):
        return pl.BlockSpec(
            (None, count, width), lambda i: (number, 0, 0), pipeline_mode=pl.Buffered(1)
        )

    return kernel_call(
        rows_back_kernel,
        (hidden_grads, hidden_grads, gate_weight, up_weight),
        [entry(0), entry(1), weight_tile, weight_tile],
        [pl.BlockSpec((rows, ROW_TILE), lambda i: (0, i)) for rows in splits],
        [jax.ShapeDtypeStruct((rows, D), jnp.bfloat16) for rows in splits],
        D // ROW_TILE,
        4 * count * D * width,
        59,
    )


def table_sums(near, away):
    near_part = lax.dot_general(
        near_onehot(),
        near.reshape(H, -1),
        (((1,), (1,)), ((), ())),
        precision=lax.Precision.HIGHEST,
        preferred_element_type=jnp.float32,
    )
    far_part = jnp.sum(away, -1).reshape(H, 2)
    sides = np.zeros((BUCKETS, 2), np.float32)
    sides[FAR_BEFORE, 0] = sides[FAR_AFTER, 1] = 1.0
    return near_part + jnp.sum(sides[:, None, :] * far_part[None], -1)


def body(
    tokens,
    cotangent,
    gain_one,
    w_query,
    w_key,
    w_value,
    w_out,
    rel_table,
    gain_two,
    w_router,
    w_gate,
    w_up,
    w_down,
    expert_ids,
    slot_index,
    slot_kept,
    seq_bucket,
):
    tok_count = tokens.shape[0]
    dp_count = lax.axis_size("dp")
    owner_count = lax.axis_size("expert")
    shares = owner_count // EXPERTS
    group = lax.axis_index("dp")
    device = lax.axis_index("expert")
    expert = device if shares == 1 else lax.div(device, shares)
    core = device & 1
    seat = pick(jnp.asarray(ring_tables(dp_count)[2]), group)

    half_rows = w_query.shape[0] // 2

    def own_half(weight):
        return lax.dynamic_slice_in_dim(
            weight, core * half_rows, half_rows, 0, allow_negative_indices=False
        )

    slot_quota = 5 * tok_count // (2 * EXPERTS * owner_count)
    slot_span = owner_count * slot_quota
    owners_each = owner_count // shares
    block_rows = owners_each * slot_quota
    slot_room = owner_count * block_rows

    def routes(ids, slots, kept):
        owner = slots // slot_span
        dest = ids * shares + owner // owners_each
        local_slot = (
            (dest ^ device) * block_rows
            + (owner % owners_each) * slot_quota
            + slots % slot_span
            - device * slot_quota
        )
        target = jnp.where(kept == 1, local_slot, slot_room)
        room = jnp.arange(slot_room, dtype=jnp.int32)
        from_slot = [
            (target[:, k : k + 1] == room[None, :]).astype(jnp.bfloat16) for k in range(2)
        ]
        to_slot = jnp.logical_or(
            target[:, 0][None, :] == room[:, None], target[:, 1][None, :] == room[:, None]
        ).astype(jnp.bfloat16)
        return from_slot, to_slot

    def parts_of(rows):
        return rows[:block_rows], rows[block_rows : 2 * block_rows], rows[2 * block_rows :]

    def outgoing(rows, to_slot):
        return [matmul(part, rows).astype(jnp.bfloat16) for part in reversed(parts_of(to_slot))][::-1]

    def route(rows):
        logits = matmul(rows, w_router)
        raised = jnp.exp(logits - jnp.max(logits, -1, keepdims=True))
        return raised / jnp.sum(raised, -1, keepdims=True)

    weight_ring = RingGather(
        jnp.concatenate([own_half(weight) for weight in (w_query, w_key, w_value, w_out)], 1), seat
    )
    weight_ring.step()
    row_one = tokens.astype(jnp.float32)
    inv_one = lax.rsqrt(jnp.mean(row_one * row_one, -1, keepdims=True) + EPSILON)
    normed = (row_one * inv_one * gain_one).astype(jnp.bfloat16)
    theirs = [swap(weight_ring.pieces[0][0], 1)]

    def weight_step(*others):
        if weight_ring.taken < dp_count // 2:
            weight_ring.step(*others)
            theirs.extend(swap(piece, 1) for piece in weight_ring.sent)

    weight_step(inv_one)
    ids, slots, kept = tie((expert_ids, slot_index, slot_kept), weight_ring.sent)
    from_slot, to_slot = routes(ids, slots, kept)
    def core_columns(rows):
        split = rows.reshape(tok_count, dp_count, 2, half_rows)
        return [pick(split, side, 2).reshape(tok_count, -1) for side in (core, 1 - core)]

    normed_mine, normed_other = core_columns(normed)
    weight_step(to_slot, theirs[0], normed_mine, normed_other)
    cots, table = tie((cotangent, rel_table), weight_ring.sent)
    cot_blocks = outgoing(cots, to_slot)
    bias = lax.dot_general(
        after(table, *cot_blocks),
        near_onehot(),
        (((0,), (0,)), ((), ())),
        precision=lax.Precision.HIGHEST,
        preferred_element_type=jnp.float32,
    ).reshape(H, 3, SHORT, SHORT)
    far = jnp.stack([rel_table[FAR_BEFORE], rel_table[FAR_AFTER]])
    weight_step(bias, *theirs[1:3])
    while weight_ring.taken < dp_count // 2:
        weight_step()
    gate_ring = RingGather(pick(w_gate, expert), seat)
    gate_ring.step(*weight_ring.sent)
    theirs.extend(swap(piece, 1) for piece in weight_ring.arrived())
    places = []
    for side in range(2):
        for piece, step, start in weight_ring.pieces:

            def place(spots, step=step, side=side, start=start, rows=piece.shape[0]):
                return (spots[step], spots[dp_count + side], pl.ds(start, rows))

            places.append(place)
    spots = jnp.concatenate([seat, jnp.stack([core, 1 - core])])
    pieces = [piece for piece, _, _ in weight_ring.pieces] + theirs
    full_qkv = lay_together(spots, pieces, (dp_count, 2, half_rows, 3 * D), places, LAY_TILE)
    full_out = lay_together(spots, pieces, (dp_count, 2, half_rows, D), places, LAY_TILE, 3 * D)
    full_qkv, full_out = full_qkv.reshape(D, 3 * D), full_out.reshape(D, D)
    up_own, down_own = tie((pick(w_up, expert), pick(w_down, expert)), (full_qkv,))
    up_ring = RingGather(up_own, seat)
    down_ring = RingGather(down_own, seat)

    gate_ring.step(full_qkv, up_own, down_own)
    (normed_now,) = tie((normed,), gate_ring.sent)
    qkv = matmul(normed_now, full_qkv).astype(jnp.bfloat16)
    context, lse = attend_forward(qkv, seq_bucket, far, bias)
    (context,) = tie((context,), gate_ring.arrived())
    gate_ring.step(context)
    (context,) = tie((context,), gate_ring.sent)
    mid_rows = row_one + matmul(context, full_out)
    inv_two = lax.rsqrt(jnp.mean(mid_rows * mid_rows, -1, keepdims=True) + EPSILON)
    normed_two = (mid_rows * inv_two * gain_two).astype(jnp.bfloat16)
    row_blocks = outgoing(normed_two, to_slot)
    row_exchange = Exchange(*row_blocks)
    gate_ring.step(*row_blocks)
    up_ring.step(*gate_ring.sent)
    gate_full = gate_ring.finish(*up_ring.sent)
    router = route(after(normed_two, gate_full))
    chosen = (ids[:, :, None] == jnp.arange(EXPERTS, dtype=jnp.int32)).astype(jnp.float32)
    kept_pair = kept.astype(jnp.float32)
    gate_vals = jnp.sum(chosen * router[:, None, :], -1) * kept_pair
    up_ring.step(gate_vals)

    slot_rows = row_exchange.forward(*up_ring.sent).together(seat)
    cot_exchange = Exchange(*tie(cot_blocks, (slot_rows,)))
    down_ring.step(slot_rows)
    (gate_now,) = tie((gate_full,), (*down_ring.sent, cot_exchange.near))
    act, slope = gate_forward(slot_rows, gate_now)
    act, slope = tie((act, slope), up_ring.arrived())
    up_ring.step(act)
    (rows_now,) = tie((slot_rows,), up_ring.sent)
    slot_gate = lax.dynamic_index_in_dim(
        route(rows_now), expert, 1, allow_negative_indices=False
    )
    slot_rows_t = rows_now.T
    cot_exchange.forward(slot_gate, slot_rows_t, *up_ring.arrived())
    slot_cots = cot_exchange.together(seat)
    slot_grads = (slot_gate * slot_cots.astype(jnp.float32)).astype(jnp.bfloat16)
    up_ring.step(slot_gate, slot_rows_t)
    down_ring.step(*up_ring.arrived())
    up_full = up_ring.finish(*down_ring.sent, slot_grads)
    down_ring.step(up_full, slot_grads)
    (up_full,) = tie((up_full,), down_ring.sent)
    hidden, lift_slope, down_parts = up_forward(slot_rows, up_full, act, slope, slot_grads)
    hidden, lift_slope = tie((hidden, lift_slope), down_ring.arrived())
    down_ring.step(hidden)
    down_sum = RingSum(down_parts.reshape(dp_count, -1, D), seat)
    down_sum.step(*down_ring.sent)
    down_full = down_ring.finish(*down_sum.sent)

    expert_rows = matmul(hidden, down_full).astype(jnp.bfloat16)
    expert_blocks = tie(parts_of(expert_rows), down_sum.arrived())
    returned = Exchange(*expert_blocks)
    down_sum.step(expert_rows)
    (back_grads,) = tie((slot_grads,), down_sum.sent)
    hidden_grads = hidden_back(back_grads, down_full, lift_slope, act, slot_rows_t)
    (hidden_grads,) = tie(
        (hidden_grads,),
        (*down_sum.arrived(), returned.near, *(returned.arrived() if owner_count > 4 else (returned.far,))),
    )
    returned.forward(hidden_grads)
    gate_up_sum = RingSum(hidden_grads, seat, 2)
    gate_up_sum.step(hidden_grads)
    down_sum.step(*gate_up_sum.sent, *returned.arrived())
    (hidden_now,) = tie((hidden_grads,), (*down_sum.sent, *gate_up_sum.sent))
    splits = (block_rows, block_rows, slot_room - 2 * block_rows)
    grad_rows = rows_back(hidden_now, gate_full, up_full, splits)
    returned_grads = Exchange(*grad_rows)
    gate_up_sum.step(*grad_rows)

    returned = returned.together(seat, *gate_up_sum.sent, *down_sum.arrived())
    pair_values = [matmul(picks, returned) for picks in from_slot]
    block_out = (
        mid_rows + pair_values[0] * gate_vals[:, 0:1] + pair_values[1] * gate_vals[:, 1:2]
    ).astype(jnp.bfloat16)
    grad_final = cotangent.astype(jnp.float32)
    grad_gates = (
        jnp.stack([jnp.sum(grad_final * values, -1) for values in pair_values], 1) * kept_pair
    )
    grad_router = jnp.sum(chosen * grad_gates[:, :, None], 1)
    grad_logits = (
        router * (grad_router - jnp.sum(router * grad_router, -1, keepdims=True))
    ).astype(jnp.bfloat16)
    context_mine, context_other = core_columns(after(context, grad_logits))
    returned_grads.forward(grad_logits, context_mine, context_other)
    down_sum.step(grad_logits, *gate_up_sum.arrived())
    gate_up_sum.step(*down_sum.sent)
    returned_grads = returned_grads.together(seat, *gate_up_sum.sent)
    grad_normed_two = matmul(grad_logits, w_router.T) + matmul(
        from_slot[0] + from_slot[1], returned_grads
    )
    grad_mid_norm, gain_two_local = norm_backward(grad_normed_two, mid_rows, inv_two, gain_two)
    grad_mid = grad_final + grad_mid_norm

    grad_branch = grad_mid.astype(jnp.bfloat16)
    grad_context = dot_dims(grad_branch, full_out, 1, 1).astype(jnp.bfloat16)

    def half_product(columns, grads):
        product = dot_dims(columns, grads, 0, 0).astype(jnp.bfloat16)
        return product.reshape(dp_count, half_rows, -1)

    out_other = half_product(context_other, grad_branch)
    out_mine = half_product(context_mine, grad_branch)
    (grad_context,) = tie((grad_context,), (out_mine, out_other))
    out_other = swap(out_other, 1)
    grad_query, grad_key, grad_value, near, away = attend_backward(
        qkv, grad_context, lse, seq_bucket, far, bias
    )
    grad_query, grad_key, grad_value, near, away = tie(
        (grad_query, grad_key, grad_value, near, away), (*down_sum.arrived(), out_other)
    )
    qkv_grads = jnp.concatenate([grad_query, grad_key, grad_value], 1)
    qkv_other = half_product(normed_other, qkv_grads)
    qkv_mine = half_product(after(normed_mine, qkv_other), qkv_grads)
    gate_up_sum.step(qkv_other, qkv_mine)
    qkv_other = swap(after(qkv_other, *gate_up_sum.sent), 1)
    down_share = down_sum.finish(*gate_up_sum.sent, joined=True)
    down_blocks = Spread(after(down_share, *gate_up_sum.sent))
    qkv_mine, out_mine = tie((qkv_mine, out_mine), gate_up_sum.sent)
    weight_parts = jnp.concatenate(
        [
            (mine.astype(jnp.float32) + other.astype(jnp.float32)).astype(jnp.bfloat16)
            for mine, other in ((qkv_mine, qkv_other), (out_mine, out_other))
        ],
        2,
    )
    weight_sum = RingSum(weight_parts, seat)
    near, away = tie((near, away), gate_up_sum.sent)
    table_local = table_sums(near, away)
    weight_sum.step(weight_parts, table_local, *down_blocks.arrived())
    (late_grads,) = tie((qkv_grads,), weight_sum.sent)
    grad_normed = dot_dims(late_grads, full_qkv, 1, 1)
    grad_row_one, gain_one_local = norm_backward(grad_normed, row_one, inv_one, gain_one)
    input_grad = grad_mid + grad_row_one
    down_blocks.hop(*weight_sum.sent)

    gate_up_share = gate_up_sum.finish(input_grad)
    gate_blocks, up_blocks = Spread(gate_up_share[0]), Spread(gate_up_share[1])
    weight_sum.step(gate_up_share, *down_blocks.arrived())
    (late_rows,) = tie((normed_two,), weight_sum.sent)
    small = SumAll((gain_one_local, table_local, gain_two_local, matmul(late_rows.T, grad_logits)))
    weight_sum.step(small.hop(*weight_sum.sent), *gate_blocks.arrived())
    Spread.hop_own(gate_blocks, up_blocks, gate_up_share, *weight_sum.sent)
    weight_sum.step(small.hop(*weight_sum.sent), *up_blocks.arrived(), *up_blocks.own_last)
    gate_blocks.hop(*weight_sum.sent)
    up_blocks.hop(*weight_sum.sent)
    down_out = down_blocks.outputs(device, *weight_sum.sent)
    rounded = weight_sum.finish(
        down_out, small.hop(*weight_sum.sent), *gate_blocks.arrived(), *up_blocks.arrived()
    )
    gate_out = gate_blocks.outputs(device, rounded, small.hop(rounded))
    up_out = up_blocks.outputs(device, gate_out)
    bit = owner_count // 2
    while bit > 1:
        arriving = after(swap(rounded, bit), gate_out, up_out)
        share = rounded.astype(jnp.float32) + arriving.astype(jnp.float32)
        rounded = share.astype(jnp.bfloat16)
        bit //= 2
    other = swap(rounded, 1)
    small.hop(rounded)
    gain_one_grad, table_grad, gain_two_grad, router_grad = small.finish()
    weight_grads = jnp.concatenate(
        [jnp.where(core == 0, rounded, other), jnp.where(core == 0, other, rounded)], 1
    ).astype(jnp.float32)
    query_grad, key_grad, value_grad, out_grad = (
        weight_grads[i // 2, :, i % 2 * D : (i % 2 + 1) * D] for i in range(4)
    )
    return (
        block_out,
        input_grad,
        gain_one_grad,
        query_grad,
        key_grad,
        value_grad,
        out_grad,
        table_grad,
        gain_two_grad,
        router_grad,
        gate_out,
        up_out,
        down_out,
    )


def solution(mesh):
    placed = (
        P(("dp", "expert"), None),
        P(("dp", "expert"), None),
        P(),
        P("dp", None),
        P("dp", None),
        P("dp", None),
        P("dp", None),
        P(),
        P(),
        P(),
        P(None, "dp", None),
        P(None, "dp", None),
        P(None, "dp", None),
        P(("dp", "expert"), None),
        P(("dp", "expert"), None),
        P(("dp", "expert"), None),
        P(("dp", "expert")),
    )
    return jax.shard_map(
        body,
        mesh=mesh,
        in_specs=placed,
        out_specs=(
            P(("dp", "expert"), None),
            P(("dp", "expert"), None),
            P(),
            P("dp", None),
            P("dp", None),
            P("dp", None),
            P("dp", None),
            P(),
            P(),
            P(),
            P(None, "dp", None),
            P(None, "dp", None),
            P(None, "dp", None),
        ),
        check_vma=False,
    )
```
